32 devices in a mesh: rows: 8 (over z, x), seq: 4 (over y, core).
Axes of the slice: x: 2, y: 2, z: 4, core: 2. Of those that a mesh axis runs over, the one named last changes fastest.
Arguments:
- tokens: bfloat16 [16, 1024, 768], P('rows', 'seq'), may hold values from -6 to 6
- cotangent: bfloat16 [16, 1024, 768], P('rows', 'seq'), may hold values from -6 to 6
- segment_ids: int32 [16, 1024], P('rows'), may hold values from 0 to 1, as said below
- mask_positions: int32 [16, 2, 80], P('rows'), may hold values from -1 to 1023, as said below
- query_weight: bfloat16 [768, 768], replicated, may hold values from -0.21875 to 0.21875
- query_bias: float32 [768], replicated, may hold values from -2 to 2
- key_weight: bfloat16 [768, 768], replicated, may hold values from -0.21875 to 0.21875
- value_weight: bfloat16 [768, 768], replicated, may hold values from -0.21875 to 0.21875
- value_bias: float32 [768], replicated, may hold values from -2 to 2
- output_weight: bfloat16 [768, 768], replicated, may hold values from -3.5 to 3.5
- output_bias: float32 [768], replicated, may hold values from -2 to 2
- first_gain: float32 [768], replicated, may hold values from 0.5 to 1.5
- first_shift: float32 [768], replicated, may hold values from -2 to 2
- up_weight: bfloat16 [768, 3072], replicated, may hold values from -0.21875 to 0.21875
- up_bias: float32 [3072], replicated, may hold values from -2 to 2
- down_weight: bfloat16 [3072, 768], replicated, may hold values from -0.109375 to 0.109375
- down_bias: float32 [768], replicated, may hold values from -2 to 2
- second_gain: float32 [768], replicated, may hold values from 0.5 to 1.5
- second_shift: float32 [768], replicated, may hold values from -2 to 2
Outputs:
- layer_output: bfloat16 [16, 1024, 768], P('rows', 'seq')
- input_grad: float32 [16, 1024, 768], P('rows', 'seq')
- grad_query_weight: float32 [768, 768], replicated
- grad_query_bias: float32 [768], replicated
- grad_key_weight: float32 [768, 768], replicated
- grad_value_weight: float32 [768, 768], replicated
- grad_value_bias: float32 [768], replicated
- grad_output_weight: float32 [768, 768], replicated
- grad_output_bias: float32 [768], replicated
- grad_first_gain: float32 [768], replicated
- grad_first_shift: float32 [768], replicated
- grad_up_weight: float32 [768, 3072], P(None, ('rows', 'seq'))
- grad_up_bias: float32 [3072], replicated
- grad_down_weight: float32 [3072, 768], P(('rows', 'seq'))
- grad_down_bias: float32 [768], replicated
- grad_second_gain: float32 [768], replicated
- grad_second_shift: float32 [768], replicated
The draws below stay inside these ranges and needn't reach their ends.
Inputs may be any that keep to these rules, and one draw needn't show every extreme that they name: `segment_ids`: each row is 0 up to a split point and 1 after it; both sequences are nonempty and one of them holds more than 768 positions. `mask_positions`: entry [r, s, j] is a masked position of sequence s (0 the first, 1 the second) of row r, counted within the row; each sequence has 1 to 80 distinct masked positions inside it, listed first; remaining entries are -1.
All inputs are finite; a program needn't handle non-finite values.
Results may differ from the reference program's by a relative error of at most 0.013.
The reference program's roundings to bfloat16 on the way count: a program that leaves them out, or rounds other values in their place, can miss the bound.
Values may be sent and summed in bfloat16 or wider, within the bound.
A program may use at most 192 MiB of HBM per device.

```python
import jax
import jax.numpy as jnp
from jax import lax

MODEL_DIMENSION = 768
HEADS = 12
HEAD_DIM = 64
FF = 3072
PACKED_ROW_TOKENS = 1024
MASKS = 80
STRETCH = 256
PACKED_ROW_COUNT = 16


def split_points(key):
    side_key, offset_key = jax.random.split(key)
    start_offset = jax.random.randint(offset_key, (PACKED_ROW_COUNT,), 1, STRETCH)
    half_side = jax.random.randint(side_key, (PACKED_ROW_COUNT,), 0, 2)
    return jnp.where(half_side == 1, PACKED_ROW_TOKENS - start_offset, start_offset).astype(jnp.int32)


def draw_segment_ids(key, part):
    stretch_limits = split_points(key)
    token_positions = jnp.arange(PACKED_ROW_TOKENS, dtype=jnp.int32)
    return (token_positions[None, :] >= stretch_limits[:, None]).astype(jnp.int32)


def shuffle_row(row_random_key):
    return jax.random.permutation(row_random_key, PACKED_ROW_TOKENS)


def draw_mask_positions(key, part):
    stretch_limits = split_points(key)
    key = jax.random.fold_in(key, 7)
    count_key, order_key = jax.random.split(key)
    counts = jax.random.randint(count_key, (PACKED_ROW_COUNT, 2), 1, MASKS + 1)
    longest_leading = stretch_limits[0] > PACKED_ROW_TOKENS // 2
    forced = jnp.where(longest_leading, jnp.array([MASKS, 1], jnp.int32), jnp.array([1, MASKS], jnp.int32))
    counts = counts.at[0].set(forced)
    segment_lengths = jnp.stack([stretch_limits, PACKED_ROW_TOKENS - stretch_limits], axis=1)
    counts = jnp.minimum(counts, segment_lengths)
    length_ranks = jax.vmap(shuffle_row)(jax.random.split(order_key, PACKED_ROW_COUNT)).astype(jnp.int32)
    length_ranks = length_ranks.at[0, PACKED_ROW_TOKENS - 1].set(-1)
    token_positions = jnp.arange(PACKED_ROW_TOKENS, dtype=jnp.int32)
    second = token_positions[None, :] >= stretch_limits[:, None]

    def pick(within_stretch):
        score_value = jnp.where(within_stretch, length_ranks, length_ranks + 2 * PACKED_ROW_TOKENS)
        return jnp.argsort(score_value, axis=1, stable=True)[:, :MASKS].astype(jnp.int32)
    picks = jnp.stack([pick(jnp.logical_not(second)), pick(second)], axis=1)
    slots = jnp.arange(MASKS, dtype=jnp.int32)
    return jnp.where(slots[None, None, :] < counts[:, :, None], picks, -1).astype(jnp.int32)


def spiked(values, own_key, source, target, parts, factor):
    owner, partner = [(jnp.arange(values.shape[position]) // (values.shape[position] // parts)).reshape([-1 if axis == position else 1 for axis in range(values.ndim)]) for position in (source, target)]
    chosen = jax.random.permutation(own_key, parts)[partner]
    strong = (owner == chosen) | (owner == (partner + parts // 2) % parts)
    return jnp.where(strong, factor * values, values)


def shard_levels(stream_key, dims, cuts, smallest, top_value):
    factor_of, own = 1.0, jax.random.fold_in(stream_key, 6)
    for dim, parts in cuts:
        steps = jnp.exp(jax.random.uniform(jax.random.fold_in(own, dim), (parts,), jnp.float32, smallest / len(cuts), top_value / len(cuts)))
        factor_of = factor_of * jnp.repeat(steps, dims[dim] // parts).reshape([-1 if axis == dim else 1 for axis in range(len(dims))])
    return factor_of


def bell_draw(rng, dims, scale, limit, shards=(), kind=jnp.bfloat16):
    values = scale * jax.random.normal(rng, dims, jnp.float32)
    if shards:
        values = values * shard_levels(rng, dims, shards, -0.22, 0.18)
    return jnp.clip(values, -limit, limit).astype(kind)


def heavy_noise(key, shape, scale, limit, cuts, heavy, kind=jnp.bfloat16):
    values = scale * jax.random.normal(key, shape, jnp.float32)
    if cuts:
        values = values * shard_levels(key, shape, cuts, -0.22, 0.18)
    return jnp.clip(spiked(values, jax.random.fold_in(key, 3), *heavy), -limit, limit).astype(kind)


def setup_inputs(seed: int = 0) -> dict:
    key_of = jax.random.split(jax.random.key(seed), 20)
    return {
        "tokens": bell_draw(key_of[0], (PACKED_ROW_COUNT, PACKED_ROW_TOKENS, MODEL_DIMENSION), 1.0, 6.0, ((0, 8), (1, 4))),
        "cotangent": heavy_noise(key_of[1], (PACKED_ROW_COUNT, PACKED_ROW_TOKENS, MODEL_DIMENSION), 1.0, 6.0, ((0, 8), (1, 4)), (0, 2, 8, 2.0)),
        "segment_ids": draw_segment_ids(jax.random.fold_in(key_of[19], 71), 0),
        "mask_positions": draw_mask_positions(jax.random.fold_in(key_of[19], 71), 0),
        "query_weight": bell_draw(key_of[4], (MODEL_DIMENSION, MODEL_DIMENSION), MODEL_DIMENSION ** -0.5, 0.21875),
        "query_bias": bell_draw(key_of[5], (MODEL_DIMENSION,), 0.3, 2.0, (), jnp.float32),
        "key_weight": bell_draw(key_of[6], (MODEL_DIMENSION, MODEL_DIMENSION), MODEL_DIMENSION ** -0.5, 0.21875),
        "value_weight": bell_draw(key_of[7], (MODEL_DIMENSION, MODEL_DIMENSION), MODEL_DIMENSION ** -0.5, 0.21875),
        "value_bias": bell_draw(key_of[8], (MODEL_DIMENSION,), 0.3, 2.0, (), jnp.float32),
        "output_weight": bell_draw(key_of[9], (MODEL_DIMENSION, MODEL_DIMENSION), (MODEL_DIMENSION // STRETCH) ** -0.5, 3.5),
        "output_bias": bell_draw(key_of[10], (MODEL_DIMENSION,), 0.3, 2.0, (), jnp.float32),
        "first_gain": jnp.clip(1.0 + 0.1 * jax.random.normal(key_of[11], (MODEL_DIMENSION,), jnp.float32), 0.5, 1.5),
        "first_shift": bell_draw(key_of[12], (MODEL_DIMENSION,), 0.3, 2.0, (), jnp.float32),
        "up_weight": bell_draw(key_of[13], (MODEL_DIMENSION, FF), MODEL_DIMENSION ** -0.5, 0.21875),
        "up_bias": bell_draw(key_of[14], (FF,), 0.3, 2.0, (), jnp.float32),
        "down_weight": bell_draw(key_of[15], (FF, MODEL_DIMENSION), FF ** -0.5, 0.109375),
        "down_bias": bell_draw(key_of[16], (MODEL_DIMENSION,), 0.3, 2.0, (), jnp.float32),
        "second_gain": jnp.clip(1.0 + 0.1 * jax.random.normal(key_of[17], (MODEL_DIMENSION,), jnp.float32), 0.5, 1.5),
        "second_shift": bell_draw(key_of[18], (MODEL_DIMENSION,), 0.3, 2.0, (), jnp.float32),
    }


@jax.custom_vjp
def low(v):
    return lax.optimization_barrier(v.astype(jnp.bfloat16)).astype(jnp.float32)

@jax.custom_vjp
def low_back(v):
    return v

def low_keep(v):
    return (low(v), None)

def low_pass(kept, grad):
    return (grad,)

def back_keep(v):
    return (v, None)

def back_low(kept, grad):
    return (low(grad),)
low.defvjp(low_keep, low_pass)
low_back.defvjp(back_keep, back_low)
EPSILON = 1e-12
MASKED_SCORE = -1000000000.0

def both_ways(value):
    return low_back(low(value))

def matmul(left, right):
    return jnp.dot(left, right, precision=lax.Precision.HIGHEST)

def layer_norm(hidden, norm_gain, norm_shift):
    row_mean = lax.optimization_barrier(jnp.mean(hidden, axis=-1, keepdims=True))
    centred = hidden - row_mean
    variance = lax.optimization_barrier(jnp.mean(centred * centred, axis=-1, keepdims=True))
    return centred * lax.rsqrt(variance + EPSILON) * norm_gain + norm_shift

def gelu_tanh(value):
    return jax.nn.gelu(value, approximate=True)

def forward(inputs, same_segment, query_weight, query_bias, key_weight, value_weight, value_bias, output_weight, output_bias, first_gain, first_shift, up_weight, up_bias, down_weight, down_bias, second_gain, second_shift):
    length = inputs.shape[0]
    score_scale = HEAD_DIM ** (-0.5)
    queries = both_ways(matmul(inputs, query_weight) + query_bias).reshape(length, HEADS, HEAD_DIM)
    keys_all = both_ways(matmul(inputs, key_weight)).reshape(length, HEADS, HEAD_DIM)
    values_all = both_ways(matmul(inputs, value_weight) + value_bias).reshape(length, HEADS, HEAD_DIM)
    scores = jnp.einsum('qhe,khe->hqk', queries, keys_all, precision=lax.Precision.HIGHEST)
    scores = low_back(scores * score_scale)
    scores = jnp.where(same_segment[None], scores, MASKED_SCORE)
    probs = low(jax.nn.softmax(scores, axis=-1))
    context = jnp.einsum('hqk,khe->qhe', probs, values_all, precision=lax.Precision.HIGHEST)
    context = both_ways(context.reshape(length, HEADS * HEAD_DIM))
    branch = low_back(matmul(context, output_weight) + output_bias)
    normed = layer_norm(inputs + branch, first_gain, first_shift)
    hidden_pre = low_back(matmul(low(normed), up_weight) + up_bias)
    hidden_act = low(gelu_tanh(hidden_pre))
    feed = low_back(matmul(hidden_act, down_weight) + down_bias)
    return layer_norm(normed + feed, second_gain, second_shift)

def reference(tokens, cotangent, segment_ids, mask_positions, query_weight, query_bias, key_weight, value_weight, value_bias, output_weight, output_bias, first_gain, first_shift, up_weight, up_bias, down_weight, down_bias, second_gain, second_shift):
    weights = tuple((weight.astype(jnp.float32) for weight in (query_weight, query_bias, key_weight, value_weight, value_bias, output_weight, output_bias, first_gain, first_shift, up_weight, up_bias, down_weight, down_bias, second_gain, second_shift)))
    token_positions = jnp.arange(PACKED_ROW_TOKENS, dtype=jnp.int32)

    def one_row(totals, row_data):
        row_tokens, row_cotangent, row_segments, row_masks = row_data
        same_segment = row_segments[:, None] == row_segments[None, :]
        masked = jnp.any(row_masks.reshape(1, -1) == token_positions[:, None], axis=1)
        out_grad = row_cotangent.astype(jnp.float32) * masked.astype(jnp.float32)[:, None]

        def apply_layer(inputs, *params):
            return forward(inputs, same_segment, *params)
        result, pull = jax.vjp(apply_layer, row_tokens.astype(jnp.float32), *weights)
        grads = pull(out_grad)
        totals = tuple((total + grad for total, grad in zip(totals, grads[1:])))
        return (totals, (result.astype(jnp.bfloat16), grads[0]))
    start = tuple((jnp.zeros_like(weight) for weight in weights))
    totals, outputs = lax.scan(one_row, start, (tokens, cotangent, segment_ids, mask_positions))
    layer_output, input_grad = outputs
    return (layer_output, input_grad, totals[0], totals[1], totals[2], totals[3], totals[4], totals[5], totals[6], totals[7], totals[8], totals[9], totals[10], totals[11], totals[12], totals[13], totals[14])
```

```python
import functools

import jax
import jax.numpy as jnp
from jax import lax
from jax.experimental import pallas as pl
from jax.experimental.pallas import tpu as pltpu
from jax.sharding import PartitionSpec as P

HEADS = 12
EPSILON = 1e-12
MASKED_SCORE = -1000000000.0
F32 = jnp.float32
BF16 = jnp.bfloat16
MESH = pl.DeviceIdType.MESH
VMEM_LIMIT = 56 * 2**20


def dot(left, right):
    return lax.dot_general(left, right, (((1,), (0,)), ((), ())), preferred_element_type=F32)


def dot_nt(left, right):
    return lax.dot_general(left, right, (((1,), (1,)), ((), ())), preferred_element_type=F32)


def dot_tn(left, right):
    return lax.dot_general(left, right, (((0,), (0,)), ((), ())), preferred_element_type=F32)


def norm_parts(hidden):
    centred = hidden - jnp.mean(hidden, axis=-1, keepdims=True)
    variance = jnp.mean(centred * centred, axis=-1, keepdims=True)
    scale = lax.rsqrt(variance + EPSILON)
    return centred * scale, scale


def norm_back(grad, normed, scale, gain):
    scaled = grad * gain
    along = jnp.mean(scaled * normed, axis=-1, keepdims=True)
    return (scaled - jnp.mean(scaled, axis=-1, keepdims=True) - normed * along) * scale


GELU_A = 0.7978845608028654
GELU_B = 0.044715


def gelu_parts(value):
    square = value * value
    bent = jnp.tanh(GELU_A * value * (1.0 + GELU_B * square))
    half = 0.5 * (1.0 + bent)
    slope = half + 0.5 * value * (1.0 - bent * bent) * (GELU_A * (1.0 + 3.0 * GELU_B * square))
    return value * half, slope


def gelu_only(value):
    bent = jnp.tanh(GELU_A * value * (1.0 + GELU_B * value * value))
    return 0.5 * value * (1.0 + bent)


def lane_is(shape, low, high):
    lane = lax.broadcasted_iota(jnp.int32, shape, len(shape) - 1)
    return (lane >= low) & (lane < high)


def project_kernel(core, half, peer, pos, seg, slots, wq, bq, wk, wv, bv, keys, values, queries, context, probs, picked):
    width = keys.shape[1]
    mine = pl.ds(pl.multiple_of(core[0] * width, 128), width)
    count = slots.shape[0]
    tokens_half = half.shape[0]
    chosen = jnp.where(slots[...] == pos[...], 1.0, 0.0).astype(BF16)
    rows = dot(chosen[:, :tokens_half], half[...]) + dot(chosen[:, tokens_half:], peer[...])
    rows = rows.astype(BF16)
    picked[...] = rows
    queries[...] = (dot(rows, wq[:, mine]) + bq[:, mine]).astype(BF16)
    for place, part in ((0, half), (tokens_half, peer)):
        for start in range(0, tokens_half, 256):
            block = part[start : start + 256, :]
            there = slice(place + start, place + start + 256)
            keys[there, :] = dot(block, wk[:, mine]).astype(BF16)
            values[there, :] = (dot(block, wv[:, mine]) + bv[:, mine]).astype(BF16)
    sequence = lax.broadcasted_iota(jnp.int32, (count, 1), 0) // (count // 2)
    same = seg[...] == sequence
    for pair in range(width // 128):
        lanes = slice(pair * 128, pair * 128 + 128)
        pair_queries = queries[:, lanes].astype(F32) * 0.125
        pair_keys, pair_values = keys[:, lanes], values[:, lanes]
        outs = []
        for side in range(2):
            keep = lane_is((count, 128), side * 64, side * 64 + 64)
            head_queries = jnp.where(keep, pair_queries, 0.0).astype(BF16)
            scores = jnp.where(same, dot_nt(head_queries, pair_keys), MASKED_SCORE)
            weights = jnp.exp(scores - jnp.max(scores, axis=-1, keepdims=True))
            share = weights / jnp.sum(weights, axis=-1, keepdims=True)
            probs[pair * 2 + side] = share
            outs.append(dot(share.astype(BF16), pair_values))
        first = lane_is((count, 128), 0, 64)
        context[:, lanes] = jnp.where(first, outs[0], outs[1]).astype(BF16)


def masked_kernel(core, ctx_own, ctx_peer, picked, cot_half, cot_peer, pos, slots, wo, bo, g1, s1, wup, bup, wdown, bdown, g2, s2, normed_low, feed, branch_low, grad_h1, small):
    count, width = ctx_own.shape
    hidden = wup.shape[1]
    model = wup.shape[0]
    tokens_half = cot_half.shape[0]
    mine = pl.multiple_of(core[0] * count, 16)
    is_first = core[0] == 0
    left = jnp.where(is_first, ctx_own[...], ctx_peer[...])
    right = jnp.where(is_first, ctx_peer[...], ctx_own[...])
    branch = dot(left, wo[:width, :]) + dot(right, wo[width:, :]) + bo[...]
    h1 = picked[pl.ds(mine, count), :].astype(F32) + branch
    n1, r1 = norm_parts(h1)
    y1 = n1 * g1[...] + s1[...]
    y1_low = y1.astype(BF16)
    normed_low[...] = y1_low
    total = y1 + bdown[...]
    slopes = []
    step = model
    for start in range(0, hidden, step):
        pre = dot(y1_low, wup[:, start : start + step]) + bup[:, start : start + step]
        act, slope = gelu_parts(pre)
        slopes.append(slope)
        total = total + dot(act.astype(BF16), wdown[start : start + step, :])
    n2, r2 = norm_parts(total)
    chosen = jnp.where(slots[pl.ds(mine, count), :] == pos[...], 1.0, 0.0).astype(BF16)
    grad = dot(chosen[:, :tokens_half], cot_half[...]) + dot(chosen[:, tokens_half:], cot_peer[...])
    gh2 = norm_back(grad, n2, r2, g2[...])
    gf = gh2.astype(BF16)
    feed[...] = gf
    gy1 = gh2
    small[...] = jnp.zeros_like(small)
    for place, start in enumerate(range(0, hidden, step)):
        ga = dot_nt(gf, wdown[start : start + step, :])
        gp = (ga * slopes[place]).astype(BF16)
        small[place : place + 1, :] = jnp.sum(gp.astype(F32), axis=0, keepdims=True)
        gy1 = gy1 + dot_nt(gp, wup[:, start : start + step])
    gh1 = norm_back(gy1, n1, r1, g1[...])
    grad_h1[...] = gh1
    gb = gh1.astype(BF16)
    branch_low[...] = gb
    base = hidden // step
    for place, value in enumerate((gy1 * n1, gy1, grad * n2, grad, gb.astype(F32), gf.astype(F32))):
        small[base + place : base + place + 1, :] = jnp.sum(value, axis=0, keepdims=True)


def back_kernel(core, keys, values, queries, context, probs, picked, gb_own, gb_peer, gh1, half, peer, pos_col, slots_row, wq, wk, wv, wo, grads, igrad_own, igrad_peer, bias, dq_low, dk_low, dv_low):
    width = keys.shape[1]
    count = queries.shape[0]
    own = gb_own.shape[0]
    tokens_half = half.shape[0]
    is_first = core[0] == 0
    mine = pl.ds(pl.multiple_of(core[0] * width, 128), width)
    mine_rows = pl.ds(pl.multiple_of(core[0] * width, 128), width)
    top = jnp.where(is_first, gb_own[...], gb_peer[...])
    low = jnp.where(is_first, gb_peer[...], gb_own[...])
    gb = jnp.concatenate([top, low], axis=0)
    gctx = dot_nt(gb, wo[mine_rows, :]).astype(BF16)
    for pair in range(width // 128):
        lanes = slice(pair * 128, pair * 128 + 128)
        pair_keys, pair_values, pair_queries = keys[:, lanes], values[:, lanes], queries[:, lanes]
        pair_gctx = gctx[:, lanes]
        dqs, dks, dvs = [], [], []
        for side in range(2):
            keep = lane_is((count, 128), side * 64, side * 64 + 64)
            head_gctx = jnp.where(keep, pair_gctx.astype(F32), 0.0).astype(BF16)
            share = probs[pair * 2 + side]
            gp = dot_nt(head_gctx, pair_values)
            spread = jnp.sum(share * gp, axis=-1, keepdims=True)
            gs = (share * (gp - spread)).astype(BF16)
            dqs.append(dot(gs, pair_keys))
            dks.append(dot_tn(gs, pair_queries))
            dvs.append(dot_tn(share.astype(BF16), pair_gctx))
        first = lane_is((count, 128), 0, 64)
        dq_low[:, lanes] = (jnp.where(first, dqs[0], dqs[1]) * 0.125).astype(BF16)
        first = lane_is((2 * tokens_half, 128), 0, 64)
        dk_low[:, lanes] = (jnp.where(first, dks[0], dks[1]) * 0.125).astype(BF16)
        dv_low[:, lanes] = jnp.where(first, dvs[0], dvs[1]).astype(BF16)
    grads[1] = dot_tn(picked[...], dq_low[...]).astype(BF16)
    gwo = dot_tn(context[...], gb).astype(BF16)
    grads[0, :width, :] = gwo[:, :width]
    grads[0, width:, :] = gwo[:, width:]
    for place, part in ((2, dk_low), (3, dv_low)):
        total = dot_tn(half[...], part[:tokens_half, :]) + dot_tn(peer[...], part[tokens_half:, :])
        grads[place] = total.astype(BF16)
    bias[0:1, :] = jnp.sum(dq_low[...].astype(F32), axis=0, keepdims=True)
    bias[1:2, :] = jnp.sum(dv_low[...].astype(F32), axis=0, keepdims=True)
    spread_rows = dot_nt(dq_low[...], wq[:, mine])
    zero = jnp.zeros((own, wq.shape[0]), F32)
    spread_rows = spread_rows + jnp.concatenate(
        [jnp.where(is_first, gh1[...], zero), jnp.where(is_first, zero, gh1[...])], axis=0
    )
    high = spread_rows.astype(BF16)
    rest = (spread_rows - high.astype(F32)).astype(BF16)
    for start in range(0, 2 * tokens_half, 256):
        here = slice(start, start + 256)
        chosen = jnp.where(pos_col[here, :] == slots_row[...], 1.0, 0.0).astype(BF16)
        total = dot(chosen, high) + dot(chosen, rest)
        total = total + dot_nt(dk_low[here, :], wk[:, mine]) + dot_nt(dv_low[here, :], wv[:, mine])
        if start < tokens_half:
            igrad_own[here, :] = total
        else:
            igrad_peer[start - tokens_half : start - tokens_half + 256, :] = total.astype(BF16)


def attend_kernel(core, half, peer, seg, seg_col, keys, values, wq, bq, own, other):
    width = keys.shape[1]
    mine = pl.ds(pl.multiple_of(core[0] * width, 128), width)
    tile = 256
    for part, out in ((half, own), (peer, other)):
        place = 0 if part is half else half.shape[0]

        def body(step, carry, part=part, out=out, place=place):
            here = pl.ds(pl.multiple_of(step * tile, tile), tile)
            queries = (dot(part[here, :], wq[:, mine]) + bq[:, mine]).astype(BF16).astype(F32) * 0.125
            same = seg_col[pl.ds(pl.multiple_of(place + step * tile, tile), tile), :] == seg[...]
            for pair in range(width // 128):
                lanes = slice(pair * 128, pair * 128 + 128)
                outs = []
                for side in range(2):
                    keep = lane_is((tile, 128), side * 64, side * 64 + 64)
                    head_queries = jnp.where(keep, queries[:, lanes], 0.0).astype(BF16)
                    scores = jnp.where(same, dot_nt(head_queries, keys[:, lanes]), MASKED_SCORE)
                    weights = jnp.exp(scores - jnp.max(scores, axis=-1, keepdims=True))
                    total = jnp.sum(weights, axis=-1, keepdims=True)
                    outs.append(dot(weights.astype(BF16), values[:, lanes]) / total)
                first = lane_is((tile, 128), 0, 64)
                out[here, lanes] = jnp.where(first, outs[0], outs[1]).astype(BF16)
            return carry

        lax.fori_loop(0, part.shape[0] // tile, body, 0)


def feed_kernel(core, ctx_own, ctx_peer, half, wo, bo, g1, s1, wup, bup, wdown, bdown, g2, s2, own, other):
    width = ctx_own.shape[1]
    hidden, model = wdown.shape
    is_first = core[0] == 0
    tile = own.shape[0]
    for start, out in ((0, own), (tile, other)):
        here = slice(start, start + tile)
        left = jnp.where(is_first, ctx_own[here, :], ctx_peer[here, :])
        right = jnp.where(is_first, ctx_peer[here, :], ctx_own[here, :])
        branch = dot(left, wo[:width, :]) + dot(right, wo[width:, :]) + bo[...]
        n1, _ = norm_parts(half[here, :].astype(F32) + branch)
        y1 = n1 * g1[...] + s1[...]
        y1_low = y1.astype(BF16)
        total = y1 + bdown[...]
        for place in range(0, hidden, model):
            pre = dot(y1_low, wup[:, place : place + model]) + bup[:, place : place + model]
            total = total + dot(gelu_only(pre).astype(BF16), wdown[place : place + model, :])
        n2, _ = norm_parts(total)
        out[...] = (n2 * g2[...] + s2[...]).astype(BF16)


def hidden_kernel(slot, normed, feed, wup, bup, wdown, out):
    units = out.shape[0]
    model = normed.shape[1]
    mine = pl.ds(pl.multiple_of(slot[0] * units, 128), units)
    pre = dot(normed[...], wup[:, mine]) + bup[:, mine]
    act, slope = gelu_parts(pre)
    ga = dot_nt(feed[...], wdown[mine, :])
    gp = (ga * slope).astype(BF16)
    out[:, :model] = dot_tn(gp, normed[...]).astype(BF16)
    out[:, model:] = dot_tn(act.astype(BF16), feed[...]).astype(BF16)


def place_here():
    row, seq = lax.axis_index("rows"), lax.axis_index("seq")
    return row // 2, row % 2, seq // 2, seq % 2


def device(z, x, y, core):
    return (z * 2 + x, y * 2 + core)


def greet(partners):
    barrier = pltpu.get_barrier_semaphore()
    for partner in partners:
        pl.semaphore_signal(barrier, inc=1, device_id=partner, device_id_type=MESH)
    pl.semaphore_wait(barrier, len(partners))


def send(src, dst, sems, index, target):
    copy = pltpu.make_async_remote_copy(
        src_ref=src, dst_ref=dst, send_sem=sems[0].at[index], recv_sem=sems[1].at[index], device_id=target, device_id_type=MESH
    )
    copy.start()
    return copy


def factors_kernel(normed, feed, all_normed, all_feed, send_sem, recv_sem):
    z, x, y, core = place_here()
    sems = (send_sem, recv_sem)
    others = [(z + k) % 4 for k in (1, 2, 3)]
    twin = device(z, x, y, 1 - core)
    greet([device(o, x, y, core) for o in others] + [twin])
    copies = []
    for which, (src, dst) in enumerate(((normed, all_normed), (feed, all_feed))):
        dst[core, z] = src[...]
        for k, other in enumerate(others):
            copies.append(send(src, dst.at[core, z], sems, which * 4 + k, device(other, x, y, core)))
    for copy in copies:
        copy.wait()
    copies = []
    for which, dst in enumerate((all_normed, all_feed)):
        copies.append(send(dst.at[core], dst.at[core], sems, which * 4 + 3, twin))
    for copy in copies:
        copy.wait()


def sum_kernel(grads, hidden, small, out, hidden_out, small_out, first_in, first_sum, second_in, second_sum, third_in, hidden_in, small_in, small_z, send_sem, recv_sem, hsend, hrecv, ssend, srecv):
    z, x, y, core = place_here()
    jobs, rows, _ = grads.shape
    half, quarter, chunk = rows // 2, rows // 4, rows // 16
    units = hidden_out.shape[0]
    sems, hsems, ssems = (send_sem, recv_sem), (hsend, hrecv), (ssend, srecv)
    others = [(z + k) % 4 for k in (1, 2, 3)]
    at_y, at_x, twin = device(z, x, 1 - y, core), device(z, 1 - x, y, core), device(z, x, y, 1 - core)
    columns = [device(o, x, y, core) for o in others]
    spots = [(cx, cy, cc) for cx in range(2) for cy in range(2) for cc in range(2)]
    barrier = pltpu.get_barrier_semaphore()
    for cx, cy, cc in spots:
        @pl.when(jnp.logical_not((cx == x) & (cy == y) & (cc == core)))
        def _(cx=cx, cy=cy, cc=cc):
            pl.semaphore_signal(barrier, inc=1, device_id=device(z, cx, cy, cc), device_id_type=MESH)
    for target in columns:
        pl.semaphore_signal(barrier, inc=1, device_id=target, device_id_type=MESH)
    pl.semaphore_wait(barrier, 10)

    order = [(y, x, at_y, at_x) if job % 2 == 0 else (x, y, at_x, at_y) for job in range(jobs)]
    first = []
    for job in range(jobs):
        p1, _, d1, _ = order[job]
        src = grads.at[job, pl.ds(pl.multiple_of((1 - p1) * half, 16), half)]
        first.append(send(src, first_in.at[job], sems, job * 10, d1))
    source = x * 2 + y

    def is_me(cy, cc):
        return (core == x) & (cy == y) & (cc == core)

    for cy in range(2):
        for cc in range(2):
            part = hidden.at[pl.ds((cy * 2 + cc) * units, units)]

            @pl.when(jnp.logical_not(is_me(cy, cc)))
            def _(cy=cy, cc=cc, part=part):
                pltpu.make_async_remote_copy(
                    src_ref=part, dst_ref=hidden_in.at[source], send_sem=hsend.at[cy * 2 + cc], recv_sem=hrecv.at[source],
                    device_id=device(z, core, cy, cc), device_id_type=MESH,
                ).start()

            @pl.when(is_me(cy, cc))
            def _(part=part):
                hidden_in[source] = part[...]
    small_in[0] = small[...]
    for step, target in enumerate((twin, at_y, at_x)):
        copy = send(small_in.at[2 * step], small_in.at[2 * step + 1], ssems, step, target)
        copy.wait()
        small_in[2 * step + 2] = small_in[2 * step] + small_in[2 * step + 1]
    small_z[z] = small_in[6]
    small_copies = [send(small_in.at[6], small_z.at[z], ssems, 3 + k, t) for k, t in enumerate(columns)]

    second = []
    for job in range(jobs):
        p1, p2, _, d2 = order[job]
        first[job].wait()
        kept = grads[job, pl.ds(pl.multiple_of(p1 * half, 16), half)].astype(F32)
        first_sum[job] = (kept + first_in[job].astype(F32)).astype(BF16)
        src = first_sum.at[job, pl.ds(pl.multiple_of((1 - p2) * quarter, 16), quarter)]
        second.append(send(src, second_in.at[job], sems, job * 10 + 1, d2))
    third = []
    for job in range(jobs):
        p1, p2, _, _ = order[job]
        second[job].wait()
        kept = first_sum[job, pl.ds(pl.multiple_of(p2 * quarter, 16), quarter)].astype(F32)
        second_sum[job] = (kept + second_in[job].astype(F32)).astype(BF16)
        copies = []
        for k, other in enumerate(others):
            src = second_sum.at[job, pl.ds(pl.multiple_of(other * chunk, 16), chunk)]
            copies.append(send(src, third_in.at[job, k], sems, job * 10 + 2 + k, columns[k]))
        third.append(copies)
    fourth = []
    for job in range(jobs):
        p1, p2, _, _ = order[job]
        for copy in third[job]:
            copy.wait()
        total = second_sum[job, pl.ds(pl.multiple_of(z * chunk, 16), chunk)].astype(F32)
        for k in range(3):
            total = total + third_in[job, k].astype(F32)
        place = pl.ds(pl.multiple_of(p1 * half + p2 * quarter + z * chunk, 16), chunk)
        out[core, job, place] = total.astype(BF16)
        spot = out.at[core, job, place]
        fourth.append([send(spot, spot, sems, job * 10 + 5 + k, columns[k]) for k in range(3)])
    fifth = []
    for job in range(jobs):
        p1, p2, _, d2 = order[job]
        for copy in fourth[job]:
            copy.wait()
        spot = out.at[core, job, pl.ds(pl.multiple_of(p1 * half + p2 * quarter, 16), quarter)]
        fifth.append(send(spot, spot, sems, job * 10 + 8, d2))
    sixth = []
    for job in range(jobs):
        p1, _, d1, _ = order[job]
        fifth[job].wait()
        spot = out.at[core, job, pl.ds(pl.multiple_of(p1 * half, 16), half)]
        sixth.append(send(spot, spot, sems, job * 10 + 9, d1))
    for cy in range(2):
        for cc in range(2):
            @pl.when(jnp.logical_not(is_me(cy, cc)))
            def _(cy=cy, cc=cc):
                part = hidden.at[pl.ds((cy * 2 + cc) * units, units)]
                pltpu.make_async_remote_copy(
                    src_ref=part, dst_ref=hidden_in.at[source], send_sem=hsend.at[cy * 2 + cc], recv_sem=hrecv.at[source],
                    device_id=device(z, core, cy, cc), device_id_type=MESH,
                ).wait_send()
    for cx in range(2):
        for cy in range(2):
            @pl.when(jnp.logical_not((cx == x) & (cy == y) & (core == x)))
            def _(cx=cx, cy=cy):
                slot = hidden_in.at[cx * 2 + cy]
                pltpu.make_async_remote_copy(
                    src_ref=slot, dst_ref=slot, send_sem=hsend.at[0], recv_sem=hrecv.at[cx * 2 + cy],
                    device_id=twin, device_id_type=MESH,
                ).wait_recv()
    total = hidden_in[0].astype(F32)
    for k in range(1, 4):
        total = total + hidden_in[k].astype(F32)
    hidden_out[...] = total
    for copy in small_copies:
        copy.wait()
    small_out[...] = (small_z[0] + small_z[1]) + (small_z[2] + small_z[3])
    last = []
    for job in range(jobs):
        sixth[job].wait()
        last.append(send(out.at[core, job], out.at[core, job], sems, jobs * 10 + job, twin))
    for copy in last:
        copy.wait()


def vmem(count):
    return [pl.BlockSpec(memory_space=pltpu.VMEM)] * count


def local_call(body, outs, name, scratch=()):
    def call(core, *operands):
        return pl.pallas_call(
            body,
            out_shape=outs,
            in_specs=[pl.BlockSpec(memory_space=pltpu.SMEM)] + vmem(len(operands)),
            out_specs=vmem(len(outs)),
            scratch_shapes=list(scratch),
            compiler_params=pltpu.CompilerParams(vmem_limit_bytes=VMEM_LIMIT),
            name=name,
        )(core, *operands)

    return call


def on_device(
    rows_total,
    tokens,
    cotangent,
    segment_ids,
    mask_positions,
    query_weight,
    query_bias,
    key_weight,
    value_weight,
    value_bias,
    output_weight,
    output_bias,
    first_gain,
    first_shift,
    up_weight,
    up_bias,
    down_weight,
    down_bias,
    second_gain,
    second_shift,
):
    _, stretch, model = tokens.shape
    hidden = up_weight.shape[1]
    width = model // 2
    heads = HEADS // 2
    masks = mask_positions.shape[2]
    seq = lax.axis_index("seq")
    row = seq // 2
    core = seq % 2
    across = [(i, (i + 2) % 4) for i in range(4)]
    beside = [(i, i + 1 - 2 * (i % 2)) for i in range(4)]

    def swap(value):
        return lax.ppermute(value, "seq", across)

    def trade(value):
        return lax.ppermute(value, "seq", beside)

    def take(array, index):
        return lax.dynamic_index_in_dim(array, index, 0, keepdims=False)

    half = jnp.concatenate([take(tokens, row), swap(take(tokens, 1 - row))], axis=0)
    peer = trade(half)
    cot_half = jnp.concatenate([take(cotangent, row), swap(take(cotangent, 1 - row))], axis=0)
    cot_peer = trade(cot_half)
    blocks = jnp.stack([2 * row + core, 2 * (1 - row) + core, 2 * row + 1 - core, 2 * (1 - row) + 1 - core])
    positions = (blocks[:, None] * stretch + jnp.arange(stretch, dtype=jnp.int32)[None, :]).reshape(-1)
    segments = jnp.take(take(segment_ids, row).reshape(4, stretch), blocks, axis=0).reshape(-1)
    slots = take(mask_positions, row).reshape(-1)
    pos, seg, slot_col = positions[None, :], segments[None, :], slots[:, None]
    pos_col, seg_col, slot_row = positions[:, None], segments[:, None], slots[None, :]
    core_scalar = core.reshape(1).astype(jnp.int32)
    line = lambda value: value.reshape(1, -1)
    full = 4 * stretch
    count = 2 * masks
    shaped = jax.ShapeDtypeStruct

    keys, values, queries, context, probs, picked = local_call(
        project_kernel,
        (
            shaped((full, width), BF16),
            shaped((full, width), BF16),
            shaped((count, width), BF16),
            shaped((count, width), BF16),
            shaped((heads, count, full), F32),
            shaped((count, model), BF16),
        ),
        "project",
    )(core_scalar, half, peer, pos, seg, slot_col, query_weight, line(query_bias), key_weight, value_weight, line(value_bias))

    two = context.reshape(2, masks, width)
    ctx_peer = trade(take(two, 1 - core))
    normed_low, feed, branch_low, grad_h1, small = local_call(
        masked_kernel,
        (
            shaped((masks, model), BF16),
            shaped((masks, model), BF16),
            shaped((masks, model), BF16),
            shaped((masks, model), F32),
            shaped((16, model), F32),
        ),
        "masked",
    )(
        core_scalar, take(two, core), ctx_peer, picked, cot_half, cot_peer, pos, slot_col, output_weight, line(output_bias),
        line(first_gain), line(first_shift), up_weight, line(up_bias), down_weight, line(down_bias), line(second_gain), line(second_shift),
    )
    branch_peer = trade(branch_low)
    grads, igrad_own, igrad_peer, bias = local_call(
        back_kernel,
        (
            shaped((4, model, width), BF16),
            shaped((2 * stretch, model), F32),
            shaped((2 * stretch, model), BF16),
            shaped((2, width), F32),
        ),
        "back",
        [pltpu.VMEM((count, width), BF16), pltpu.VMEM((full, width), BF16), pltpu.VMEM((full, width), BF16)],
    )(
        core_scalar, keys, values, queries, context, probs, picked, branch_low, branch_peer, grad_h1, half, peer, pos_col, slot_row,
        query_weight, key_weight, value_weight, output_weight,
    )
    igrad = igrad_own + trade(igrad_peer).astype(F32)
    igrad_other = swap(igrad[stretch:].astype(BF16)).astype(F32)
    igrad_mine = igrad[:stretch]
    input_grad = jnp.where(row == 0, jnp.stack([igrad_mine, igrad_other]), jnp.stack([igrad_other, igrad_mine]))

    ctx_own, ctx_other = local_call(
        attend_kernel, (shaped((2 * stretch, width), BF16), shaped((2 * stretch, width), BF16)), "attend"
    )(core_scalar, half, peer, seg, seg_col, keys, values, query_weight, line(query_bias))
    out_mine, out_other = local_call(
        feed_kernel, (shaped((stretch, model), BF16), shaped((stretch, model), BF16)), "feed"
    )(
        core_scalar, ctx_own, trade(ctx_other), half, output_weight, line(output_bias), line(first_gain), line(first_shift),
        up_weight, line(up_bias), down_weight, line(down_bias), line(second_gain), line(second_shift),
    )
    out_other = swap(out_other)
    layer_output = jnp.where(row == 0, jnp.stack([out_mine, out_other]), jnp.stack([out_other, out_mine]))

    wide = jnp.zeros((2, model), F32)
    bias_rows = lax.dynamic_update_slice(wide, bias, (0, core * width))
    base = hidden // model + 6
    small = jnp.concatenate([small[:base], bias_rows, small[base + 2 :]], axis=0)

    if rows_total == 8:
        all_normed, all_feed = pl.pallas_call(
            factors_kernel,
            out_shape=(shaped((2, 4, masks, model), BF16),) * 2,
            in_specs=vmem(2),
            out_specs=vmem(2),
            scratch_shapes=[pltpu.SemaphoreType.DMA((8,)), pltpu.SemaphoreType.DMA((8,))],
            compiler_params=pltpu.CompilerParams(collective_id=0, has_side_effects=True, vmem_limit_bytes=VMEM_LIMIT),
            name="factors",
        )(normed_low, feed)
        units = hidden // 8
        place = (lax.axis_index("rows") // 2) * 2 + core
        (hidden_part,) = local_call(hidden_kernel, (shaped((units, 2 * model), BF16),), "hidden")(
            place.reshape(1).astype(jnp.int32), all_normed.reshape(8 * masks, model), all_feed.reshape(8 * masks, model),
            up_weight, line(up_bias), down_weight,
        )
        jobs = 4
        summed, hidden_grads, small = pl.pallas_call(
            sum_kernel,
            out_shape=(shaped((2, jobs, model, width), BF16), shaped((units // 4, 2 * model), F32), shaped((16, model), F32)),
            in_specs=vmem(3),
            out_specs=vmem(3),
            scratch_shapes=[
                pltpu.VMEM((jobs, model // 2, width), BF16),
                pltpu.VMEM((jobs, model // 2, width), BF16),
                pltpu.VMEM((jobs, model // 4, width), BF16),
                pltpu.VMEM((jobs, model // 4, width), BF16),
                pltpu.VMEM((jobs, 3, model // 16, width), BF16),
                pltpu.VMEM((4, units // 4, 2 * model), BF16),
                pltpu.VMEM((7, 16, model), F32),
                pltpu.VMEM((4, 16, model), F32),
                pltpu.SemaphoreType.DMA((jobs * 11,)),
                pltpu.SemaphoreType.DMA((jobs * 11,)),
                pltpu.SemaphoreType.DMA((4,)),
                pltpu.SemaphoreType.DMA((4,)),
                pltpu.SemaphoreType.DMA((6,)),
                pltpu.SemaphoreType.DMA((6,)),
            ],
            compiler_params=pltpu.CompilerParams(collective_id=1, has_side_effects=True, vmem_limit_bytes=VMEM_LIMIT),
            name="sums",
        )(grads, hidden_part, small)
        grad_wo = summed[:, 0].reshape(2, 2, width, width).transpose(0, 2, 1, 3).reshape(model, model).astype(F32)
        grad_wq, grad_wk, grad_wv = (summed[:, k].transpose(1, 0, 2).reshape(model, model).astype(F32) for k in (1, 2, 3))
    else:
        both = ("rows", "seq")
        small = lax.psum(small, both)
        zero = jnp.zeros((model, model), F32)
        wide_grads = [lax.dynamic_update_slice(zero, grads[k].astype(F32), (0, core * width)) for k in (1, 2, 3)]
        rows_wo = grads[0].reshape(2, width, width).transpose(1, 0, 2).reshape(width, model).astype(F32)
        wide_grads.append(lax.dynamic_update_slice(zero, rows_wo, (core * width, 0)))
        grad_wq, grad_wk, grad_wv, grad_wo = lax.psum(tuple(wide_grads), both)
        pieces = []
        units = hidden // 8
        for part in range(8):
            (piece,) = local_call(hidden_kernel, (shaped((units, 2 * model), BF16),), "hidden")(
                jnp.full((1,), part, jnp.int32), normed_low, feed, up_weight, line(up_bias), down_weight
            )
            pieces.append(piece.astype(F32))
        hidden_grads = lax.psum_scatter(jnp.concatenate(pieces, axis=0), both, scatter_dimension=0, tiled=True)

    base = hidden // model
    vector = lambda index: small[index]
    return (
        layer_output,
        input_grad,
        grad_wq,
        vector(base + 6),
        grad_wk,
        grad_wv,
        vector(base + 7),
        grad_wo,
        vector(base + 4),
        vector(base),
        vector(base + 1),
        hidden_grads[:, :model].T,
        small[:base].reshape(hidden),
        hidden_grads[:, model:],
        vector(base + 5),
        vector(base + 2),
        vector(base + 3),
    )


def solution(mesh):
    split = P("rows", "seq", None)
    in_specs = (split, split, P("rows", None), P("rows", None, None)) + (P(),) * 15
    out_specs = (split, split) + (P(),) * 9 + (P(None, ("rows", "seq")), P(), P(("rows", "seq"), None), P(), P(), P())
    return jax.shard_map(
        functools.partial(on_device, mesh.shape["rows"]), mesh=mesh, in_specs=in_specs, out_specs=out_specs, check_vma=False
    )
```

```python
import functools

import jax
import jax.numpy as jnp
from jax import lax
from jax.experimental import pallas as pl
from jax.experimental.pallas import tpu as pltpu
from jax.sharding import PartitionSpec as P

HEADS = 12
EPSILON = 1e-12
MASKED_SCORE = -1000000000.0
F32 = jnp.float32
BF16 = jnp.bfloat16
MESH = pl.DeviceIdType.MESH
VMEM_LIMIT = 56 * 2**20


def dot(left, right):
    return lax.dot_general(left, right, (((1,), (0,)), ((), ())), preferred_element_type=F32)


def dot_nt(left, right):
    return lax.dot_general(left, right, (((1,), (1,)), ((), ())), preferred_element_type=F32)


def dot_tn(left, right):
    return lax.dot_general(left, right, (((0,), (0,)), ((), ())), preferred_element_type=F32)


def norm_parts(hidden):
    centred = hidden - jnp.mean(hidden, axis=-1, keepdims=True)
    variance = jnp.mean(centred * centred, axis=-1, keepdims=True)
    scale = lax.rsqrt(variance + EPSILON)
    return centred * scale, scale


def norm_back(grad, normed, scale, gain):
    scaled = grad * gain
    along = jnp.mean(scaled * normed, axis=-1, keepdims=True)
    return (scaled - jnp.mean(scaled, axis=-1, keepdims=True) - normed * along) * scale


GELU_A = 0.7978845608028654
GELU_B = 0.044715


def gelu_parts(value):
    square = value * value
    bent = jnp.tanh(GELU_A * value * (1.0 + GELU_B * square))
    half = 0.5 * (1.0 + bent)
    slope = half + 0.5 * value * (1.0 - bent * bent) * (GELU_A * (1.0 + 3.0 * GELU_B * square))
    return value * half, slope


def gelu_only(value):
    bent = jnp.tanh(GELU_A * value * (1.0 + GELU_B * value * value))
    return 0.5 * value * (1.0 + bent)


def lane_is(shape, low, high):
    lane = lax.broadcasted_iota(jnp.int32, shape, len(shape) - 1)
    return (lane >= low) & (lane < high)


def project_kernel(core, half, peer, pos, seg, slots, wq, bq, wk, wv, bv, keys, values, queries, context, probs, picked):
    width = keys.shape[1]
    mine = pl.ds(pl.multiple_of(core[0] * width, 128), width)
    count = slots.shape[0]
    tokens_half = half.shape[0]
    chosen = jnp.where(slots[...] == pos[...], 1.0, 0.0).astype(BF16)
    rows = dot(chosen[:, :tokens_half], half[...]) + dot(chosen[:, tokens_half:], peer[...])
    rows = rows.astype(BF16)
    picked[...] = rows
    queries[...] = (dot(rows, wq[:, mine]) + bq[:, mine]).astype(BF16)
    for place, part in ((0, half), (tokens_half, peer)):
        for start in range(0, tokens_half, 256):
            block = part[start : start + 256, :]
            there = slice(place + start, place + start + 256)
            keys[there, :] = dot(block, wk[:, mine]).astype(BF16)
            values[there, :] = (dot(block, wv[:, mine]) + bv[:, mine]).astype(BF16)
    sequence = lax.broadcasted_iota(jnp.int32, (count, 1), 0) // (count // 2)
    same = seg[...] == sequence
    for pair in range(width // 128):
        lanes = slice(pair * 128, pair * 128 + 128)
        pair_queries = queries[:, lanes].astype(F32) * 0.125
        pair_keys, pair_values = keys[:, lanes], values[:, lanes]
        outs = []
        for side in range(2):
            keep = lane_is((count, 128), side * 64, side * 64 + 64)
            head_queries = jnp.where(keep, pair_queries, 0.0).astype(BF16)
            scores = jnp.where(same, dot_nt(head_queries, pair_keys), MASKED_SCORE)
            weights = jnp.exp(scores - jnp.max(scores, axis=-1, keepdims=True))
            share = weights / jnp.sum(weights, axis=-1, keepdims=True)
            probs[pair * 2 + side] = share
            outs.append(dot(share.astype(BF16), pair_values))
        first = lane_is((count, 128), 0, 64)
        context[:, lanes] = jnp.where(first, outs[0], outs[1]).astype(BF16)


def masked_kernel(core, ctx_own, ctx_peer, picked, cot_half, cot_peer, pos, slots, wo, bo, g1, s1, wup, bup, wdown, bdown, g2, s2, normed_low, feed, branch_low, grad_h1, small):
    count, width = ctx_own.shape
    hidden = wup.shape[1]
    model = wup.shape[0]
    tokens_half = cot_half.shape[0]
    mine = pl.multiple_of(core[0] * count, 16)
    is_first = core[0] == 0
    left = jnp.where(is_first, ctx_own[...], ctx_peer[...])
    right = jnp.where(is_first, ctx_peer[...], ctx_own[...])
    branch = dot(left, wo[:width, :]) + dot(right, wo[width:, :]) + bo[...]
    h1 = picked[pl.ds(mine, count), :].astype(F32) + branch
    n1, r1 = norm_parts(h1)
    y1 = n1 * g1[...] + s1[...]
    y1_low = y1.astype(BF16)
    normed_low[...] = y1_low
    total = y1 + bdown[...]
    slopes = []
    step = model
    for start in range(0, hidden, step):
        pre = dot(y1_low, wup[:, start : start + step]) + bup[:, start : start + step]
        act, slope = gelu_parts(pre)
        slopes.append(slope)
        total = total + dot(act.astype(BF16), wdown[start : start + step, :])
    n2, r2 = norm_parts(total)
    chosen = jnp.where(slots[pl.ds(mine, count), :] == pos[...], 1.0, 0.0).astype(BF16)
    grad = dot(chosen[:, :tokens_half], cot_half[...]) + dot(chosen[:, tokens_half:], cot_peer[...])
    gh2 = norm_back(grad, n2, r2, g2[...])
    gf = gh2.astype(BF16)
    feed[...] = gf
    gy1 = gh2
    small[...] = jnp.zeros_like(small)
    for place, start in enumerate(range(0, hidden, step)):
        ga = dot_nt(gf, wdown[start : start + step, :])
        gp = (ga * slopes[place]).astype(BF16)
        small[place : place + 1, :] = jnp.sum(gp.astype(F32), axis=0, keepdims=True)
        gy1 = gy1 + dot_nt(gp, wup[:, start : start + step])
    gh1 = norm_back(gy1, n1, r1, g1[...])
    grad_h1[...] = gh1
    gb = gh1.astype(BF16)
    branch_low[...] = gb
    base = hidden // step
    for place, value in enumerate((gy1 * n1, gy1, grad * n2, grad, gb.astype(F32), gf.astype(F32))):
        small[base + place : base + place + 1, :] = jnp.sum(value, axis=0, keepdims=True)


def back_kernel(core, keys, values, queries, context, probs, picked, gb_own, gb_peer, gh1, half, peer, pos_col, slots_row, wq, wk, wv, wo, grads, igrad_own, igrad_peer, bias, dq_low, dk_low, dv_low):
    width = keys.shape[1]
    count = queries.shape[0]
    own = gb_own.shape[0]
    tokens_half = half.shape[0]
    is_first = core[0] == 0
    mine = pl.ds(pl.multiple_of(core[0] * width, 128), width)
    mine_rows = pl.ds(pl.multiple_of(core[0] * width, 128), width)
    top = jnp.where(is_first, gb_own[...], gb_peer[...])
    low = jnp.where(is_first, gb_peer[...], gb_own[...])
    gb = jnp.concatenate([top, low], axis=0)
    gctx = dot_nt(gb, wo[mine_rows, :]).astype(BF16)
    for pair in range(width // 128):
        lanes = slice(pair * 128, pair * 128 + 128)
        pair_keys, pair_values, pair_queries = keys[:, lanes], values[:, lanes], queries[:, lanes]
        pair_gctx = gctx[:, lanes]
        dqs, dks, dvs = [], [], []
        for side in range(2):
            keep = lane_is((count, 128), side * 64, side * 64 + 64)
            head_gctx = jnp.where(keep, pair_gctx.astype(F32), 0.0).astype(BF16)
            share = probs[pair * 2 + side]
            gp = dot_nt(head_gctx, pair_values)
            spread = jnp.sum(share * gp, axis=-1, keepdims=True)
            gs = (share * (gp - spread)).astype(BF16)
            dqs.append(dot(gs, pair_keys))
            dks.append(dot_tn(gs, pair_queries))
            dvs.append(dot_tn(share.astype(BF16), pair_gctx))
        first = lane_is((count, 128), 0, 64)
        dq_low[:, lanes] = (jnp.where(first, dqs[0], dqs[1]) * 0.125).astype(BF16)
        first = lane_is((2 * tokens_half, 128), 0, 64)
        dk_low[:, lanes] = (jnp.where(first, dks[0], dks[1]) * 0.125).astype(BF16)
        dv_low[:, lanes] = jnp.where(first, dvs[0], dvs[1]).astype(BF16)
    grads[1] = dot_tn(picked[...], dq_low[...]).astype(BF16)
    gwo = dot_tn(context[...], gb).astype(BF16)
    grads[0, :width, :] = gwo[:, :width]
    grads[0, width:, :] = gwo[:, width:]
    for place, part in ((2, dk_low), (3, dv_low)):
        total = dot_tn(half[...], part[:tokens_half, :]) + dot_tn(peer[...], part[tokens_half:, :])
        grads[place] = total.astype(BF16)
    bias[0:1, :] = jnp.sum(dq_low[...].astype(F32), axis=0, keepdims=True)
    bias[1:2, :] = jnp.sum(dv_low[...].astype(F32), axis=0, keepdims=True)
    spread_rows = dot_nt(dq_low[...], wq[:, mine])
    zero = jnp.zeros((own, wq.shape[0]), F32)
    spread_rows = spread_rows + jnp.concatenate(
        [jnp.where(is_first, gh1[...], zero), jnp.where(is_first, zero, gh1[...])], axis=0
    )
    high = spread_rows.astype(BF16)
    rest = (spread_rows - high.astype(F32)).astype(BF16)
    for start in range(0, 2 * tokens_half, 256):
        here = slice(start, start + 256)
        chosen = jnp.where(pos_col[here, :] == slots_row[...], 1.0, 0.0).astype(BF16)
        total = dot(chosen, high) + dot(chosen, rest)
        total = total + dot_nt(dk_low[here, :], wk[:, mine]) + dot_nt(dv_low[here, :], wv[:, mine])
        if start < tokens_half:
            igrad_own[here, :] = total
        else:
            igrad_peer[start - tokens_half : start - tokens_half + 256, :] = total.astype(BF16)


def attend_kernel(core, half, peer, seg, seg_col, keys, values, wq, bq, own, other):
    width = keys.shape[1]
    mine = pl.ds(pl.multiple_of(core[0] * width, 128), width)
    tile = 256
    for part, out in ((half, own), (peer, other)):
        place = 0 if part is half else half.shape[0]

        def body(step, carry, part=part, out=out, place=place):
            here = pl.ds(pl.multiple_of(step * tile, tile), tile)
            queries = (dot(part[here, :], wq[:, mine]) + bq[:, mine]).astype(BF16).astype(F32) * 0.125
            same = seg_col[pl.ds(pl.multiple_of(place + step * tile, tile), tile), :] == seg[...]
            for pair in range(width // 128):
                lanes = slice(pair * 128, pair * 128 + 128)
                outs = []
                for side in range(2):
                    keep = lane_is((tile, 128), side * 64, side * 64 + 64)
                    head_queries = jnp.where(keep, queries[:, lanes], 0.0).astype(BF16)
                    scores = jnp.where(same, dot_nt(head_queries, keys[:, lanes]), MASKED_SCORE)
                    weights = jnp.exp(scores - jnp.max(scores, axis=-1, keepdims=True))
                    total = jnp.sum(weights, axis=-1, keepdims=True)
                    outs.append(dot(weights.astype(BF16), values[:, lanes]) / total)
                first = lane_is((tile, 128), 0, 64)
                out[here, lanes] = jnp.where(first, outs[0], outs[1]).astype(BF16)
            return carry

        lax.fori_loop(0, part.shape[0] // tile, body, 0)


def feed_kernel(core, ctx_own, ctx_peer, half, wo, bo, g1, s1, wup, bup, wdown, bdown, g2, s2, own, other):
    width = ctx_own.shape[1]
    hidden, model = wdown.shape
    is_first = core[0] == 0
    tile = own.shape[0]
    for start, out in ((0, own), (tile, other)):
        here = slice(start, start + tile)
        left = jnp.where(is_first, ctx_own[here, :], ctx_peer[here, :])
        right = jnp.where(is_first, ctx_peer[here, :], ctx_own[here, :])
        branch = dot(left, wo[:width, :]) + dot(right, wo[width:, :]) + bo[...]
        n1, _ = norm_parts(half[here, :].astype(F32) + branch)
        y1 = n1 * g1[...] + s1[...]
        y1_low = y1.astype(BF16)
        total = y1 + bdown[...]
        for place in range(0, hidden, model):
            pre = dot(y1_low, wup[:, place : place + model]) + bup[:, place : place + model]
            total = total + dot(gelu_only(pre).astype(BF16), wdown[place : place + model, :])
        n2, _ = norm_parts(total)
        out[...] = (n2 * g2[...] + s2[...]).astype(BF16)


def hidden_kernel(slot, normed, feed, wup, bup, wdown, out):
    units = out.shape[0]
    model = normed.shape[1]
    mine = pl.ds(pl.multiple_of(slot[0] * units, 128), units)
    pre = dot(normed[...], wup[:, mine]) + bup[:, mine]
    act, slope = gelu_parts(pre)
    ga = dot_nt(feed[...], wdown[mine, :])
    gp = (ga * slope).astype(BF16)
    out[:, :model] = dot_tn(gp, normed[...]).astype(BF16)
    out[:, model:] = dot_tn(act.astype(BF16), feed[...]).astype(BF16)


def place_here():
    row, seq = lax.axis_index("rows"), lax.axis_index("seq")
    return row // 2, row % 2, seq // 2, seq % 2


def device(z, x, y, core):
    return (z * 2 + x, y * 2 + core)


def layer_kernel(
    tokens, cotangent, segments, slots, vecs, wq, wk, wv, wo, wup, wdown,
    layer_out, input_grad, out_o, out_q, out_k, out_v, hidden_out, small_out,
    xs, cs, wq_v, wk_v, wv_v, wo_v, wup_v, wdown_v, keys, values, queries, context, probs, picked, chosen, ctx_both, gb_both,
    slopes, dq_low, dkv_low, grads, hidden_grads, hidden_in, fac_normed, fac_feed, grad_h1, small_in, small_z,
    all_queries, all_context, ctx_in, total, y1_keep, out_send, dx_send, dx_in, dx_own, igrad_send, igrad_in,
    in_o, in_q, in_k, in_v, mid_o, mid_q, mid_k, mid_v, local_sem, send_sem, recv_sem,
):
    z, x, y, core = place_here()
    row = y
    stretch, model = tokens.shape[1:]
    half = 2 * stretch
    full = 2 * half
    width = wq_v.shape[1]
    masks = slots.shape[2]
    count = 2 * masks
    hidden = wup.shape[1]
    parts = hidden // model
    units = hidden_out.shape[0]
    others = [(z + k) % 4 for k in (1, 2, 3)]
    at_y, at_x, twin = device(z, x, 1 - y, core), device(z, 1 - x, y, core), device(z, x, y, 1 - core)
    columns = [device(o, x, y, core) for o in others]
    mine = pl.ds(pl.multiple_of(core * width, 128), width)
    my_slots = pl.ds(pl.multiple_of(core * masks, 16), masks)
    twin_slots = pl.ds(pl.multiple_of((1 - core) * masks, 16), masks)
    pending = []

    def local(src, dst, index):
        copy = pltpu.make_async_copy(src, dst, local_sem.at[index])
        copy.start()
        return copy

    def remote(src, dst, index, target):
        return pltpu.make_async_remote_copy(
            src_ref=src, dst_ref=dst, send_sem=send_sem.at[index], recv_sem=recv_sem.at[index],
            device_id=target, device_id_type=MESH,
        )

    def push(src, dst, index, target):
        copy = remote(src, dst, index, target)
        copy.start()
        pending.append(copy)
        return copy

    def vector(index):
        return vecs[index : index + 1, :]

    def half_vector(index):
        return vecs[index : index + 1, mine]

    own_tokens = local(tokens.at[row], xs.at[pl.ds(0, stretch)], 0)
    get_wk = local(wk.at[:, mine], wk_v, 1)
    get_wv = local(wv.at[:, mine], wv_v, 2)
    get_wq = local(wq.at[:, mine], wq_v, 3)
    own_cot = local(cotangent.at[row], cs.at[pl.ds(0, stretch)], 4)
    get_wo = local(wo, wo_v, 5)
    get_up = local(wup, wup_v, 6)
    get_down = local(wdown, wdown_v, 7)

    barrier = pltpu.get_barrier_semaphore()
    for cx in range(2):
        for cy in range(2):
            for cc in range(2):
                @pl.when(jnp.logical_not((cx == x) & (cy == y) & (cc == core)))
                def _(cx=cx, cy=cy, cc=cc):
                    pl.semaphore_signal(barrier, inc=1, device_id=device(z, cx, cy, cc), device_id_type=MESH)
    for target in columns:
        pl.semaphore_signal(barrier, inc=1, device_id=target, device_id_type=MESH)
    pl.semaphore_wait(barrier, 10)

    piece = stretch // 2
    tok_y = [
        push(tokens.at[1 - row, pl.ds(k * piece, piece)], xs.at[pl.ds(stretch + k * piece, piece)], k, at_y) for k in range(2)
    ]
    tok_c = push(tokens.at[row], xs.at[pl.ds(half, stretch)], 2, twin)
    cot_y = push(cotangent.at[1 - row], cs.at[pl.ds(stretch, stretch)], 3, at_y)
    cot_c = push(cotangent.at[row], cs.at[pl.ds(half, stretch)], 4, twin)

    def key_values(start):
        here = pl.ds(start, stretch)
        block = xs[here, :]
        keys[here, :] = dot(block, wk_v[...]).astype(BF16)
        values[here, :] = (dot(block, wv_v[...]) + half_vector(5)).astype(BF16)

    blocks = [2 * y + core, 2 * (1 - y) + core, 2 * y + 1 - core, 2 * (1 - y) + 1 - core]
    lane = lax.broadcasted_iota(jnp.int32, (1, stretch), 1)
    pos_row = jnp.concatenate([lane + block * stretch for block in blocks], axis=1)
    seg_here = segments[pl.ds(row, 1), :]
    split = jnp.sum((1 - seg_here).astype(F32), axis=1, keepdims=True)
    pos_row = pos_row.astype(F32)
    seg_row = jnp.where(pos_row >= split, 1.0, 0.0)
    slot_rows = slots[row].astype(F32)
    diagonal = lax.broadcasted_iota(jnp.int32, (masks, masks), 0) == lax.broadcasted_iota(jnp.int32, (masks, masks), 1)
    for sequence in range(2):
        column = jnp.sum(jnp.where(diagonal, slot_rows[sequence : sequence + 1, :], 0.0), axis=1, keepdims=True)
        chosen[sequence * masks : (sequence + 1) * masks, :] = jnp.where(column == pos_row, 1.0, 0.0).astype(BF16)

    own_tokens.wait()
    get_wk.wait()
    get_wv.wait()
    key_values(0)
    tok_c.wait_recv()
    key_values(half)
    forward = []
    for k in range(2):
        tok_y[k].wait_recv()
        src = xs.at[pl.ds(stretch + k * piece, piece)]
        forward.append(push(src, xs.at[pl.ds(half + stretch + k * piece, piece)], 5 + k, twin))
    key_values(stretch)
    for copy in forward:
        copy.wait_recv()
    key_values(half + stretch)

    rows = dot(chosen[...], xs[...]).astype(BF16)
    picked[...] = rows
    get_wq.wait()
    queries[...] = (dot(rows, wq_v[...]) + half_vector(4)).astype(BF16)
    sequence = lax.broadcasted_iota(jnp.int32, (count, 1), 0) // masks
    same = seg_row == sequence.astype(F32)
    pairs = width // 128
    for pair in range(pairs):
        lanes = slice(pair * 128, pair * 128 + 128)
        pair_queries = queries[:, lanes].astype(F32) * 0.125
        pair_keys, pair_values = keys[:, lanes], values[:, lanes]
        outs = []
        for side in range(2):
            keep = lane_is((count, 128), side * 64, side * 64 + 64)
            head_queries = jnp.where(keep, pair_queries, 0.0).astype(BF16)
            scores = jnp.where(same, dot_nt(head_queries, pair_keys), MASKED_SCORE)
            weights = jnp.exp(scores - jnp.max(scores, axis=-1, keepdims=True))
            share = weights / jnp.sum(weights, axis=-1, keepdims=True)
            probs[pair * 2 + side] = share
            outs.append(dot(share.astype(BF16), pair_values))
        first = lane_is((count, 128), 0, 64)
        context[:, lanes] = jnp.where(first, outs[0], outs[1]).astype(BF16)
    ctx_both[core] = context[my_slots, :]
    ctx_c = push(context.at[twin_slots], ctx_both.at[core], 7, twin)

    own_cot.wait()
    cot_y.wait_recv()
    cot_f = push(cs.at[pl.ds(stretch, stretch)], cs.at[pl.ds(half + stretch, stretch)], 8, twin)
    for start in range(0, full, stretch):
        value = (dot(xs[start : start + stretch, :], wq_v[...]) + half_vector(4)).astype(BF16)
        all_queries[start : start + stretch, :] = (value.astype(F32) * 0.125).astype(BF16)
    get_wo.wait()
    ctx_c.wait_recv()

    branch = dot(ctx_both[0], wo_v[:width, :]) + dot(ctx_both[1], wo_v[width:, :]) + vector(6)
    n1, r1 = norm_parts(picked[my_slots, :].astype(F32) + branch)
    y1 = n1 * vector(7) + vector(8)
    y1_low = y1.astype(BF16)
    fac_normed[core, z] = y1_low
    spot = fac_normed.at[core, z]
    norm_z = [push(spot, spot, 9 + k, columns[k]) for k in range(3)]
    get_up.wait()
    get_down.wait()
    sum2 = y1 + vector(9)
    for part in range(parts):
        there = slice(part * model, (part + 1) * model)
        act, slope = gelu_parts(dot(y1_low, wup_v[:, there]) + vector(part))
        slopes[part] = slope
        sum2 = sum2 + dot(act.astype(BF16), wdown_v[there, :])
    n2, r2 = norm_parts(sum2)
    cot_c.wait_recv()
    cot_f.wait_recv()
    grad = dot(chosen[my_slots, :], cs[...])
    gh2 = norm_back(grad, n2, r2, vector(10))
    gf = gh2.astype(BF16)
    fac_feed[core, z] = gf
    spot = fac_feed.at[core, z]
    feed_z = [push(spot, spot, 12 + k, columns[k]) for k in range(3)]
    gy1 = gh2
    small_in[0] = jnp.zeros(small_in.shape[1:], F32)
    for part in range(parts):
        there = slice(part * model, (part + 1) * model)
        gp = (dot_nt(gf, wdown_v[there, :]) * slopes[part]).astype(BF16)
        small_in[0, part : part + 1, :] = jnp.sum(gp.astype(F32), axis=0, keepdims=True)
        gy1 = gy1 + dot_nt(gp, wup_v[:, there])
    gh1 = norm_back(gy1, n1, r1, vector(7))
    grad_h1[...] = gh1
    gb = gh1.astype(BF16)
    gb_both[core] = gb
    gb_c = push(gb_both.at[core], gb_both.at[core], 15, twin)
    for place, value in enumerate((gy1 * n1, gy1, grad * n2, grad, gb.astype(F32), gf.astype(F32))):
        small_in[0, parts + place : parts + place + 1, :] = jnp.sum(value, axis=0, keepdims=True)
    gb_c.wait_recv()

    spots = {"x": x, "y": y, "z": z}
    sizes = {"x": 2, "y": 2, "z": 4}
    dims = {"x": [at_x], "y": [at_y], "z": columns}
    orders = ["xyz", "zyx", "xyz", "xyz"]
    ins = [in_o, in_q, in_k, in_v]
    mids = [mid_o, mid_q, mid_k, mid_v]
    outs = [out_o, out_q, out_k, out_v]

    def regions(job):
        base, size, found = 0, model, [(0, model)]
        for dim in orders[job]:
            size = size // sizes[dim]
            base = base + spots[dim] * size
            found.append((base, size))
        return found

    def in_place(job, stage):
        at, size = 0, model
        for dim in orders[job][:stage]:
            size = size // sizes[dim]
            at += size * (sizes[dim] - 1)
        return at, size // sizes[orders[job][stage]]

    def mid_place(job, stage):
        at, size = 0, model
        for dim in orders[job][:stage]:
            size = size // sizes[dim]
            at += size
        return at

    def out_at(job, base, size):
        if job == 0:
            side = base // width
            offset = base - side * width
            at = pl.ds(pl.multiple_of(core * width + offset, 16), size)
            return outs[0].at[at, pl.ds(pl.multiple_of(side * width, 128), width)]
        return outs[job].at[pl.ds(pl.multiple_of(base, 16), size), mine]

    def reduce_copies(job, stage):
        dim = orders[job][stage]
        at, size = in_place(job, stage)
        copies = []
        for k, target in enumerate(dims[dim]):
            other = (spots[dim] + k + 1) % sizes[dim]
            if stage == 0:
                src = grads.at[job, pl.ds(pl.multiple_of(other * size, 16), size)]
            else:
                src = mids[job].at[pl.ds(pl.multiple_of(mid_place(job, stage - 1) + other * size, 16), size)]
            dst = ins[job].at[pl.ds(at + k * size, size)]
            copies.append(remote(src, dst, 40 + job * 20 + stage * 3 + k, target))
        return copies

    def reduce_start(job, stage):
        for copy in reduce_copies(job, stage):
            copy.start()

    def reduce_end(job, stage):
        for copy in reduce_copies(job, stage):
            copy.wait()
        dim = orders[job][stage]
        at, size = in_place(job, stage)
        here = spots[dim] * size
        if stage == 0:
            value = grads[job, pl.ds(pl.multiple_of(here, 16), size)].astype(F32)
        else:
            value = mids[job][pl.ds(pl.multiple_of(mid_place(job, stage - 1) + here, 16), size)].astype(F32)
        for k in range(len(dims[dim])):
            value = value + ins[job][pl.ds(at + k * size, size)].astype(F32)
        value = value.astype(BF16)
        if stage < 2:
            mids[job][pl.ds(mid_place(job, stage), size)] = value
            reduce_start(job, stage + 1)
        else:
            base, _ = regions(job)[3]
            out_at(job, base, size)[...] = value
            gather_start(job, 2)

    def gather_copies(job, stage):
        base, size = regions(job)[stage + 1]
        spot = out_at(job, base, size)
        return [
            remote(spot, spot, 40 + job * 20 + 9 + stage * 3 + k, target)
            for k, target in enumerate(dims[orders[job][stage]])
        ]

    def twin_copy(job):
        spot = outs[0].at[mine, :] if job == 0 else outs[job].at[:, mine]
        return remote(spot, spot, 40 + job * 20 + 18, twin)

    def gather_start(job, stage):
        for copy in gather_copies(job, stage):
            copy.start()

    def gather_end(job, stage):
        for copy in gather_copies(job, stage):
            copy.wait()
        if stage > 0:
            gather_start(job, stage - 1)
        else:
            twin_copy(job).start()

    def small_copies(stage):
        if stage < 3:
            target = (twin, at_y, at_x)[stage]
            return [remote(small_in.at[2 * stage], small_in.at[2 * stage + 1], 16 + stage, target)]
        return [remote(small_in.at[6], small_z.at[z], 19 + k, target) for k, target in enumerate(columns)]

    def small_start(stage):
        for copy in small_copies(stage):
            copy.start()

    def small_end(stage):
        for copy in small_copies(stage):
            copy.wait()
        if stage < 3:
            small_in[2 * stage + 2] = small_in[2 * stage] + small_in[2 * stage + 1]
            if stage == 2:
                small_z[z] = small_in[6]
            small_start(stage + 1)
        else:
            small_out[...] = (small_z[0] + small_z[1]) + (small_z[2] + small_z[3])

    source = x * 2 + y

    def factor_copies():
        return [remote(ref.at[core], ref.at[core], 22 + k, twin) for k, ref in enumerate((fac_normed, fac_feed))]

    def factors_on():
        for copy in norm_z + feed_z:
            copy.wait_recv()
        for copy in factor_copies():
            copy.start()

    def is_me(cy, cc):
        return (core == x) & (cy == y) & (cc == core)

    def hidden_copy(cy, cc):
        part = hidden_grads.at[pl.ds((cy * 2 + cc) * units, units)]
        return pltpu.make_async_remote_copy(
            src_ref=part, dst_ref=hidden_in.at[source], send_sem=send_sem.at[24 + cy * 2 + cc], recv_sem=recv_sem.at[24 + source],
            device_id=device(z, core, cy, cc), device_id_type=MESH,
        )

    def hidden_make():
        for copy in factor_copies():
            copy.wait()
        slot = z * 2 + core
        size = hidden_grads.shape[0]
        normed = fac_normed[...].reshape(8 * masks, model)
        feed = fac_feed[...].reshape(8 * masks, model)
        at = pl.ds(pl.multiple_of(slot * size, 128), size)
        act, slope = gelu_parts(dot(normed, wup_v[:, at]) + vecs[pl.ds(z, 1), mine])
        gp = (dot_nt(feed, wdown_v[at, :]) * slope).astype(BF16)
        hidden_grads[:, :model] = dot_tn(gp, normed).astype(BF16)
        hidden_grads[:, model:] = dot_tn(act.astype(BF16), feed).astype(BF16)
        for cy in range(2):
            for cc in range(2):
                @pl.when(jnp.logical_not(is_me(cy, cc)))
                def _(cy=cy, cc=cc):
                    hidden_copy(cy, cc).start()

                @pl.when(is_me(cy, cc))
                def _(cy=cy, cc=cc):
                    hidden_in[source] = hidden_grads[pl.ds((cy * 2 + cc) * units, units)]

    def hidden_end():
        for cy in range(2):
            for cc in range(2):
                @pl.when(jnp.logical_not(is_me(cy, cc)))
                def _(cy=cy, cc=cc):
                    hidden_copy(cy, cc).wait_send()
        for cx in range(2):
            for cy in range(2):
                @pl.when(jnp.logical_not((cx == x) & (cy == y) & (core == x)))
                def _(cx=cx, cy=cy):
                    slot = hidden_in.at[cx * 2 + cy]
                    pltpu.make_async_remote_copy(
                        src_ref=slot, dst_ref=slot, send_sem=send_sem.at[24], recv_sem=recv_sem.at[24 + cx * 2 + cy],
                        device_id=twin, device_id_type=MESH,
                    ).wait_recv()
        value = hidden_in[0].astype(F32)
        for k in range(1, 4):
            value = value + hidden_in[k].astype(F32)
        hidden_out[...] = value

    gb = gb_both[...].reshape(count, model)
    gctx = dot_nt(gb, wo_v[mine, :]).astype(BF16)
    value = dot_tn(context[...], gb).astype(BF16)
    grads[0, :width, :] = value[:, :width]
    grads[0, width:, :] = value[:, width:]
    reduce_start(0, 0)
    for pair in range(pairs):
        lanes = slice(pair * 128, pair * 128 + 128)
        pair_keys, pair_values, pair_queries = keys[:, lanes], values[:, lanes], queries[:, lanes]
        pair_gctx = gctx[:, lanes]
        dqs, dks, dvs = [], [], []
        for side in range(2):
            keep = lane_is((count, 128), side * 64, side * 64 + 64)
            head_gctx = jnp.where(keep, pair_gctx.astype(F32), 0.0).astype(BF16)
            share = probs[pair * 2 + side]
            gp = dot_nt(head_gctx, pair_values)
            spread = jnp.sum(share * gp, axis=-1, keepdims=True)
            gs = (share * (gp - spread)).astype(BF16)
            dqs.append(dot(gs, pair_keys))
            dks.append(dot_tn(gs, pair_queries))
            dvs.append(dot_tn(share.astype(BF16), pair_gctx))
        first = lane_is((count, 128), 0, 64)
        dq_low[:, lanes] = (jnp.where(first, dqs[0], dqs[1]) * 0.125).astype(BF16)
        first = lane_is((full, 128), 0, 64)
        dkv_low[:, lanes] = (jnp.where(first, dks[0], dks[1]) * 0.125).astype(BF16)
        dkv_low[:, width + pair * 128 : width + pair * 128 + 128] = jnp.where(first, dvs[0], dvs[1]).astype(BF16)
        if pair == 0:
            factors_on()
        if pair == 1:
            reduce_end(0, 0)
    for start in range(0, model, 256):
        value = dot_tn(xs[:, start : start + 256], dkv_low[...]).astype(BF16)
        grads[2, start : start + 256, :] = value[:, :width]
        grads[3, start : start + 256, :] = value[:, width:]
    reduce_start(2, 0)
    reduce_start(3, 0)
    grads[1] = dot_tn(picked[...], dq_low[...]).astype(BF16)
    reduce_start(1, 0)
    reduce_end(0, 1)
    small_in[0, parts + 6 : parts + 7, mine] = jnp.sum(dq_low[...].astype(F32), axis=0, keepdims=True)
    small_in[0, parts + 7 : parts + 8, mine] = jnp.sum(dkv_low[:, width:].astype(F32), axis=0, keepdims=True)
    small_start(0)

    spread_rows = dot_nt(dq_low[...], wq_v[...])
    zero = jnp.zeros((masks, model), F32)
    is_first = core == 0
    gh1 = grad_h1[...]
    spread_rows = spread_rows + jnp.concatenate([jnp.where(is_first, gh1, zero), jnp.where(is_first, zero, gh1)], axis=0)
    high = spread_rows.astype(BF16)
    rest = (spread_rows - high.astype(F32)).astype(BF16)
    dx_c = None
    for start in (half, half + stretch, 0, stretch):
        here = slice(start, start + stretch)
        value = dot_tn(chosen[:, here], high) + dot_tn(chosen[:, here], rest)
        value = value + dot_nt(dkv_low[here, :width], wk_v[...]) + dot_nt(dkv_low[here, width:], wv_v[...])
        if start < half:
            dx_own[here, :] = value
        else:
            dx_send[start - half : start - half + stretch, :] = value.astype(BF16)
            if start > half:
                dx_c = push(dx_send, dx_in, 28, twin)

    igrad_copy = remote(igrad_send, igrad_in, 29, at_y)

    def igrad_step():
        dx_c.wait_recv()
        input_grad[row] = dx_own[:stretch, :] + dx_in[:stretch, :].astype(F32)
        igrad_send[...] = (dx_own[stretch:, :] + dx_in[stretch:, :].astype(F32)).astype(BF16)
        remote(igrad_send, igrad_in, 29, at_y).start()

    hidden_make()

    def hooks(step, table):
        for at, actions in table.items():
            @pl.when(step == at)
            def _(actions=actions):
                for action in actions:
                    action[0](*action[1:])

    def ctx_copy():
        return remote(all_context.at[pl.ds(half, half)], ctx_in, 30, twin)

    attend_table = {
        0: [(reduce_end, 2, 0), (small_end, 0)],
        1: [(reduce_end, 1, 0), (igrad_step,)],
        2: [(reduce_end, 0, 2), (small_end, 1)],
        3: [(reduce_end, 3, 0), (reduce_end, 2, 1)],
        4: [(gather_end, 0, 2), (reduce_end, 1, 1)],
        5: [(reduce_end, 2, 2), (small_end, 2)],
        6: [(reduce_end, 3, 1), (gather_end, 0, 1)],
        7: [(reduce_end, 1, 2), (gather_end, 2, 2)],
        8: [(reduce_end, 3, 2), (small_end, 3)],
        9: [(gather_end, 2, 1), (gather_end, 1, 2)],
        10: [(gather_end, 3, 2)],
        11: [(gather_end, 0, 0), (gather_end, 1, 1)],
    }
    feed_table = {
        1: [(gather_end, 3, 1)],
        3: [(gather_end, 2, 0)],
        5: [(gather_end, 1, 0)],
        6: [(hidden_end,)],
    }

    def attend_step(step, carry):
        tile, pair = (step // pairs + 2) % 4, step % pairs
        here = pl.ds(pl.multiple_of(tile * stretch, stretch), stretch)
        lanes = pl.ds(pl.multiple_of(pair * 128, 128), 128)
        block = 2 * (y + (tile % 2) * (1 - 2 * y)) + core + (tile // 2) * (1 - 2 * core)
        place = lax.broadcasted_iota(jnp.int32, (stretch, 1), 0) + block * stretch
        seg_col = jnp.where(place.astype(F32) >= split, 1.0, 0.0)
        same_here = seg_col == seg_row
        pair_queries = all_queries[here, lanes].astype(F32)
        pair_keys, pair_values = keys[:, lanes], values[:, lanes]
        found = []
        for side in range(2):
            keep = lane_is((stretch, 128), side * 64, side * 64 + 64)
            head_queries = jnp.where(keep, pair_queries, 0.0).astype(BF16)
            scores = jnp.where(same_here, dot_nt(head_queries, pair_keys), MASKED_SCORE)
            weights = jnp.exp(scores - jnp.max(scores, axis=-1, keepdims=True))
            found.append(dot(weights.astype(BF16), pair_values) / jnp.sum(weights, axis=-1, keepdims=True))
        first = lane_is((stretch, 128), 0, 64)
        all_context[here, lanes] = jnp.where(first, found[0], found[1]).astype(BF16)

        @pl.when(step == 2 * pairs - 1)
        def _():
            ctx_copy().start()

        hooks(step, attend_table)
        return carry

    lax.fori_loop(0, 4 * pairs, attend_step, 0)
    ctx_copy().wait()

    def out_copy():
        return remote(out_send, layer_out.at[row], 31, at_y)

    def feed_step(step, carry):
        tile, part = 1 - step // parts, step % parts
        here = pl.ds(pl.multiple_of(tile * stretch, stretch), stretch)

        @pl.when(part == 0)
        def _():
            left = jnp.where(is_first, all_context[here, :], ctx_in[here, :])
            right = jnp.where(is_first, ctx_in[here, :], all_context[here, :])
            here_branch = dot(left, wo_v[:width, :]) + dot(right, wo_v[width:, :]) + vector(6)
            normed, _ = norm_parts(xs[here, :].astype(F32) + here_branch)
            value = normed * vector(7) + vector(8)
            y1_keep[...] = value.astype(BF16)
            total[...] = value + vector(9)

        there = pl.ds(pl.multiple_of(part * model, model), model)
        pre = dot(y1_keep[...], wup_v[:, there]) + vecs[pl.ds(part, 1), :]
        total[...] += dot(gelu_only(pre).astype(BF16), wdown_v[there, :])

        @pl.when(part == parts - 1)
        def _():
            normed, _ = norm_parts(total[...])
            value = (normed * vector(10) + vector(11)).astype(BF16)

            @pl.when(tile == 1)
            def _():
                out_send[...] = value
                out_copy().start()

            @pl.when(tile == 0)
            def _():
                layer_out[row] = value

        hooks(step, feed_table)
        return carry

    lax.fori_loop(0, 2 * parts, feed_step, 0)
    gather_end(3, 0)
    igrad_copy.wait()
    input_grad[1 - row] = igrad_in[...].astype(F32)
    out_copy().wait()
    for job in range(4):
        twin_copy(job).wait()
    for copy in pending:
        copy.wait_send()


def vmem(count):
    return [pl.BlockSpec(memory_space=pltpu.VMEM)] * count


def local_call(body, outs, name, scratch=()):
    def call(core, *operands):
        return pl.pallas_call(
            body,
            out_shape=outs,
            in_specs=[pl.BlockSpec(memory_space=pltpu.SMEM)] + vmem(len(operands)),
            out_specs=vmem(len(outs)),
            scratch_shapes=list(scratch),
            compiler_params=pltpu.CompilerParams(vmem_limit_bytes=VMEM_LIMIT),
            name=name,
        )(core, *operands)

    return call


def outputs(layer_output, input_grad, grad_wq, grad_wk, grad_wv, grad_wo, hidden_grads, small):
    model = grad_wq.shape[0]
    base = small.shape[0] - 12
    vector = lambda index: small[index]
    return (
        layer_output,
        input_grad,
        grad_wq.astype(F32),
        vector(base + 6),
        grad_wk.astype(F32),
        grad_wv.astype(F32),
        vector(base + 7),
        grad_wo.astype(F32),
        vector(base + 4),
        vector(base),
        vector(base + 1),
        hidden_grads[:, :model].T,
        small[:base].reshape(-1),
        hidden_grads[:, model:],
        vector(base + 5),
        vector(base + 2),
        vector(base + 3),
    )


def layer_call(tokens, cotangent, segment_ids, mask_positions, vecs, wq, wk, wv, wo, wup, wdown):
    _, stretch, model = tokens.shape
    hidden = wup.shape[1]
    masks = mask_positions.shape[2]
    count, half, full, width = 2 * masks, 2 * stretch, 4 * stretch, model // 2
    units = hidden // 32
    shaped = jax.ShapeDtypeStruct
    low = lambda *shape: pltpu.VMEM(shape, BF16)
    wide = lambda *shape: pltpu.VMEM(shape, F32)
    scratch = [
        low(full, model), low(full, model), low(model, width), low(model, width), low(model, width), low(model, model),
        low(model, hidden), low(hidden, model), low(full, width), low(full, width), low(count, width), low(count, width),
        wide(HEADS // 2, count, full), low(count, model), low(count, full), low(2, masks, width), low(2, masks, model),
        wide(hidden // model, masks, model), low(count, width), low(full, model), low(4, model, width),
        low(4 * units, 2 * model), low(4, units, 2 * model), low(2, 4, masks, model), low(2, 4, masks, model),
        wide(masks, model), wide(7, 16, model), wide(4, 16, model),
        low(full, width), low(full, width), low(half, width), wide(stretch, model), low(stretch, model), low(stretch, model),
        low(half, model), low(half, model), wide(half, model), low(stretch, model), low(stretch, model),
    ]
    for order in ("xyz", "zyx", "xyz", "xyz"):
        size, at = model, 0
        for dim in order:
            ways = 4 if dim == "z" else 2
            size //= ways
            at += size * (ways - 1)
        scratch.append(low(at, width))
    for order in ("xyz", "zyx", "xyz", "xyz"):
        size, at = model, 0
        for dim in order[:2]:
            size //= 4 if dim == "z" else 2
            at += size
        scratch.append(low(at, width))
    scratch += [pltpu.SemaphoreType.DMA((8,)), pltpu.SemaphoreType.DMA((120,)), pltpu.SemaphoreType.DMA((120,))]
    anywhere = [pl.BlockSpec(memory_space=pl.ANY)]
    return pl.pallas_call(
        layer_kernel,
        out_shape=(
            shaped((2, stretch, model), BF16),
            shaped((2, stretch, model), F32),
            shaped((model, model), BF16),
            shaped((model, model), BF16),
            shaped((model, model), BF16),
            shaped((model, model), BF16),
            shaped((units, 2 * model), F32),
            shaped((16, model), F32),
        ),
        in_specs=anywhere * 2 + vmem(3) + anywhere * 6,
        out_specs=vmem(8),
        scratch_shapes=scratch,
        compiler_params=pltpu.CompilerParams(collective_id=0, has_side_effects=True, vmem_limit_bytes=62 * 2**20),
        name="layer",
    )(tokens, cotangent, segment_ids, mask_positions, vecs, wq, wk, wv, wo, wup, wdown)


def on_device(
    rows_total,
    tokens,
    cotangent,
    segment_ids,
    mask_positions,
    query_weight,
    query_bias,
    key_weight,
    value_weight,
    value_bias,
    output_weight,
    output_bias,
    first_gain,
    first_shift,
    up_weight,
    up_bias,
    down_weight,
    down_bias,
    second_gain,
    second_shift,
):
    if rows_total == 8:
        vecs = jnp.concatenate(
            [up_bias]
            + [query_bias, value_bias, output_bias, first_gain, first_shift, down_bias, second_gain, second_shift]
        ).reshape(-1, tokens.shape[2])
        layer_output, input_grad, go, gq, gk, gv, hidden_grads, small = layer_call(
            tokens, cotangent, segment_ids, mask_positions, vecs, query_weight, key_weight, value_weight, output_weight, up_weight, down_weight
        )
        return outputs(layer_output, input_grad, gq, gk, gv, go, hidden_grads, small)
    _, stretch, model = tokens.shape
    hidden = up_weight.shape[1]
    width = model // 2
    heads = HEADS // 2
    masks = mask_positions.shape[2]
    seq = lax.axis_index("seq")
    row = seq // 2
    core = seq % 2
    across = [(i, (i + 2) % 4) for i in range(4)]
    beside = [(i, i + 1 - 2 * (i % 2)) for i in range(4)]

    def swap(value):
        return lax.ppermute(value, "seq", across)

    def trade(value):
        return lax.ppermute(value, "seq", beside)

    def take(array, index):
        return lax.dynamic_index_in_dim(array, index, 0, keepdims=False)

    half = jnp.concatenate([take(tokens, row), swap(take(tokens, 1 - row))], axis=0)
    peer = trade(half)
    cot_half = jnp.concatenate([take(cotangent, row), swap(take(cotangent, 1 - row))], axis=0)
    cot_peer = trade(cot_half)
    blocks = jnp.stack([2 * row + core, 2 * (1 - row) + core, 2 * row + 1 - core, 2 * (1 - row) + 1 - core])
    positions = (blocks[:, None] * stretch + jnp.arange(stretch, dtype=jnp.int32)[None, :]).reshape(-1)
    segments = jnp.take(take(segment_ids, row).reshape(4, stretch), blocks, axis=0).reshape(-1)
    slots = take(mask_positions, row).reshape(-1)
    pos, seg, slot_col = positions[None, :], segments[None, :], slots[:, None]
    pos_col, seg_col, slot_row = positions[:, None], segments[:, None], slots[None, :]
    core_scalar = core.reshape(1).astype(jnp.int32)
    line = lambda value: value.reshape(1, -1)
    full = 4 * stretch
    count = 2 * masks
    shaped = jax.ShapeDtypeStruct

    keys, values, queries, context, probs, picked = local_call(
        project_kernel,
        (
            shaped((full, width), BF16),
            shaped((full, width), BF16),
            shaped((count, width), BF16),
            shaped((count, width), BF16),
            shaped((heads, count, full), F32),
            shaped((count, model), BF16),
        ),
        "project",
    )(core_scalar, half, peer, pos, seg, slot_col, query_weight, line(query_bias), key_weight, value_weight, line(value_bias))

    two = context.reshape(2, masks, width)
    ctx_peer = trade(take(two, 1 - core))
    normed_low, feed, branch_low, grad_h1, small = local_call(
        masked_kernel,
        (
            shaped((masks, model), BF16),
            shaped((masks, model), BF16),
            shaped((masks, model), BF16),
            shaped((masks, model), F32),
            shaped((16, model), F32),
        ),
        "masked",
    )(
        core_scalar, take(two, core), ctx_peer, picked, cot_half, cot_peer, pos, slot_col, output_weight, line(output_bias),
        line(first_gain), line(first_shift), up_weight, line(up_bias), down_weight, line(down_bias), line(second_gain), line(second_shift),
    )
    branch_peer = trade(branch_low)
    grads, igrad_own, igrad_peer, bias = local_call(
        back_kernel,
        (
            shaped((4, model, width), BF16),
            shaped((2 * stretch, model), F32),
            shaped((2 * stretch, model), BF16),
            shaped((2, width), F32),
        ),
        "back",
        [pltpu.VMEM((count, width), BF16), pltpu.VMEM((full, width), BF16), pltpu.VMEM((full, width), BF16)],
    )(
        core_scalar, keys, values, queries, context, probs, picked, branch_low, branch_peer, grad_h1, half, peer, pos_col, slot_row,
        query_weight, key_weight, value_weight, output_weight,
    )
    igrad = igrad_own + trade(igrad_peer).astype(F32)
    igrad_other = swap(igrad[stretch:].astype(BF16)).astype(F32)
    igrad_mine = igrad[:stretch]
    input_grad = jnp.where(row == 0, jnp.stack([igrad_mine, igrad_other]), jnp.stack([igrad_other, igrad_mine]))

    ctx_own, ctx_other = local_call(
        attend_kernel, (shaped((2 * stretch, width), BF16), shaped((2 * stretch, width), BF16)), "attend"
    )(core_scalar, half, peer, seg, seg_col, keys, values, query_weight, line(query_bias))
    out_mine, out_other = local_call(
        feed_kernel, (shaped((stretch, model), BF16), shaped((stretch, model), BF16)), "feed"
    )(
        core_scalar, ctx_own, trade(ctx_other), half, output_weight, line(output_bias), line(first_gain), line(first_shift),
        up_weight, line(up_bias), down_weight, line(down_bias), line(second_gain), line(second_shift),
    )
    out_other = swap(out_other)
    layer_output = jnp.where(row == 0, jnp.stack([out_mine, out_other]), jnp.stack([out_other, out_mine]))

    wide = jnp.zeros((2, model), F32)
    bias_rows = lax.dynamic_update_slice(wide, bias, (0, core * width))
    base = hidden // model + 6
    small = jnp.concatenate([small[:base], bias_rows, small[base + 2 :]], axis=0)

    both = ("rows", "seq")
    small = lax.psum(small, both)
    zero = jnp.zeros((model, model), F32)
    wide_grads = [lax.dynamic_update_slice(zero, grads[k].astype(F32), (0, core * width)) for k in (1, 2, 3)]
    rows_wo = grads[0].reshape(2, width, width).transpose(1, 0, 2).reshape(width, model).astype(F32)
    wide_grads.append(lax.dynamic_update_slice(zero, rows_wo, (core * width, 0)))
    grad_wq, grad_wk, grad_wv, grad_wo = lax.psum(tuple(wide_grads), both)
    pieces = []
    units = hidden // 8
    for part in range(8):
        (piece,) = local_call(hidden_kernel, (shaped((units, 2 * model), BF16),), "hidden")(
            jnp.full((1,), part, jnp.int32), normed_low, feed, up_weight, line(up_bias), down_weight
        )
        pieces.append(piece.astype(F32))
    hidden_grads = lax.psum_scatter(jnp.concatenate(pieces, axis=0), both, scatter_dimension=0, tiled=True)

    return outputs(layer_output, input_grad, grad_wq, grad_wk, grad_wv, grad_wo, hidden_grads, small)


def solution(mesh):
    split = P("rows", "seq", None)
    in_specs = (split, split, P("rows", None), P("rows", None, None)) + (P(),) * 15
    out_specs = (split, split) + (P(),) * 9 + (P(None, ("rows", "seq")), P(), P(("rows", "seq"), None), P(), P(), P())
    return jax.shard_map(
        functools.partial(on_device, mesh.shape["rows"]), mesh=mesh, in_specs=in_specs, out_specs=out_specs, check_vma=False
    )
```

```python
import functools

import jax
import jax.numpy as jnp
from jax import lax
from jax.experimental import pallas as pl
from jax.experimental.pallas import tpu as pltpu
from jax.sharding import PartitionSpec as P

HEADS = 12
EPSILON = 1e-12
MASKED_SCORE = -1000000000.0
F32 = jnp.float32
BF16 = jnp.bfloat16
MESH = pl.DeviceIdType.MESH
VMEM_LIMIT = 56 * 2**20
ORDERS = ("xyz", "zxy", "xyz", "yxz")
PLAN = {
    "G0": ("Sr00",),
    "G23": ("Sr30",),
    "G1": ("Sr20", "Sr10"),
    "dx": ("Er00", "Ss0"),
    "a1": ("Es0", "Ss1", "Sr01"),
    "a2": ("Ed", "Er20", "Er30", "Sr31"),
    "a4": ("Es1", "Ss2", "Sr21"),
    "a5": ("Er01", "Sr02", "Ef"),
    "a6": ("Es2", "Si", "Ss3", "Er10", "Sr11", "Er31"),
    "a7": ("Er21", "EH", "Er11", "Sr22", "Er02"),
    "a8": ("Es3",),
    "a9": ("Sr32",),
    "a10": ("Er22", "Sr12"),
    "a11": ("Ei", "Sg22"),
    "f0": ("Er12", "Sg12", "Er32"),
    "f1": ("Sg32",),
    "f2": ("Eg12", "Sg11", "Eg22", "Sg21"),
    "f3": ("Sg02",),
    "f4": ("Eg11", "Eg32", "Sg31"),
    "f5": ("Sg10",),
    "f6": ("Eg02", "Sg01"),
    "f7": ("Eg21", "Sg20", "Eg31", "Eh"),
    "end": ("Sg30", "Eg01", "Sg00", "So", "Eg20", "St2", "Eg30", "St3", "Et2", "Eg10", "St1", "Et3", "Et1", "Eg00", "St0", "Et0", "Eo"),
}


def dot(left, right):
    return lax.dot_general(left, right, (((1,), (0,)), ((), ())), preferred_element_type=F32)


def dot_nt(left, right):
    return lax.dot_general(left, right, (((1,), (1,)), ((), ())), preferred_element_type=F32)


def dot_tn(left, right):
    return lax.dot_general(left, right, (((0,), (0,)), ((), ())), preferred_element_type=F32)


def norm_parts(hidden):
    centred = hidden - jnp.mean(hidden, axis=-1, keepdims=True)
    variance = jnp.mean(centred * centred, axis=-1, keepdims=True)
    scale = lax.rsqrt(variance + EPSILON)
    return centred * scale, scale


def norm_back(grad, normed, scale, gain):
    scaled = grad * gain
    along = jnp.mean(scaled * normed, axis=-1, keepdims=True)
    return (scaled - jnp.mean(scaled, axis=-1, keepdims=True) - normed * along) * scale


GELU_A = 0.7978845608028654
GELU_B = 0.044715


def gelu_parts(value):
    square = value * value
    bent = jnp.tanh(GELU_A * value * (1.0 + GELU_B * square))
    half = 0.5 * (1.0 + bent)
    slope = half + 0.5 * value * (1.0 - bent * bent) * (GELU_A * (1.0 + 3.0 * GELU_B * square))
    return value * half, slope


def gelu_only(value):
    bent = jnp.tanh(GELU_A * value * (1.0 + GELU_B * value * value))
    return 0.5 * value * (1.0 + bent)


def lane_is(shape, low, high):
    lane = lax.broadcasted_iota(jnp.int32, shape, len(shape) - 1)
    return (lane >= low) & (lane < high)


def project_kernel(core, half, peer, pos, seg, slots, wq, bq, wk, wv, bv, keys, values, queries, context, probs, picked):
    width = keys.shape[1]
    mine = pl.ds(pl.multiple_of(core[0] * width, 128), width)
    count = slots.shape[0]
    tokens_half = half.shape[0]
    chosen = jnp.where(slots[...] == pos[...], 1.0, 0.0).astype(BF16)
    rows = dot(chosen[:, :tokens_half], half[...]) + dot(chosen[:, tokens_half:], peer[...])
    rows = rows.astype(BF16)
    picked[...] = rows
    queries[...] = (dot(rows, wq[:, mine]) + bq[:, mine]).astype(BF16)
    for place, part in ((0, half), (tokens_half, peer)):
        for start in range(0, tokens_half, 256):
            block = part[start : start + 256, :]
            there = slice(place + start, place + start + 256)
            keys[there, :] = dot(block, wk[:, mine]).astype(BF16)
            values[there, :] = (dot(block, wv[:, mine]) + bv[:, mine]).astype(BF16)
    sequence = lax.broadcasted_iota(jnp.int32, (count, 1), 0) // (count // 2)
    same = seg[...] == sequence
    for pair in range(width // 128):
        lanes = slice(pair * 128, pair * 128 + 128)
        pair_queries = queries[:, lanes].astype(F32) * 0.125
        pair_keys, pair_values = keys[:, lanes], values[:, lanes]
        outs = []
        for side in range(2):
            keep = lane_is((count, 128), side * 64, side * 64 + 64)
            head_queries = jnp.where(keep, pair_queries, 0.0).astype(BF16)
            scores = jnp.where(same, dot_nt(head_queries, pair_keys), MASKED_SCORE)
            weights = jnp.exp(scores - jnp.max(scores, axis=-1, keepdims=True))
            share = weights / jnp.sum(weights, axis=-1, keepdims=True)
            probs[pair * 2 + side] = share
            outs.append(dot(share.astype(BF16), pair_values))
        first = lane_is((count, 128), 0, 64)
        context[:, lanes] = jnp.where(first, outs[0], outs[1]).astype(BF16)


def masked_kernel(core, ctx_own, ctx_peer, picked, cot_half, cot_peer, pos, slots, wo, bo, g1, s1, wup, bup, wdown, bdown, g2, s2, normed_low, feed, branch_low, grad_h1, small):
    count, width = ctx_own.shape
    hidden = wup.shape[1]
    model = wup.shape[0]
    tokens_half = cot_half.shape[0]
    mine = pl.multiple_of(core[0] * count, 16)
    is_first = core[0] == 0
    left = jnp.where(is_first, ctx_own[...], ctx_peer[...])
    right = jnp.where(is_first, ctx_peer[...], ctx_own[...])
    branch = dot(left, wo[:width, :]) + dot(right, wo[width:, :]) + bo[...]
    h1 = picked[pl.ds(mine, count), :].astype(F32) + branch
    n1, r1 = norm_parts(h1)
    y1 = n1 * g1[...] + s1[...]
    y1_low = y1.astype(BF16)
    normed_low[...] = y1_low
    total = y1 + bdown[...]
    slopes = []
    step = model
    for start in range(0, hidden, step):
        pre = dot(y1_low, wup[:, start : start + step]) + bup[:, start : start + step]
        act, slope = gelu_parts(pre)
        slopes.append(slope)
        total = total + dot(act.astype(BF16), wdown[start : start + step, :])
    n2, r2 = norm_parts(total)
    chosen = jnp.where(slots[pl.ds(mine, count), :] == pos[...], 1.0, 0.0).astype(BF16)
    grad = dot(chosen[:, :tokens_half], cot_half[...]) + dot(chosen[:, tokens_half:], cot_peer[...])
    gh2 = norm_back(grad, n2, r2, g2[...])
    gf = gh2.astype(BF16)
    feed[...] = gf
    gy1 = gh2
    small[...] = jnp.zeros_like(small)
    for place, start in enumerate(range(0, hidden, step)):
        ga = dot_nt(gf, wdown[start : start + step, :])
        gp = (ga * slopes[place]).astype(BF16)
        small[place : place + 1, :] = jnp.sum(gp.astype(F32), axis=0, keepdims=True)
        gy1 = gy1 + dot_nt(gp, wup[:, start : start + step])
    gh1 = norm_back(gy1, n1, r1, g1[...])
    grad_h1[...] = gh1
    gb = gh1.astype(BF16)
    branch_low[...] = gb
    base = hidden // step
    for place, value in enumerate((gy1 * n1, gy1, grad * n2, grad, gb.astype(F32), gf.astype(F32))):
        small[base + place : base + place + 1, :] = jnp.sum(value, axis=0, keepdims=True)


def back_kernel(core, keys, values, queries, context, probs, picked, gb_own, gb_peer, gh1, half, peer, pos_col, slots_row, wq, wk, wv, wo, grads, igrad_own, igrad_peer, bias, dq_low, dk_low, dv_low):
    width = keys.shape[1]
    count = queries.shape[0]
    own = gb_own.shape[0]
    tokens_half = half.shape[0]
    is_first = core[0] == 0
    mine = pl.ds(pl.multiple_of(core[0] * width, 128), width)
    mine_rows = pl.ds(pl.multiple_of(core[0] * width, 128), width)
    top = jnp.where(is_first, gb_own[...], gb_peer[...])
    low = jnp.where(is_first, gb_peer[...], gb_own[...])
    gb = jnp.concatenate([top, low], axis=0)
    gctx = dot_nt(gb, wo[mine_rows, :]).astype(BF16)
    for pair in range(width // 128):
        lanes = slice(pair * 128, pair * 128 + 128)
        pair_keys, pair_values, pair_queries = keys[:, lanes], values[:, lanes], queries[:, lanes]
        pair_gctx = gctx[:, lanes]
        dqs, dks, dvs = [], [], []
        for side in range(2):
            keep = lane_is((count, 128), side * 64, side * 64 + 64)
            head_gctx = jnp.where(keep, pair_gctx.astype(F32), 0.0).astype(BF16)
            share = probs[pair * 2 + side]
            gp = dot_nt(head_gctx, pair_values)
            spread = jnp.sum(share * gp, axis=-1, keepdims=True)
            gs = (share * (gp - spread)).astype(BF16)
            dqs.append(dot(gs, pair_keys))
            dks.append(dot_tn(gs, pair_queries))
            dvs.append(dot_tn(share.astype(BF16), pair_gctx))
        first = lane_is((count, 128), 0, 64)
        dq_low[:, lanes] = (jnp.where(first, dqs[0], dqs[1]) * 0.125).astype(BF16)
        first = lane_is((2 * tokens_half, 128), 0, 64)
        dk_low[:, lanes] = (jnp.where(first, dks[0], dks[1]) * 0.125).astype(BF16)
        dv_low[:, lanes] = jnp.where(first, dvs[0], dvs[1]).astype(BF16)
    grads[1] = dot_tn(picked[...], dq_low[...]).astype(BF16)
    gwo = dot_tn(context[...], gb).astype(BF16)
    grads[0, :width, :] = gwo[:, :width]
    grads[0, width:, :] = gwo[:, width:]
    for place, part in ((2, dk_low), (3, dv_low)):
        total = dot_tn(half[...], part[:tokens_half, :]) + dot_tn(peer[...], part[tokens_half:, :])
        grads[place] = total.astype(BF16)
    bias[0:1, :] = jnp.sum(dq_low[...].astype(F32), axis=0, keepdims=True)
    bias[1:2, :] = jnp.sum(dv_low[...].astype(F32), axis=0, keepdims=True)
    spread_rows = dot_nt(dq_low[...], wq[:, mine])
    zero = jnp.zeros((own, wq.shape[0]), F32)
    spread_rows = spread_rows + jnp.concatenate(
        [jnp.where(is_first, gh1[...], zero), jnp.where(is_first, zero, gh1[...])], axis=0
    )
    high = spread_rows.astype(BF16)
    rest = (spread_rows - high.astype(F32)).astype(BF16)
    for start in range(0, 2 * tokens_half, 256):
        here = slice(start, start + 256)
        chosen = jnp.where(pos_col[here, :] == slots_row[...], 1.0, 0.0).astype(BF16)
        total = dot(chosen, high) + dot(chosen, rest)
        total = total + dot_nt(dk_low[here, :], wk[:, mine]) + dot_nt(dv_low[here, :], wv[:, mine])
        if start < tokens_half:
            igrad_own[here, :] = total
        else:
            igrad_peer[start - tokens_half : start - tokens_half + 256, :] = total.astype(BF16)


def attend_kernel(core, half, peer, seg, seg_col, keys, values, wq, bq, own, other):
    width = keys.shape[1]
    mine = pl.ds(pl.multiple_of(core[0] * width, 128), width)
    tile = 256
    for part, out in ((half, own), (peer, other)):
        place = 0 if part is half else half.shape[0]

        def body(step, carry, part=part, out=out, place=place):
            here = pl.ds(pl.multiple_of(step * tile, tile), tile)
            queries = (dot(part[here, :], wq[:, mine]) + bq[:, mine]).astype(BF16).astype(F32) * 0.125
            same = seg_col[pl.ds(pl.multiple_of(place + step * tile, tile), tile), :] == seg[...]
            for pair in range(width // 128):
                lanes = slice(pair * 128, pair * 128 + 128)
                outs = []
                for side in range(2):
                    keep = lane_is((tile, 128), side * 64, side * 64 + 64)
                    head_queries = jnp.where(keep, queries[:, lanes], 0.0).astype(BF16)
                    scores = jnp.where(same, dot_nt(head_queries, keys[:, lanes]), MASKED_SCORE)
                    weights = jnp.exp(scores - jnp.max(scores, axis=-1, keepdims=True))
                    total = jnp.sum(weights, axis=-1, keepdims=True)
                    outs.append(dot(weights.astype(BF16), values[:, lanes]) / total)
                first = lane_is((tile, 128), 0, 64)
                out[here, lanes] = jnp.where(first, outs[0], outs[1]).astype(BF16)
            return carry

        lax.fori_loop(0, part.shape[0] // tile, body, 0)


def feed_kernel(core, ctx_own, ctx_peer, half, wo, bo, g1, s1, wup, bup, wdown, bdown, g2, s2, own, other):
    width = ctx_own.shape[1]
    hidden, model = wdown.shape
    is_first = core[0] == 0
    tile = own.shape[0]
    for start, out in ((0, own), (tile, other)):
        here = slice(start, start + tile)
        left = jnp.where(is_first, ctx_own[here, :], ctx_peer[here, :])
        right = jnp.where(is_first, ctx_peer[here, :], ctx_own[here, :])
        branch = dot(left, wo[:width, :]) + dot(right, wo[width:, :]) + bo[...]
        n1, _ = norm_parts(half[here, :].astype(F32) + branch)
        y1 = n1 * g1[...] + s1[...]
        y1_low = y1.astype(BF16)
        total = y1 + bdown[...]
        for place in range(0, hidden, model):
            pre = dot(y1_low, wup[:, place : place + model]) + bup[:, place : place + model]
            total = total + dot(gelu_only(pre).astype(BF16), wdown[place : place + model, :])
        n2, _ = norm_parts(total)
        out[...] = (n2 * g2[...] + s2[...]).astype(BF16)


def hidden_kernel(slot, normed, feed, wup, bup, wdown, out):
    units = out.shape[0]
    model = normed.shape[1]
    mine = pl.ds(pl.multiple_of(slot[0] * units, 128), units)
    pre = dot(normed[...], wup[:, mine]) + bup[:, mine]
    act, slope = gelu_parts(pre)
    ga = dot_nt(feed[...], wdown[mine, :])
    gp = (ga * slope).astype(BF16)
    out[:, :model] = dot_tn(gp, normed[...]).astype(BF16)
    out[:, model:] = dot_tn(act.astype(BF16), feed[...]).astype(BF16)


def place_here():
    row, seq = lax.axis_index("rows"), lax.axis_index("seq")
    return row // 2, row % 2, seq // 2, seq % 2


def device(z, x, y, core):
    return (z * 2 + x, y * 2 + core)


def layer_kernel(
    tokens, cotangent, segments_in, slots_in, up_bias_in, bq_in, bv_in, bo_in, g1_in, s1_in, bdown_in, g2_in, s2_in, wq, wk, wv, wo, wup, wdown,
    layer_out, input_grad, out_o, out_q, out_k, out_v, up_out, down_out, small_out,
    segments, slots, up_bias, bq, bv, bo, g1, s1, bdown, g2, s2, vecs, wq_t, wkv_t, wo_t, keys_t, values_t,
    xs, cs, wq_v, wk_v, wv_v, wo_v, wup_v, wdown_v, keys, values, queries, context, probs, picked, chosen, ctx_both, gb_both,
    slopes, dq_low, dkv_low, grads, hidden_grads, hidden_in, fac_normed, fac_feed, grad_h1, small_in, small_z,
    all_queries, all_context, ctx_in, total, y1_keep, out_send, igrad_send, igrad_in,
    in_o, in_q, in_k, in_v, local_sem, send_sem, recv_sem,
):
    z, x, y, core = place_here()
    row = y
    stretch, model = tokens.shape[1:]
    half = 2 * stretch
    full = 2 * half
    width = wq_v.shape[1]
    masks = slots.shape[2]
    count = 2 * masks
    hidden = wup.shape[1]
    parts = hidden // model
    units = down_out.shape[0]
    others = [(z + k) % 4 for k in (1, 2, 3)]
    at_y, at_x, twin = device(z, x, 1 - y, core), device(z, 1 - x, y, core), device(z, x, y, 1 - core)
    columns = [device(o, x, y, core) for o in others]
    mine = pl.ds(pl.multiple_of(core * width, 128), width)
    my_slots = pl.ds(pl.multiple_of(core * masks, 16), masks)
    twin_slots = pl.ds(pl.multiple_of((1 - core) * masks, 16), masks)
    pending = []

    def local(src, dst, index):
        copy = pltpu.make_async_copy(src, dst, local_sem.at[index])
        copy.start()
        return copy

    def remote(src, dst, index, target):
        return pltpu.make_async_remote_copy(
            src_ref=src, dst_ref=dst, send_sem=send_sem.at[index], recv_sem=recv_sem.at[index],
            device_id=target, device_id_type=MESH,
        )

    def push(src, dst, index, target):
        copy = remote(src, dst, index, target)
        copy.start()
        pending.append(copy)
        return copy

    def vector(index):
        return vecs[index : index + 1, :]

    def half_vector(index):
        return vecs[index : index + 1, mine]

    small_pairs = (
        (segments_in, segments), (slots_in, slots), (up_bias_in, up_bias), (bq_in, bq), (bv_in, bv), (bo_in, bo), (g1_in, g1),
        (s1_in, s1), (bdown_in, bdown), (g2_in, g2), (s2_in, s2),
    )
    own_tokens = local(tokens.at[row], xs.at[pl.ds(0, stretch)], 0)
    get_wk = local(wk.at[:, mine], wk_v, 1)
    get_wv = local(wv.at[:, mine], wv_v, 2)
    get_small = [local(src, dst, 8 + k) for k, (src, dst) in enumerate(small_pairs)]
    get_wq = local(wq.at[:, mine], wq_v, 3)
    own_cot = local(cotangent.at[row], cs.at[pl.ds(0, stretch)], 4)
    get_wo = local(wo, wo_v, 5)
    get_up = local(wup, wup_v, 6)
    get_down = local(wdown, wdown_v, 7)

    near = [(1 - x, y), (x, 1 - y), (1 - x, 1 - y)]
    greeted = [twin] + columns + [device(z, nx, ny, c) for nx, ny in near for c in range(2)]
    barrier = pltpu.get_barrier_semaphore()
    for target in greeted:
        pl.semaphore_signal(barrier, inc=1, device_id=target, device_id_type=MESH)
    pl.semaphore_wait(barrier, len(greeted))

    piece = stretch // 2
    tok_y = [
        push(tokens.at[1 - row, pl.ds(k * piece, piece)], xs.at[pl.ds(stretch + k * piece, piece)], k, at_y) for k in range(2)
    ]
    tok_c = push(tokens.at[row], xs.at[pl.ds(half, stretch)], 2, twin)
    cot_c = push(cotangent.at[row], cs.at[pl.ds(half, stretch)], 4, twin)

    for copy in get_small:
        copy.wait()
    for part in range(parts):
        vecs[part : part + 1, :] = up_bias[part * model : (part + 1) * model].reshape(1, model)
    for place, value in enumerate((bq, bv, bo, g1, s1, bdown, g2, s2)):
        vecs[parts + place : parts + place + 1, :] = value[...].reshape(1, model)

    def key_values(start):
        here = pl.ds(start, stretch)
        block = xs[here, :]
        block_keys = dot(block, wk_v[...]).astype(BF16)
        block_values = (dot(block, wv_v[...]) + half_vector(5)).astype(BF16)
        keys[here, :] = block_keys
        values[here, :] = block_values
        keys_t[:, here] = block_keys.T
        values_t[:, here] = block_values.T

    blocks = [2 * y + core, 2 * (1 - y) + core, 2 * y + 1 - core, 2 * (1 - y) + 1 - core]
    lane = lax.broadcasted_iota(jnp.int32, (1, stretch), 1)
    pos_row = jnp.concatenate([lane + block * stretch for block in blocks], axis=1)
    seg_here = segments[pl.ds(row, 1), :]
    split = jnp.sum((1 - seg_here).astype(F32), axis=1, keepdims=True)
    pos_row = pos_row.astype(F32)
    seg_row = jnp.where(pos_row >= split, 1.0, 0.0)
    slot_rows = slots[row].astype(F32)
    diagonal = lax.broadcasted_iota(jnp.int32, (masks, masks), 0) == lax.broadcasted_iota(jnp.int32, (masks, masks), 1)
    for sequence in range(2):
        column = jnp.sum(jnp.where(diagonal, slot_rows[sequence : sequence + 1, :], 0.0), axis=1, keepdims=True)
        chosen[sequence * masks : (sequence + 1) * masks, :] = jnp.where(column == pos_row, 1.0, 0.0).astype(BF16)

    own_tokens.wait()
    get_wk.wait()
    get_wv.wait()
    key_values(0)
    tok_c.wait_recv()
    key_values(half)
    get_wq.wait()
    wkv_t[:width, :] = wk_v[...].T
    wkv_t[width:, :] = wv_v[...].T
    wq_t[...] = wq_v[...].T
    forward = []
    for k in range(2):
        tok_y[k].wait_recv()
        src = xs.at[pl.ds(stretch + k * piece, piece)]
        forward.append(push(src, xs.at[pl.ds(half + stretch + k * piece, piece)], 5 + k, twin))
    cot_y = push(cotangent.at[1 - row], cs.at[pl.ds(stretch, stretch)], 3, at_y)
    key_values(stretch)
    for copy in forward:
        copy.wait_recv()
    key_values(half + stretch)

    rows = dot(chosen[...], xs[...]).astype(BF16)
    picked[...] = rows
    queries[...] = (dot(rows, wq_v[...]) + half_vector(4)).astype(BF16)
    sequence = lax.broadcasted_iota(jnp.int32, (count, 1), 0) // masks
    same = seg_row == sequence.astype(F32)
    pairs = width // 128
    for pair in range(pairs):
        lanes = slice(pair * 128, pair * 128 + 128)
        pair_queries = queries[:, lanes].astype(F32) * 0.125
        pair_keys, pair_values = keys_t[lanes, :], values[:, lanes]
        outs = []
        for side in range(2):
            keep = lane_is((count, 128), side * 64, side * 64 + 64)
            head_queries = jnp.where(keep, pair_queries, 0.0).astype(BF16)
            scores = jnp.where(same, dot(head_queries, pair_keys), MASKED_SCORE)
            weights = jnp.exp(scores - jnp.max(scores, axis=-1, keepdims=True))
            share = weights / jnp.sum(weights, axis=-1, keepdims=True)
            probs[pair * 2 + side] = share
            outs.append(dot(share.astype(BF16), pair_values))
        first = lane_is((count, 128), 0, 64)
        context[:, lanes] = jnp.where(first, outs[0], outs[1]).astype(BF16)
    ctx_both[core] = context[my_slots, :]
    ctx_c = push(context.at[twin_slots], ctx_both.at[core], 7, twin)

    own_cot.wait()
    cot_y.wait_recv()
    cot_f = push(cs.at[pl.ds(stretch, stretch)], cs.at[pl.ds(half + stretch, stretch)], 8, twin)
    for start in range(0, full, stretch):
        value = (dot(xs[start : start + stretch, :], wq_v[...]) + half_vector(4)).astype(BF16)
        all_queries[start : start + stretch, :] = (value.astype(F32) * 0.125).astype(BF16)
    get_wo.wait()
    wo_t[...] = wo_v[mine, :].T
    ctx_c.wait_recv()

    branch = dot(ctx_both[0], wo_v[:width, :]) + dot(ctx_both[1], wo_v[width:, :]) + vector(6)
    n1, r1 = norm_parts(picked[my_slots, :].astype(F32) + branch)
    y1 = n1 * vector(7) + vector(8)
    y1_low = y1.astype(BF16)
    fac_normed[core, z] = y1_low
    spot = fac_normed.at[core, z]
    norm_z = [push(spot, spot, 9 + k, columns[k]) for k in range(3)]
    get_up.wait()
    get_down.wait()
    sum2 = y1 + vector(9)
    for part in range(parts):
        there = slice(part * model, (part + 1) * model)
        act, slope = gelu_parts(dot(y1_low, wup_v[:, there]) + vector(part))
        slopes[part] = slope
        sum2 = sum2 + dot(act.astype(BF16), wdown_v[there, :])
    n2, r2 = norm_parts(sum2)
    cot_c.wait_recv()
    cot_f.wait_recv()
    grad = dot(chosen[my_slots, :], cs[...])
    gh2 = norm_back(grad, n2, r2, vector(10))
    gf = gh2.astype(BF16)
    fac_feed[core, z] = gf
    spot = fac_feed.at[core, z]
    feed_z = [push(spot, spot, 12 + k, columns[k]) for k in range(3)]
    gf_t = gf.T
    gy1_t = jnp.zeros((model, masks), F32)
    small_in[0] = jnp.zeros(small_in.shape[1:], F32)
    for part in range(parts):
        there = slice(part * model, (part + 1) * model)
        gp = (dot(wdown_v[there, :], gf_t).T * slopes[part]).astype(BF16)
        small_in[0, part : part + 1, :] = jnp.sum(gp.astype(F32), axis=0, keepdims=True)
        gy1_t = gy1_t + dot(wup_v[:, there], gp.T)
    gy1 = gh2 + gy1_t.T
    gh1 = norm_back(gy1, n1, r1, vector(7))
    grad_h1[...] = gh1
    gb = gh1.astype(BF16)
    gb_both[core] = gb
    gb_c = push(gb_both.at[core], gb_both.at[core], 15, twin)
    for place, value in enumerate((gy1 * n1, gy1, grad * n2, grad, gb.astype(F32), gf.astype(F32))):
        small_in[0, parts + place : parts + place + 1, :] = jnp.sum(value, axis=0, keepdims=True)
    gb_c.wait_recv()

    spots = {"x": x, "y": y, "z": z}
    sizes = {"x": 2, "y": 2, "z": 4}
    dims = {"x": [at_x], "y": [at_y], "z": columns}
    orders = ORDERS
    ins = [in_o, in_q, in_k, in_v]
    outs = [out_o, out_q, out_k, out_v]

    def regions(job):
        base, size, found = 0, model, [(0, model)]
        for dim in orders[job]:
            size = size // sizes[dim]
            base = base + spots[dim] * size
            found.append((base, size))
        return found

    def in_place(job, stage):
        at, size = 0, model
        for dim in orders[job][:stage]:
            size = size // sizes[dim]
            at += size * (sizes[dim] - 1)
        return at, size // sizes[orders[job][stage]]

    def out_at(job, base, size):
        if job == 0:
            side = base // width
            offset = base - side * width
            at = pl.ds(pl.multiple_of(core * width + offset, 16), size)
            return outs[0].at[at, pl.ds(pl.multiple_of(side * width, 128), width)]
        return outs[job].at[pl.ds(pl.multiple_of(base, 16), size), mine]

    def reduce_copies(job, stage):
        dim = orders[job][stage]
        at, size = in_place(job, stage)
        base, _ = regions(job)[stage]
        copies = []
        for k, target in enumerate(dims[dim]):
            other = (spots[dim] + k + 1) % sizes[dim]
            src = grads.at[job, pl.ds(pl.multiple_of(base + other * size, 16), size)]
            dst = ins[job].at[pl.ds(at + k * size, size)]
            copies.append(remote(src, dst, 40 + job * 20 + stage * 3 + k, target))
        return copies

    def reduce_start(job, stage):
        for copy in reduce_copies(job, stage):
            copy.start()

    def reduce_end(job, stage):
        for copy in reduce_copies(job, stage):
            copy.wait()
        dim = orders[job][stage]
        at, size = in_place(job, stage)
        base, _ = regions(job)[stage + 1]
        here = pl.ds(pl.multiple_of(base, 16), size)
        value = grads[job, here].astype(F32)
        for k in range(len(dims[dim])):
            value = value + ins[job][pl.ds(at + k * size, size)].astype(F32)
        value = value.astype(BF16)
        if stage < 2:
            grads[job, here] = value
        else:
            out_at(job, base, size)[...] = value

    def gather_copies(job, stage):
        base, size = regions(job)[stage + 1]
        spot = out_at(job, base, size)
        return [
            remote(spot, spot, 40 + job * 20 + 9 + stage * 3 + k, target)
            for k, target in enumerate(dims[orders[job][stage]])
        ]

    def twin_copy(job):
        spot = outs[0].at[mine, :] if job == 0 else outs[job].at[:, mine]
        return remote(spot, spot, 40 + job * 20 + 18, twin)

    def gather_start(job, stage):
        for copy in gather_copies(job, stage):
            copy.start()

    def gather_end(job, stage):
        for copy in gather_copies(job, stage):
            copy.wait()

    def small_copies(stage):
        if stage < 3:
            target = (twin, at_y, at_x)[stage]
            return [remote(small_in.at[2 * stage], small_in.at[2 * stage + 1], 16 + stage, target)]
        return [remote(small_in.at[6], small_z.at[z], 19 + k, target) for k, target in enumerate(columns)]

    def small_start(stage):
        for copy in small_copies(stage):
            copy.start()

    def small_end(stage):
        for copy in small_copies(stage):
            copy.wait()
        if stage < 3:
            small_in[2 * stage + 2] = small_in[2 * stage] + small_in[2 * stage + 1]
            if stage == 2:
                small_z[z] = small_in[6]
        else:
            small_out[...] = (small_z[0] + small_z[1]) + (small_z[2] + small_z[3])

    source = x * 2 + y

    def factor_copies():
        return [remote(ref.at[core], ref.at[core], 22 + k, twin) for k, ref in enumerate((fac_normed, fac_feed))]

    def factors_on():
        for copy in norm_z + feed_z:
            copy.wait_recv()
        for copy in factor_copies():
            copy.start()

    def is_me(cy, cc):
        return (core == x) & (cy == y) & (cc == core)

    def hidden_copy(cy, cc):
        part = hidden_grads.at[pl.ds((cy * 2 + cc) * units, units)]
        return pltpu.make_async_remote_copy(
            src_ref=part, dst_ref=hidden_in.at[source], send_sem=send_sem.at[24 + cy * 2 + cc], recv_sem=recv_sem.at[24 + source],
            device_id=device(z, core, cy, cc), device_id_type=MESH,
        )

    def hidden_make():
        for copy in factor_copies():
            copy.wait()
        slot = z * 2 + core
        size = hidden_grads.shape[0]
        normed = fac_normed[...].reshape(8 * masks, model)
        feed = fac_feed[...].reshape(8 * masks, model)
        at = pl.ds(pl.multiple_of(slot * size, 128), size)
        act, slope = gelu_parts(dot(normed, wup_v[:, at]) + vecs[pl.ds(z, 1), mine])
        gp = (dot_nt(feed, wdown_v[at, :]) * slope).astype(BF16)
        hidden_grads[:, :model] = dot_tn(gp, normed).astype(BF16)
        hidden_grads[:, model:] = dot_tn(act.astype(BF16), feed).astype(BF16)
        for cy in range(2):
            for cc in range(2):
                @pl.when(jnp.logical_not(is_me(cy, cc)))
                def _(cy=cy, cc=cc):
                    hidden_copy(cy, cc).start()

                @pl.when(is_me(cy, cc))
                def _(cy=cy, cc=cc):
                    hidden_in[source] = hidden_grads[pl.ds((cy * 2 + cc) * units, units)]

    def hidden_end():
        for cy in range(2):
            for cc in range(2):
                @pl.when(jnp.logical_not(is_me(cy, cc)))
                def _(cy=cy, cc=cc):
                    hidden_copy(cy, cc).wait_send()
        for cx in range(2):
            for cy in range(2):
                @pl.when(jnp.logical_not((cx == x) & (cy == y) & (core == x)))
                def _(cx=cx, cy=cy):
                    slot = hidden_in.at[cx * 2 + cy]
                    pltpu.make_async_remote_copy(
                        src_ref=slot, dst_ref=slot, send_sem=send_sem.at[24], recv_sem=recv_sem.at[24 + cx * 2 + cy],
                        device_id=twin, device_id_type=MESH,
                    ).wait_recv()
        value = hidden_in[0].astype(F32)
        for k in range(1, 4):
            value = value + hidden_in[k].astype(F32)
        up_out[...] = value[:, :model]
        down_out[...] = value[:, model:]

    def igrad_copy():
        return remote(igrad_send, igrad_in, 29, at_y)

    def igrad_step():
        remote(cs.at[pl.ds(0, half)], cs.at[pl.ds(half, half)], 28, twin).wait_recv()
        input_grad[row] = input_grad[row] + cs[half : half + stretch, :].astype(F32)
        igrad_send[...] = (input_grad[1 - row] + cs[half + stretch :, :].astype(F32)).astype(BF16)

    def igrad_end():
        igrad_copy().wait()
        input_grad[1 - row] = igrad_in[...].astype(F32)

    def out_copy():
        return remote(out_send, layer_out.at[row], 31, at_y)

    def act(name):
        start, kind, rest = name[0] == "S", name[1], [int(c) for c in name[2:]]
        if kind == "r":
            (reduce_start if start else reduce_end)(*rest)
        elif kind == "g":
            (gather_start if start else gather_end)(*rest)
        elif kind == "t":
            twin_copy(*rest).start() if start else twin_copy(*rest).wait()
        elif kind == "s":
            (small_start if start else small_end)(*rest)
        elif kind == "d":
            igrad_step()
        elif kind == "i":
            igrad_copy().start() if start else igrad_end()
        elif kind == "o":
            out_copy().start() if start else out_copy().wait()
        elif kind == "f":
            factors_on()
        elif kind == "H":
            hidden_make()
        elif kind == "h":
            hidden_end()

    def act_on(name):
        for each in PLAN.get(name, ()):
            act(each)

    gb = gb_both[...].reshape(count, model)
    gctx = dot(gb, wo_t[...]).astype(BF16)
    value = dot_tn(context[...], gb).astype(BF16)
    grads[0, :width, :] = value[:, :width]
    grads[0, width:, :] = value[:, width:]
    act_on("G0")
    for pair in range(pairs):
        lanes = slice(pair * 128, pair * 128 + 128)
        pair_keys, pair_values, pair_queries = keys[:, lanes], values_t[lanes, :], queries[:, lanes]
        pair_gctx = gctx[:, lanes]
        dqs, dks, dvs = [], [], []
        for side in range(2):
            keep = lane_is((count, 128), side * 64, side * 64 + 64)
            head_gctx = jnp.where(keep, pair_gctx.astype(F32), 0.0).astype(BF16)
            share = probs[pair * 2 + side]
            gp = dot(head_gctx, pair_values)
            spread = jnp.sum(share * gp, axis=-1, keepdims=True)
            gs = (share * (gp - spread)).astype(BF16)
            dqs.append(dot(gs, pair_keys))
            dks.append(dot_tn(gs, pair_queries))
            dvs.append(dot_tn(share.astype(BF16), pair_gctx))
        first = lane_is((count, 128), 0, 64)
        dq_low[:, lanes] = (jnp.where(first, dqs[0], dqs[1]) * 0.125).astype(BF16)
        first = lane_is((full, 128), 0, 64)
        dkv_low[:, lanes] = (jnp.where(first, dks[0], dks[1]) * 0.125).astype(BF16)
        dkv_low[:, width + pair * 128 : width + pair * 128 + 128] = jnp.where(first, dvs[0], dvs[1]).astype(BF16)
    act_on("heads")
    for start in range(0, model, 256):
        value = dot_tn(xs[:, start : start + 256], dkv_low[...]).astype(BF16)
        grads[2, start : start + 256, :] = value[:, :width]
        grads[3, start : start + 256, :] = value[:, width:]
    act_on("G23")
    grads[1] = dot_tn(picked[...], dq_low[...]).astype(BF16)
    act_on("G1")
    small_in[0, parts + 6 : parts + 7, mine] = jnp.sum(dq_low[...].astype(F32), axis=0, keepdims=True)
    small_in[0, parts + 7 : parts + 8, mine] = jnp.sum(dkv_low[:, width:].astype(F32), axis=0, keepdims=True)

    spread_rows = dot(dq_low[...], wq_t[...])
    zero = jnp.zeros((masks, model), F32)
    is_first = core == 0
    gh1 = grad_h1[...]
    spread_rows = spread_rows + jnp.concatenate([jnp.where(is_first, gh1, zero), jnp.where(is_first, zero, gh1)], axis=0)
    high = spread_rows.astype(BF16)
    rest = (spread_rows - high.astype(F32)).astype(BF16)
    cot_f.wait_send()
    pending[:] = [copy for copy in pending if copy is not cot_f]
    for start in (half, half + stretch, 0, stretch):
        here = slice(start, start + stretch)
        value = dot_tn(chosen[:, here], high) + dot_tn(chosen[:, here], rest)
        value = value + dot(dkv_low[here, :], wkv_t[...])
        if start < half:
            input_grad[row if start == 0 else 1 - row] = value
        else:
            cs[start - half : start - half + stretch, :] = value.astype(BF16)
            if start > half:
                push(cs.at[pl.ds(0, half)], cs.at[pl.ds(half, half)], 28, twin)

    act_on("dx")

    def hooks(step, prefix, count):
        for at in range(count):
            if prefix + str(at) in PLAN:
                @pl.when(step == at)
                def _(at=at):
                    act_on(prefix + str(at))

    def ctx_copy():
        return remote(all_context.at[pl.ds(half, half)], ctx_in, 30, twin)

    def attend_step(step, carry):
        tile, pair = (step // pairs + 2) % 4, step % pairs
        here = pl.ds(pl.multiple_of(tile * stretch, stretch), stretch)
        lanes = pl.ds(pl.multiple_of(pair * 128, 128), 128)
        block = 2 * (y + (tile % 2) * (1 - 2 * y)) + core + (tile // 2) * (1 - 2 * core)
        place = lax.broadcasted_iota(jnp.int32, (stretch, 1), 0) + block * stretch
        seg_col = jnp.where(place.astype(F32) >= split, 1.0, 0.0)
        same_here = seg_col == seg_row
        pair_queries = all_queries[here, lanes].astype(F32)
        pair_keys, pair_values = keys_t[lanes, :], values[:, lanes]
        found = []
        for side in range(2):
            keep = lane_is((stretch, 128), side * 64, side * 64 + 64)
            head_queries = jnp.where(keep, pair_queries, 0.0).astype(BF16)
            scores = jnp.where(same_here, dot(head_queries, pair_keys), MASKED_SCORE)
            weights = jnp.exp(scores - jnp.max(scores, axis=-1, keepdims=True))
            found.append(dot(weights.astype(BF16), pair_values) / jnp.sum(weights, axis=-1, keepdims=True))
        first = lane_is((stretch, 128), 0, 64)
        all_context[here, lanes] = jnp.where(first, found[0], found[1]).astype(BF16)

        @pl.when(step == 2 * pairs - 1)
        def _():
            ctx_copy().start()

        hooks(step, "a", 4 * pairs)
        return carry

    lax.fori_loop(0, 4 * pairs, attend_step, 0)
    ctx_copy().wait()

    def feed_step(step, carry):
        tile, part = 1 - step // parts, step % parts
        here = pl.ds(pl.multiple_of(tile * stretch, stretch), stretch)

        @pl.when(part == 0)
        def _():
            left = jnp.where(is_first, all_context[here, :], ctx_in[here, :])
            right = jnp.where(is_first, ctx_in[here, :], all_context[here, :])
            here_branch = dot(left, wo_v[:width, :]) + dot(right, wo_v[width:, :]) + vector(6)
            normed, _ = norm_parts(xs[here, :].astype(F32) + here_branch)
            value = normed * vector(7) + vector(8)
            y1_keep[...] = value.astype(BF16)
            total[...] = value + vector(9)

        there = pl.ds(pl.multiple_of(part * model, model), model)
        pre = dot(y1_keep[...], wup_v[:, there]) + vecs[pl.ds(part, 1), :]
        total[...] += dot(gelu_only(pre).astype(BF16), wdown_v[there, :])

        @pl.when(part == parts - 1)
        def _():
            normed, _ = norm_parts(total[...])
            value = (normed * vector(10) + vector(11)).astype(BF16)

            @pl.when(tile == 1)
            def _():
                out_send[...] = value

            @pl.when(tile == 0)
            def _():
                layer_out[row] = value

        hooks(step, "f", 2 * parts)
        return carry

    lax.fori_loop(0, 2 * parts, feed_step, 0)
    act_on("end")
    for copy in pending:
        copy.wait_send()


def vmem(count):
    return [pl.BlockSpec(memory_space=pltpu.VMEM)] * count


def local_call(body, outs, name, scratch=()):
    def call(core, *operands):
        return pl.pallas_call(
            body,
            out_shape=outs,
            in_specs=[pl.BlockSpec(memory_space=pltpu.SMEM)] + vmem(len(operands)),
            out_specs=vmem(len(outs)),
            scratch_shapes=list(scratch),
            compiler_params=pltpu.CompilerParams(vmem_limit_bytes=VMEM_LIMIT),
            name=name,
        )(core, *operands)

    return call


def outputs(layer_output, input_grad, grad_wq, grad_wk, grad_wv, grad_wo, up_part, down_part, small):
    model = grad_wq.shape[0]
    base = small.shape[0] - 12
    vector = lambda index: small[index]
    return (
        layer_output,
        input_grad,
        grad_wq.astype(F32),
        vector(base + 6),
        grad_wk.astype(F32),
        grad_wv.astype(F32),
        vector(base + 7),
        grad_wo.astype(F32),
        vector(base + 4),
        vector(base),
        vector(base + 1),
        up_part.T,
        small[:base].reshape(-1),
        down_part,
        vector(base + 5),
        vector(base + 2),
        vector(base + 3),
    )


def layer_call(tokens, cotangent, segment_ids, mask_positions, vectors, weights):
    _, stretch, model = tokens.shape
    hidden = weights[4].shape[1]
    masks = mask_positions.shape[2]
    count, half, full, width = 2 * masks, 2 * stretch, 4 * stretch, model // 2
    units = hidden // 32
    shaped = jax.ShapeDtypeStruct
    low = lambda *shape: pltpu.VMEM(shape, BF16)
    wide = lambda *shape: pltpu.VMEM(shape, F32)
    scratch = [pltpu.VMEM(small.shape, small.dtype) for small in (segment_ids, mask_positions) + vectors]
    scratch += [
        wide(hidden // model + 8, model), low(width, model), low(model, model), low(model, width), low(width, full), low(width, full),
        low(full, model), low(full, model), low(model, width), low(model, width), low(model, width), low(model, model),
        low(model, hidden), low(hidden, model), low(full, width), low(full, width), low(count, width), low(count, width),
        wide(HEADS // 2, count, full), low(count, model), low(count, full), low(2, masks, width), low(2, masks, model),
        wide(hidden // model, masks, model), low(count, width), low(full, model), low(4, model, width),
        low(4 * units, 2 * model), low(4, units, 2 * model), low(2, 4, masks, model), low(2, 4, masks, model),
        wide(masks, model), wide(7, 16, model), wide(4, 16, model),
        low(full, width), low(full, width), low(half, width), wide(stretch, model), low(stretch, model), low(stretch, model),
        low(stretch, model), low(stretch, model),
    ]
    for order in ORDERS:
        size, at = model, 0
        for dim in order:
            ways = 4 if dim == "z" else 2
            size //= ways
            at += size * (ways - 1)
        scratch.append(low(at, width))
    scratch += [pltpu.SemaphoreType.DMA((8 + 2 + len(vectors),)), pltpu.SemaphoreType.DMA((120,)), pltpu.SemaphoreType.DMA((120,))]
    anywhere = [pl.BlockSpec(memory_space=pltpu.HBM)]
    return pl.pallas_call(
        layer_kernel,
        out_shape=(
            shaped((2, stretch, model), BF16),
            shaped((2, stretch, model), F32),
            shaped((model, model), BF16),
            shaped((model, model), BF16),
            shaped((model, model), BF16),
            shaped((model, model), BF16),
            shaped((units, model), F32),
            shaped((units, model), F32),
            shaped((16, model), F32),
        ),
        in_specs=anywhere * (4 + len(vectors) + len(weights)),
        out_specs=vmem(9),
        scratch_shapes=scratch,
        compiler_params=pltpu.CompilerParams(collective_id=0, has_side_effects=True, vmem_limit_bytes=62 * 2**20),
        name="layer",
    )(tokens, cotangent, segment_ids, mask_positions, *vectors, *weights)


def on_device(
    rows_total,
    tokens,
    cotangent,
    segment_ids,
    mask_positions,
    query_weight,
    query_bias,
    key_weight,
    value_weight,
    value_bias,
    output_weight,
    output_bias,
    first_gain,
    first_shift,
    up_weight,
    up_bias,
    down_weight,
    down_bias,
    second_gain,
    second_shift,
):
    if rows_total == 8:
        vectors = (up_bias, query_bias, value_bias, output_bias, first_gain, first_shift, down_bias, second_gain, second_shift)
        weights = (query_weight, key_weight, value_weight, output_weight, up_weight, down_weight)
        layer_output, input_grad, go, gq, gk, gv, up_part, down_part, small = layer_call(
            tokens, cotangent, segment_ids, mask_positions, vectors, weights
        )
        return outputs(layer_output, input_grad, gq, gk, gv, go, up_part, down_part, small)
    _, stretch, model = tokens.shape
    hidden = up_weight.shape[1]
    width = model // 2
    heads = HEADS // 2
    masks = mask_positions.shape[2]
    seq = lax.axis_index("seq")
    row = seq // 2
    core = seq % 2
    across = [(i, (i + 2) % 4) for i in range(4)]
    beside = [(i, i + 1 - 2 * (i % 2)) for i in range(4)]

    def swap(value):
        return lax.ppermute(value, "seq", across)

    def trade(value):
        return lax.ppermute(value, "seq", beside)

    def take(array, index):
        return lax.dynamic_index_in_dim(array, index, 0, keepdims=False)

    half = jnp.concatenate([take(tokens, row), swap(take(tokens, 1 - row))], axis=0)
    peer = trade(half)
    cot_half = jnp.concatenate([take(cotangent, row), swap(take(cotangent, 1 - row))], axis=0)
    cot_peer = trade(cot_half)
    blocks = jnp.stack([2 * row + core, 2 * (1 - row) + core, 2 * row + 1 - core, 2 * (1 - row) + 1 - core])
    positions = (blocks[:, None] * stretch + jnp.arange(stretch, dtype=jnp.int32)[None, :]).reshape(-1)
    segments = jnp.take(take(segment_ids, row).reshape(4, stretch), blocks, axis=0).reshape(-1)
    slots = take(mask_positions, row).reshape(-1)
    pos, seg, slot_col = positions[None, :], segments[None, :], slots[:, None]
    pos_col, seg_col, slot_row = positions[:, None], segments[:, None], slots[None, :]
    core_scalar = core.reshape(1).astype(jnp.int32)
    line = lambda value: value.reshape(1, -1)
    full = 4 * stretch
    count = 2 * masks
    shaped = jax.ShapeDtypeStruct

    keys, values, queries, context, probs, picked = local_call(
        project_kernel,
        (
            shaped((full, width), BF16),
            shaped((full, width), BF16),
            shaped((count, width), BF16),
            shaped((count, width), BF16),
            shaped((heads, count, full), F32),
            shaped((count, model), BF16),
        ),
        "project",
    )(core_scalar, half, peer, pos, seg, slot_col, query_weight, line(query_bias), key_weight, value_weight, line(value_bias))

    two = context.reshape(2, masks, width)
    ctx_peer = trade(take(two, 1 - core))
    normed_low, feed, branch_low, grad_h1, small = local_call(
        masked_kernel,
        (
            shaped((masks, model), BF16),
            shaped((masks, model), BF16),
            shaped((masks, model), BF16),
            shaped((masks, model), F32),
            shaped((16, model), F32),
        ),
        "masked",
    )(
        core_scalar, take(two, core), ctx_peer, picked, cot_half, cot_peer, pos, slot_col, output_weight, line(output_bias),
        line(first_gain), line(first_shift), up_weight, line(up_bias), down_weight, line(down_bias), line(second_gain), line(second_shift),
    )
    branch_peer = trade(branch_low)
    grads, igrad_own, igrad_peer, bias = local_call(
        back_kernel,
        (
            shaped((4, model, width), BF16),
            shaped((2 * stretch, model), F32),
            shaped((2 * stretch, model), BF16),
            shaped((2, width), F32),
        ),
        "back",
        [pltpu.VMEM((count, width), BF16), pltpu.VMEM((full, width), BF16), pltpu.VMEM((full, width), BF16)],
    )(
        core_scalar, keys, values, queries, context, probs, picked, branch_low, branch_peer, grad_h1, half, peer, pos_col, slot_row,
        query_weight, key_weight, value_weight, output_weight,
    )
    igrad = igrad_own + trade(igrad_peer).astype(F32)
    igrad_other = swap(igrad[stretch:].astype(BF16)).astype(F32)
    igrad_mine = igrad[:stretch]
    input_grad = jnp.where(row == 0, jnp.stack([igrad_mine, igrad_other]), jnp.stack([igrad_other, igrad_mine]))

    ctx_own, ctx_other = local_call(
        attend_kernel, (shaped((2 * stretch, width), BF16), shaped((2 * stretch, width), BF16)), "attend"
    )(core_scalar, half, peer, seg, seg_col, keys, values, query_weight, line(query_bias))
    out_mine, out_other = local_call(
        feed_kernel, (shaped((stretch, model), BF16), shaped((stretch, model), BF16)), "feed"
    )(
        core_scalar, ctx_own, trade(ctx_other), half, output_weight, line(output_bias), line(first_gain), line(first_shift),
        up_weight, line(up_bias), down_weight, line(down_bias), line(second_gain), line(second_shift),
    )
    out_other = swap(out_other)
    layer_output = jnp.where(row == 0, jnp.stack([out_mine, out_other]), jnp.stack([out_other, out_mine]))

    wide = jnp.zeros((2, model), F32)
    bias_rows = lax.dynamic_update_slice(wide, bias, (0, core * width))
    base = hidden // model + 6
    small = jnp.concatenate([small[:base], bias_rows, small[base + 2 :]], axis=0)

    both = ("rows", "seq")
    small = lax.psum(small, both)
    zero = jnp.zeros((model, model), F32)
    wide_grads = [lax.dynamic_update_slice(zero, grads[k].astype(F32), (0, core * width)) for k in (1, 2, 3)]
    rows_wo = grads[0].reshape(2, width, width).transpose(1, 0, 2).reshape(width, model).astype(F32)
    wide_grads.append(lax.dynamic_update_slice(zero, rows_wo, (core * width, 0)))
    grad_wq, grad_wk, grad_wv, grad_wo = lax.psum(tuple(wide_grads), both)
    pieces = []
    units = hidden // 8
    for part in range(8):
        (piece,) = local_call(hidden_kernel, (shaped((units, 2 * model), BF16),), "hidden")(
            jnp.full((1,), part, jnp.int32), normed_low, feed, up_weight, line(up_bias), down_weight
        )
        pieces.append(piece.astype(F32))
    hidden_grads = lax.psum_scatter(jnp.concatenate(pieces, axis=0), both, scatter_dimension=0, tiled=True)

    up_part, down_part = hidden_grads[:, :model], hidden_grads[:, model:]
    return outputs(layer_output, input_grad, grad_wq, grad_wk, grad_wv, grad_wo, up_part, down_part, small)


def solution(mesh):
    split = P("rows", "seq", None)
    in_specs = (split, split, P("rows", None), P("rows", None, None)) + (P(),) * 15
    out_specs = (split, split) + (P(),) * 9 + (P(None, ("rows", "seq")), P(), P(("rows", "seq"), None), P(), P(), P())
    return jax.shard_map(
        functools.partial(on_device, mesh.shape["rows"]), mesh=mesh, in_specs=in_specs, out_specs=out_specs, check_vma=False
    )
```

```python
import functools

import jax
import jax.numpy as jnp
from jax import lax
from jax.experimental import pallas as pl
from jax.experimental.pallas import tpu as pltpu
from jax.sharding import PartitionSpec as P

HEADS = 12
EPSILON = 1e-12
MASKED_SCORE = -1000000000.0
F32 = jnp.float32
BF16 = jnp.bfloat16
MESH = pl.DeviceIdType.MESH
VMEM_LIMIT = 56 * 2**20
ORDERS = ("yxz", "yxz", "xyz", "zxy")
PLAN = {
    "G0": ("Sr00",),
    "p0": ("Sr10",),
    "p1": ("Sr20",),
    "dx": ("Ss0", "Sr30"),
    "a1": ("Es0", "Ss1", "Er20", "Sr21", "Ed", "Si", "Er00", "Sr01"),
    "a2": ("Ef", "Er10", "Sr11"),
    "a4": ("Es1", "Ss2"),
    "a5": ("EH", "Es2", "Ss3", "Er11", "Sr12", "Er21", "Er01"),
    "a6": ("Sr22",),
    "a8": ("Er30", "Sr31"),
    "a9": ("Ei",),
    "f0": ("Er31", "Sr32", "Sr02"),
    "f1": ("Er12", "Sg12"),
    "f2": ("Es3", "Er22", "Er32", "Sg32"),
    "f3": ("So",),
    "f4": ("Eg32", "Sg31", "Sg22"),
    "f5": ("Er02", "Sg02", "Eg12", "Sg11", "Eh"),
    "f6": ("Eg31",),
    "end": ("Sg30", "Eg11", "Sg10", "Eg22", "Sg21", "Eg02", "Sg01", "Eo", "Eg01", "Sg00", "Eg21", "Sg20", "Eg30", "St3", "Eg10", "St1", "Eg20", "St2", "Et3", "Et1", "Eg00", "St0", "Et2", "Et0"),
}


def dot(left, right):
    return lax.dot_general(left, right, (((1,), (0,)), ((), ())), preferred_element_type=F32)


def dot_nt(left, right):
    return lax.dot_general(left, right, (((1,), (1,)), ((), ())), preferred_element_type=F32)


def dot_tn(left, right):
    return lax.dot_general(left, right, (((0,), (0,)), ((), ())), preferred_element_type=F32)


def norm_parts(hidden):
    centred = hidden - jnp.mean(hidden, axis=-1, keepdims=True)
    variance = jnp.mean(centred * centred, axis=-1, keepdims=True)
    scale = lax.rsqrt(variance + EPSILON)
    return centred * scale, scale


def norm_back(grad, normed, scale, gain):
    scaled = grad * gain
    along = jnp.mean(scaled * normed, axis=-1, keepdims=True)
    return (scaled - jnp.mean(scaled, axis=-1, keepdims=True) - normed * along) * scale


GELU_A = 0.7978845608028654
GELU_B = 0.044715


def gelu_parts(value):
    square = value * value
    bent = jnp.tanh(GELU_A * value * (1.0 + GELU_B * square))
    half = 0.5 * (1.0 + bent)
    slope = half + 0.5 * value * (1.0 - bent * bent) * (GELU_A * (1.0 + 3.0 * GELU_B * square))
    return value * half, slope


def gelu_only(value):
    bent = jnp.tanh(GELU_A * value * (1.0 + GELU_B * value * value))
    return 0.5 * value * (1.0 + bent)


def lane_is(shape, low, high):
    lane = lax.broadcasted_iota(jnp.int32, shape, len(shape) - 1)
    return (lane >= low) & (lane < high)


def project_kernel(core, half, peer, pos, seg, slots, wq, bq, wk, wv, bv, keys, values, queries, context, probs, picked):
    width = keys.shape[1]
    mine = pl.ds(pl.multiple_of(core[0] * width, 128), width)
    count = slots.shape[0]
    tokens_half = half.shape[0]
    chosen = jnp.where(slots[...] == pos[...], 1.0, 0.0).astype(BF16)
    rows = dot(chosen[:, :tokens_half], half[...]) + dot(chosen[:, tokens_half:], peer[...])
    rows = rows.astype(BF16)
    picked[...] = rows
    queries[...] = (dot(rows, wq[:, mine]) + bq[:, mine]).astype(BF16)
    for place, part in ((0, half), (tokens_half, peer)):
        for start in range(0, tokens_half, 256):
            block = part[start : start + 256, :]
            there = slice(place + start, place + start + 256)
            keys[there, :] = dot(block, wk[:, mine]).astype(BF16)
            values[there, :] = (dot(block, wv[:, mine]) + bv[:, mine]).astype(BF16)
    sequence = lax.broadcasted_iota(jnp.int32, (count, 1), 0) // (count // 2)
    same = seg[...] == sequence
    for pair in range(width // 128):
        lanes = slice(pair * 128, pair * 128 + 128)
        pair_queries = queries[:, lanes].astype(F32) * 0.125
        pair_keys, pair_values = keys[:, lanes], values[:, lanes]
        outs = []
        for side in range(2):
            keep = lane_is((count, 128), side * 64, side * 64 + 64)
            head_queries = jnp.where(keep, pair_queries, 0.0).astype(BF16)
            scores = jnp.where(same, dot_nt(head_queries, pair_keys), MASKED_SCORE)
            weights = jnp.exp(scores - jnp.max(scores, axis=-1, keepdims=True))
            share = weights / jnp.sum(weights, axis=-1, keepdims=True)
            probs[pair * 2 + side] = share
            outs.append(dot(share.astype(BF16), pair_values))
        first = lane_is((count, 128), 0, 64)
        context[:, lanes] = jnp.where(first, outs[0], outs[1]).astype(BF16)


def masked_kernel(core, ctx_own, ctx_peer, picked, cot_half, cot_peer, pos, slots, wo, bo, g1, s1, wup, bup, wdown, bdown, g2, s2, normed_low, feed, branch_low, grad_h1, small):
    count, width = ctx_own.shape
    hidden = wup.shape[1]
    model = wup.shape[0]
    tokens_half = cot_half.shape[0]
    mine = pl.multiple_of(core[0] * count, 16)
    is_first = core[0] == 0
    left = jnp.where(is_first, ctx_own[...], ctx_peer[...])
    right = jnp.where(is_first, ctx_peer[...], ctx_own[...])
    branch = dot(left, wo[:width, :]) + dot(right, wo[width:, :]) + bo[...]
    h1 = picked[pl.ds(mine, count), :].astype(F32) + branch
    n1, r1 = norm_parts(h1)
    y1 = n1 * g1[...] + s1[...]
    y1_low = y1.astype(BF16)
    normed_low[...] = y1_low
    total = y1 + bdown[...]
    slopes = []
    step = model
    for start in range(0, hidden, step):
        pre = dot(y1_low, wup[:, start : start + step]) + bup[:, start : start + step]
        act, slope = gelu_parts(pre)
        slopes.append(slope)
        total = total + dot(act.astype(BF16), wdown[start : start + step, :])
    n2, r2 = norm_parts(total)
    chosen = jnp.where(slots[pl.ds(mine, count), :] == pos[...], 1.0, 0.0).astype(BF16)
    grad = dot(chosen[:, :tokens_half], cot_half[...]) + dot(chosen[:, tokens_half:], cot_peer[...])
    gh2 = norm_back(grad, n2, r2, g2[...])
    gf = gh2.astype(BF16)
    feed[...] = gf
    gy1 = gh2
    small[...] = jnp.zeros_like(small)
    for place, start in enumerate(range(0, hidden, step)):
        ga = dot_nt(gf, wdown[start : start + step, :])
        gp = (ga * slopes[place]).astype(BF16)
        small[place : place + 1, :] = jnp.sum(gp.astype(F32), axis=0, keepdims=True)
        gy1 = gy1 + dot_nt(gp, wup[:, start : start + step])
    gh1 = norm_back(gy1, n1, r1, g1[...])
    grad_h1[...] = gh1
    gb = gh1.astype(BF16)
    branch_low[...] = gb
    base = hidden // step
    for place, value in enumerate((gy1 * n1, gy1, grad * n2, grad, gb.astype(F32), gf.astype(F32))):
        small[base + place : base + place + 1, :] = jnp.sum(value, axis=0, keepdims=True)


def back_kernel(core, keys, values, queries, context, probs, picked, gb_own, gb_peer, gh1, half, peer, pos_col, slots_row, wq, wk, wv, wo, grads, igrad_own, igrad_peer, bias, dq_low, dk_low, dv_low):
    width = keys.shape[1]
    count = queries.shape[0]
    own = gb_own.shape[0]
    tokens_half = half.shape[0]
    is_first = core[0] == 0
    mine = pl.ds(pl.multiple_of(core[0] * width, 128), width)
    mine_rows = pl.ds(pl.multiple_of(core[0] * width, 128), width)
    top = jnp.where(is_first, gb_own[...], gb_peer[...])
    low = jnp.where(is_first, gb_peer[...], gb_own[...])
    gb = jnp.concatenate([top, low], axis=0)
    gctx = dot_nt(gb, wo[mine_rows, :]).astype(BF16)
    for pair in range(width // 128):
        lanes = slice(pair * 128, pair * 128 + 128)
        pair_keys, pair_values, pair_queries = keys[:, lanes], values[:, lanes], queries[:, lanes]
        pair_gctx = gctx[:, lanes]
        dqs, dks, dvs = [], [], []
        for side in range(2):
            keep = lane_is((count, 128), side * 64, side * 64 + 64)
            head_gctx = jnp.where(keep, pair_gctx.astype(F32), 0.0).astype(BF16)
            share = probs[pair * 2 + side]
            gp = dot_nt(head_gctx, pair_values)
            spread = jnp.sum(share * gp, axis=-1, keepdims=True)
            gs = (share * (gp - spread)).astype(BF16)
            dqs.append(dot(gs, pair_keys))
            dks.append(dot_tn(gs, pair_queries))
            dvs.append(dot_tn(share.astype(BF16), pair_gctx))
        first = lane_is((count, 128), 0, 64)
        dq_low[:, lanes] = (jnp.where(first, dqs[0], dqs[1]) * 0.125).astype(BF16)
        first = lane_is((2 * tokens_half, 128), 0, 64)
        dk_low[:, lanes] = (jnp.where(first, dks[0], dks[1]) * 0.125).astype(BF16)
        dv_low[:, lanes] = jnp.where(first, dvs[0], dvs[1]).astype(BF16)
    grads[1] = dot_tn(picked[...], dq_low[...]).astype(BF16)
    gwo = dot_tn(context[...], gb).astype(BF16)
    grads[0, :width, :] = gwo[:, :width]
    grads[0, width:, :] = gwo[:, width:]
    for place, part in ((2, dk_low), (3, dv_low)):
        total = dot_tn(half[...], part[:tokens_half, :]) + dot_tn(peer[...], part[tokens_half:, :])
        grads[place] = total.astype(BF16)
    bias[0:1, :] = jnp.sum(dq_low[...].astype(F32), axis=0, keepdims=True)
    bias[1:2, :] = jnp.sum(dv_low[...].astype(F32), axis=0, keepdims=True)
    spread_rows = dot_nt(dq_low[...], wq[:, mine])
    zero = jnp.zeros((own, wq.shape[0]), F32)
    spread_rows = spread_rows + jnp.concatenate(
        [jnp.where(is_first, gh1[...], zero), jnp.where(is_first, zero, gh1[...])], axis=0
    )
    high = spread_rows.astype(BF16)
    rest = (spread_rows - high.astype(F32)).astype(BF16)
    for start in range(0, 2 * tokens_half, 256):
        here = slice(start, start + 256)
        chosen = jnp.where(pos_col[here, :] == slots_row[...], 1.0, 0.0).astype(BF16)
        total = dot(chosen, high) + dot(chosen, rest)
        total = total + dot_nt(dk_low[here, :], wk[:, mine]) + dot_nt(dv_low[here, :], wv[:, mine])
        if start < tokens_half:
            igrad_own[here, :] = total
        else:
            igrad_peer[start - tokens_half : start - tokens_half + 256, :] = total.astype(BF16)


def attend_kernel(core, half, peer, seg, seg_col, keys, values, wq, bq, own, other):
    width = keys.shape[1]
    mine = pl.ds(pl.multiple_of(core[0] * width, 128), width)
    tile = 256
    for part, out in ((half, own), (peer, other)):
        place = 0 if part is half else half.shape[0]

        def body(step, carry, part=part, out=out, place=place):
            here = pl.ds(pl.multiple_of(step * tile, tile), tile)
            queries = (dot(part[here, :], wq[:, mine]) + bq[:, mine]).astype(BF16).astype(F32) * 0.125
            same = seg_col[pl.ds(pl.multiple_of(place + step * tile, tile), tile), :] == seg[...]
            for pair in range(width // 128):
                lanes = slice(pair * 128, pair * 128 + 128)
                outs = []
                for side in range(2):
                    keep = lane_is((tile, 128), side * 64, side * 64 + 64)
                    head_queries = jnp.where(keep, queries[:, lanes], 0.0).astype(BF16)
                    scores = jnp.where(same, dot_nt(head_queries, keys[:, lanes]), MASKED_SCORE)
                    weights = jnp.exp(scores - jnp.max(scores, axis=-1, keepdims=True))
                    total = jnp.sum(weights, axis=-1, keepdims=True)
                    outs.append(dot(weights.astype(BF16), values[:, lanes]) / total)
                first = lane_is((tile, 128), 0, 64)
                out[here, lanes] = jnp.where(first, outs[0], outs[1]).astype(BF16)
            return carry

        lax.fori_loop(0, part.shape[0] // tile, body, 0)


def feed_kernel(core, ctx_own, ctx_peer, half, wo, bo, g1, s1, wup, bup, wdown, bdown, g2, s2, own, other):
    width = ctx_own.shape[1]
    hidden, model = wdown.shape
    is_first = core[0] == 0
    tile = own.shape[0]
    for start, out in ((0, own), (tile, other)):
        here = slice(start, start + tile)
        left = jnp.where(is_first, ctx_own[here, :], ctx_peer[here, :])
        right = jnp.where(is_first, ctx_peer[here, :], ctx_own[here, :])
        branch = dot(left, wo[:width, :]) + dot(right, wo[width:, :]) + bo[...]
        n1, _ = norm_parts(half[here, :].astype(F32) + branch)
        y1 = n1 * g1[...] + s1[...]
        y1_low = y1.astype(BF16)
        total = y1 + bdown[...]
        for place in range(0, hidden, model):
            pre = dot(y1_low, wup[:, place : place + model]) + bup[:, place : place + model]
            total = total + dot(gelu_only(pre).astype(BF16), wdown[place : place + model, :])
        n2, _ = norm_parts(total)
        out[...] = (n2 * g2[...] + s2[...]).astype(BF16)


def hidden_kernel(slot, normed, feed, wup, bup, wdown, out):
    units = out.shape[0]
    model = normed.shape[1]
    mine = pl.ds(pl.multiple_of(slot[0] * units, 128), units)
    pre = dot(normed[...], wup[:, mine]) + bup[:, mine]
    act, slope = gelu_parts(pre)
    ga = dot_nt(feed[...], wdown[mine, :])
    gp = (ga * slope).astype(BF16)
    out[:, :model] = dot_tn(gp, normed[...]).astype(BF16)
    out[:, model:] = dot_tn(act.astype(BF16), feed[...]).astype(BF16)


def place_here():
    row, seq = lax.axis_index("rows"), lax.axis_index("seq")
    return row // 2, row % 2, seq // 2, seq % 2


def device(z, x, y, core):
    return (z * 2 + x, y * 2 + core)


def layer_kernel(
    tokens, cotangent, segments_in, slots_in, up_bias_in, bq_in, bv_in, bo_in, g1_in, s1_in, bdown_in, g2_in, s2_in, wq, wk, wv, wo, wup, wdown,
    layer_out, input_grad, out_o, out_0, out_1, out_2, up_out, down_out, small_out,
    segments, slots, up_bias, bq, bv, bo, g1, s1, bdown, g2, s2, vecs, wq_t, wkv_t, wo_t, keys_t, values_t,
    xs, xs_t, cots, cot_part, cot_in, cot_sum, cot_far, dx_send, dx_in, wq_v, wk_v, wv_v, wo_v, wup_v, wdown_v, keys, values, queries, context, probs, picked, chosen, ctx_both, gb_both,
    slopes, dq_low, dkv_low, grads, hidden_grads, hidden_in, fac_normed, fac_feed, grad_h1, small_in, small_z,
    all_queries, all_context, ctx_in, total, y1_keep, out_send, igrad_send, igrad_in,
    in_o, in_0, in_1, in_2, local_sem, send_sem, recv_sem,
):
    z, x, y, core = place_here()
    row = y
    stretch, model = tokens.shape[1:]
    half = 2 * stretch
    full = 2 * half
    width = wq_v.shape[1]
    masks = slots.shape[2]
    count = 2 * masks
    hidden = wup.shape[1]
    parts = hidden // model
    units = down_out.shape[0]
    others = [(z + k) % 4 for k in (1, 2, 3)]
    at_y, at_x, twin = device(z, x, 1 - y, core), device(z, 1 - x, y, core), device(z, x, y, 1 - core)
    columns = [device(o, x, y, core) for o in others]
    mine = pl.ds(pl.multiple_of(core * width, 128), width)
    my_slots = pl.ds(pl.multiple_of(core * masks, 16), masks)
    twin_slots = pl.ds(pl.multiple_of((1 - core) * masks, 16), masks)
    pending = []

    def local(src, dst, index):
        copy = pltpu.make_async_copy(src, dst, local_sem.at[index])
        copy.start()
        return copy

    def remote(src, dst, index, target):
        return pltpu.make_async_remote_copy(
            src_ref=src, dst_ref=dst, send_sem=send_sem.at[index], recv_sem=recv_sem.at[index],
            device_id=target, device_id_type=MESH,
        )

    def push(src, dst, index, target):
        copy = remote(src, dst, index, target)
        copy.start()
        pending.append(copy)
        return copy

    def vector(index):
        return vecs[index : index + 1, :]

    def half_vector(index):
        return vecs[index : index + 1, mine]

    small_pairs = (
        (segments_in, segments), (slots_in, slots), (up_bias_in, up_bias), (bq_in, bq), (bv_in, bv), (bo_in, bo), (g1_in, g1),
        (s1_in, s1), (bdown_in, bdown), (g2_in, g2), (s2_in, s2),
    )
    own_tokens = local(tokens.at[row], xs.at[pl.ds(0, stretch)], 0)
    get_wk = local(wk.at[:, mine], wk_v, 1)
    get_wv = local(wv.at[:, mine], wv_v, 2)
    get_small = [local(src, dst, 8 + k) for k, (src, dst) in enumerate(small_pairs)]
    get_wq = local(wq.at[:, mine], wq_v, 3)
    own_cot = local(cotangent, cots, 4)
    get_wo = local(wo, wo_v, 5)
    get_up = local(wup, wup_v, 6)
    get_down = local(wdown, wdown_v, 7)

    near = [(1 - x, y), (x, 1 - y), (1 - x, 1 - y)]
    greeted = [twin] + columns + [device(z, nx, ny, c) for nx, ny in near for c in range(2)]
    barrier = pltpu.get_barrier_semaphore()
    for target in greeted:
        pl.semaphore_signal(barrier, inc=1, device_id=target, device_id_type=MESH)
    pl.semaphore_wait(barrier, len(greeted))

    piece = stretch // 2
    tok_y = [
        push(tokens.at[1 - row, pl.ds(k * piece, piece)], xs.at[pl.ds(stretch + k * piece, piece)], k, at_y) for k in range(2)
    ]
    tok_c = push(tokens.at[row], xs.at[pl.ds(half, stretch)], 2, twin)

    for copy in get_small:
        copy.wait()
    for part in range(parts):
        vecs[part : part + 1, :] = up_bias[part * model : (part + 1) * model].reshape(1, model)
    for place, value in enumerate((bq, bv, bo, g1, s1, bdown, g2, s2)):
        vecs[parts + place : parts + place + 1, :] = value[...].reshape(1, model)

    def key_values(start):
        here = pl.ds(start, stretch)
        block = xs[here, :]
        block_keys = dot(block, wk_v[...]).astype(BF16)
        block_values = (dot(block, wv_v[...]) + half_vector(5)).astype(BF16)
        keys[here, :] = block_keys
        values[here, :] = block_values
        xs_t[:, here] = block.T
        keys_t[:, here] = block_keys.T
        values_t[:, here] = block_values.T

    blocks = [2 * y + core, 2 * (1 - y) + core, 2 * y + 1 - core, 2 * (1 - y) + 1 - core]
    lane = lax.broadcasted_iota(jnp.int32, (1, stretch), 1)
    pos_row = jnp.concatenate([lane + block * stretch for block in blocks], axis=1)
    seg_here = segments[pl.ds(row, 1), :]
    split = jnp.sum((1 - seg_here).astype(F32), axis=1, keepdims=True)
    pos_row = pos_row.astype(F32)
    seg_row = jnp.where(pos_row >= split, 1.0, 0.0)
    diagonal = lax.broadcasted_iota(jnp.int32, (masks, masks), 0) == lax.broadcasted_iota(jnp.int32, (masks, masks), 1)

    def slot_column(which, sequence):
        line = slots[which].astype(F32)[sequence : sequence + 1, :]
        return jnp.sum(jnp.where(diagonal, line, 0.0), axis=1, keepdims=True)

    for sequence in range(2):
        column = slot_column(row, sequence)
        chosen[sequence * masks : (sequence + 1) * masks, :] = jnp.where(column == pos_row, 1.0, 0.0).astype(BF16)
    own_cot.wait()
    for sequence in range(2):
        here = chosen[sequence * masks : (sequence + 1) * masks, :stretch]
        cot_part[0, sequence] = dot(here, cots[row]).astype(BF16)
        there = jnp.where(slot_column(1 - row, sequence) == pos_row[:, :stretch], 1.0, 0.0).astype(BF16)
        cot_part[1, sequence] = dot(there, cots[1 - row]).astype(BF16)
    cot_c = push(cot_part.at[:, 1 - core], cot_in, 4, twin)

    own_tokens.wait()
    get_wk.wait()
    get_wv.wait()
    key_values(0)
    tok_c.wait_recv()
    key_values(half)
    get_wq.wait()
    for pair in range(width // 128):
        lanes = slice(pair * 128, pair * 128 + 128)
        wkv_t[pair * 256 : pair * 256 + 128, :] = wk_v[:, lanes].T
        wkv_t[pair * 256 + 128 : pair * 256 + 256, :] = wv_v[:, lanes].T
    wq_t[...] = wq_v[...].T
    forward = []
    for k in range(2):
        tok_y[k].wait_recv()
        src = xs.at[pl.ds(stretch + k * piece, piece)]
        forward.append(push(src, xs.at[pl.ds(half + stretch + k * piece, piece)], 5 + k, twin))
    cot_c.wait_recv()
    cot_sum[...] = cot_part[:, core] + cot_in[...]
    cot_y = push(cot_sum.at[1], cot_far, 3, at_y)
    key_values(stretch)
    for copy in forward:
        copy.wait_recv()
    key_values(half + stretch)

    rows = dot(chosen[...], xs[...]).astype(BF16)
    picked[...] = rows
    queries[...] = (dot(rows, wq_v[...]) + half_vector(4)).astype(BF16)
    sequence = lax.broadcasted_iota(jnp.int32, (count, 1), 0) // masks
    same = seg_row == sequence.astype(F32)
    pairs = width // 128
    for pair in range(pairs):
        lanes = slice(pair * 128, pair * 128 + 128)
        pair_queries = queries[:, lanes].astype(F32) * 0.125
        pair_keys, pair_values = keys_t[lanes, :], values[:, lanes]
        outs = []
        for side in range(2):
            keep = lane_is((count, 128), side * 64, side * 64 + 64)
            head_queries = jnp.where(keep, pair_queries, 0.0).astype(BF16)
            scores = jnp.where(same, dot(head_queries, pair_keys), MASKED_SCORE)
            weights = jnp.exp(scores - jnp.max(scores, axis=-1, keepdims=True))
            share = weights / jnp.sum(weights, axis=-1, keepdims=True)
            share = share.astype(BF16)
            probs[pair * 2 + side] = share
            outs.append(dot(share, pair_values))
        first = lane_is((count, 128), 0, 64)
        context[:, lanes] = jnp.where(first, outs[0], outs[1]).astype(BF16)
    ctx_both[core] = context[my_slots, :]
    ctx_c = push(context.at[twin_slots], ctx_both.at[core], 7, twin)

    for start in range(0, full, stretch):
        value = (dot(xs[start : start + stretch, :], wq_v[...]) + half_vector(4)).astype(BF16)
        all_queries[start : start + stretch, :] = (value.astype(F32) * 0.125).astype(BF16)
    get_wo.wait()
    wo_t[...] = wo_v[mine, :].T
    ctx_c.wait_recv()

    branch = dot(ctx_both[0], wo_v[:width, :]) + dot(ctx_both[1], wo_v[width:, :]) + vector(6)
    n1, r1 = norm_parts(picked[my_slots, :].astype(F32) + branch)
    y1 = n1 * vector(7) + vector(8)
    y1_low = y1.astype(BF16)
    fac_normed[core, z] = y1_low
    spot = fac_normed.at[core, z]
    norm_z = [push(spot, spot, 9 + k, columns[k]) for k in range(3)]
    get_up.wait()
    get_down.wait()
    sum2 = y1 + vector(9)
    for part in range(parts):
        there = slice(part * model, (part + 1) * model)
        act, slope = gelu_parts(dot(y1_low, wup_v[:, there]) + vector(part))
        slopes[part] = slope
        sum2 = sum2 + dot(act.astype(BF16), wdown_v[there, :])
    n2, r2 = norm_parts(sum2)
    cot_y.wait_recv()
    grad = cot_sum[0].astype(F32) + cot_far[...].astype(F32)
    gh2 = norm_back(grad, n2, r2, vector(10))
    gf = gh2.astype(BF16)
    fac_feed[core, z] = gf
    spot = fac_feed.at[core, z]
    feed_z = [push(spot, spot, 12 + k, columns[k]) for k in range(3)]
    gf_t = gf.T
    gy1_t = jnp.zeros((model, masks), F32)
    small_in[0] = jnp.zeros(small_in.shape[1:], F32)
    for part in range(parts):
        there = slice(part * model, (part + 1) * model)
        gp = (dot(wdown_v[there, :], gf_t).T * slopes[part]).astype(BF16)
        small_in[0, part : part + 1, :] = jnp.sum(gp.astype(F32), axis=0, keepdims=True)
        gy1_t = gy1_t + dot(wup_v[:, there], gp.T)
    gy1 = gh2 + gy1_t.T
    gh1 = norm_back(gy1, n1, r1, vector(7))
    grad_h1[...] = gh1
    gb = gh1.astype(BF16)
    gb_both[core] = gb
    gb_c = push(gb_both.at[core], gb_both.at[core], 15, twin)
    for place, value in enumerate((gy1 * n1, gy1, grad * n2, grad, gb.astype(F32), gf.astype(F32))):
        small_in[0, parts + place : parts + place + 1, :] = jnp.sum(value, axis=0, keepdims=True)
    gb_c.wait_recv()

    spots = {"x": x, "y": y, "z": z}
    sizes = {"x": 2, "y": 2, "z": 4}
    dims = {"x": [at_x], "y": [at_y], "z": columns}
    orders = ORDERS
    ins = [in_o, in_0, in_1, in_2]
    outs = [out_o, out_0, out_1, out_2]

    def regions(job):
        base, size, found = 0, model, [(0, model)]
        for dim in orders[job]:
            size = size // sizes[dim]
            base = base + spots[dim] * size
            found.append((base, size))
        return found

    def in_place(job, stage):
        at, size = 0, model
        for dim in orders[job][:stage]:
            size = size // sizes[dim]
            at += size * (sizes[dim] - 1)
        return at, size // sizes[orders[job][stage]]

    def out_at(job, base, size):
        return outs[job].at[pl.ds(pl.multiple_of(base, 16), size), mine]

    def reduce_copies(job, stage):
        dim = orders[job][stage]
        at, size = in_place(job, stage)
        base, _ = regions(job)[stage]
        copies = []
        for k, target in enumerate(dims[dim]):
            other = (spots[dim] + k + 1) % sizes[dim]
            src = grads.at[job, pl.ds(pl.multiple_of(base + other * size, 16), size)]
            dst = ins[job].at[pl.ds(at + k * size, size)]
            copies.append(remote(src, dst, 40 + job * 20 + stage * 3 + k, target))
        return copies

    def reduce_start(job, stage):
        for copy in reduce_copies(job, stage):
            copy.start()

    def reduce_end(job, stage):
        for copy in reduce_copies(job, stage):
            copy.wait()
        dim = orders[job][stage]
        at, size = in_place(job, stage)
        base, _ = regions(job)[stage + 1]
        here = pl.ds(pl.multiple_of(base, 16), size)
        value = grads[job, here].astype(F32)
        for k in range(len(dims[dim])):
            value = value + ins[job][pl.ds(at + k * size, size)].astype(F32)
        value = value.astype(BF16)
        if stage < 2:
            grads[job, here] = value
        else:
            out_at(job, base, size)[...] = value

    def gather_copies(job, stage):
        base, size = regions(job)[stage + 1]
        spot = out_at(job, base, size)
        return [
            remote(spot, spot, 40 + job * 20 + 9 + stage * 3 + k, target)
            for k, target in enumerate(dims[orders[job][stage]])
        ]

    def twin_copy(job):
        spot = outs[job].at[:, mine]
        return remote(spot, spot, 40 + job * 20 + 18, twin)

    def gather_start(job, stage):
        for copy in gather_copies(job, stage):
            copy.start()

    def gather_end(job, stage):
        for copy in gather_copies(job, stage):
            copy.wait()

    def small_copies(stage):
        if stage < 3:
            target = (twin, at_y, at_x)[stage]
            return [remote(small_in.at[2 * stage], small_in.at[2 * stage + 1], 16 + stage, target)]
        return [remote(small_in.at[6], small_z.at[z], 19 + k, target) for k, target in enumerate(columns)]

    def small_start(stage):
        for copy in small_copies(stage):
            copy.start()

    def small_end(stage):
        for copy in small_copies(stage):
            copy.wait()
        if stage < 3:
            small_in[2 * stage + 2] = small_in[2 * stage] + small_in[2 * stage + 1]
            if stage == 2:
                small_z[z] = small_in[6]
        else:
            small_out[...] = (small_z[0] + small_z[1]) + (small_z[2] + small_z[3])

    source = x * 2 + y

    def factor_copies():
        return [remote(ref.at[core], ref.at[core], 22 + k, twin) for k, ref in enumerate((fac_normed, fac_feed))]

    def factors_on():
        for copy in norm_z + feed_z:
            copy.wait_recv()
        for copy in factor_copies():
            copy.start()

    def is_me(cy, cc):
        return (core == x) & (cy == y) & (cc == core)

    def hidden_copy(cy, cc):
        part = hidden_grads.at[pl.ds((cy * 2 + cc) * units, units)]
        return pltpu.make_async_remote_copy(
            src_ref=part, dst_ref=hidden_in.at[source], send_sem=send_sem.at[24 + cy * 2 + cc], recv_sem=recv_sem.at[24 + source],
            device_id=device(z, core, cy, cc), device_id_type=MESH,
        )

    def hidden_make():
        for copy in factor_copies():
            copy.wait()
        slot = z * 2 + core
        size = hidden_grads.shape[0]
        normed = fac_normed[...].reshape(8 * masks, model)
        feed = fac_feed[...].reshape(8 * masks, model)
        at = pl.ds(pl.multiple_of(slot * size, 128), size)
        act, slope = gelu_parts(dot(normed, wup_v[:, at]) + vecs[pl.ds(z, 1), mine])
        gp = (dot_nt(feed, wdown_v[at, :]) * slope).astype(BF16)
        hidden_grads[:, :model] = dot_tn(gp, normed).astype(BF16)
        hidden_grads[:, model:] = dot_tn(act.astype(BF16), feed).astype(BF16)
        for cy in range(2):
            for cc in range(2):
                @pl.when(jnp.logical_not(is_me(cy, cc)))
                def _(cy=cy, cc=cc):
                    hidden_copy(cy, cc).start()

                @pl.when(is_me(cy, cc))
                def _(cy=cy, cc=cc):
                    hidden_in[source] = hidden_grads[pl.ds((cy * 2 + cc) * units, units)]

    def hidden_end():
        for cy in range(2):
            for cc in range(2):
                @pl.when(jnp.logical_not(is_me(cy, cc)))
                def _(cy=cy, cc=cc):
                    hidden_copy(cy, cc).wait_send()
        for cx in range(2):
            for cy in range(2):
                @pl.when(jnp.logical_not((cx == x) & (cy == y) & (core == x)))
                def _(cx=cx, cy=cy):
                    slot = hidden_in.at[cx * 2 + cy]
                    pltpu.make_async_remote_copy(
                        src_ref=slot, dst_ref=slot, send_sem=send_sem.at[24], recv_sem=recv_sem.at[24 + cx * 2 + cy],
                        device_id=twin, device_id_type=MESH,
                    ).wait_recv()
        value = hidden_in[0].astype(F32)
        for k in range(1, 4):
            value = value + hidden_in[k].astype(F32)
        up_out[...] = value[:, :model]
        down_out[...] = value[:, model:]

    def igrad_copy():
        return remote(igrad_send, igrad_in, 29, at_y)

    def igrad_step():
        remote(dx_send, dx_in, 28, twin).wait_recv()
        input_grad[row] = input_grad[row] + dx_in[:stretch, :].astype(F32)
        igrad_send[...] = (input_grad[1 - row] + dx_in[stretch:, :].astype(F32)).astype(BF16)

    def igrad_end():
        igrad_copy().wait()
        input_grad[1 - row] = igrad_in[...].astype(F32)

    def out_copy():
        return remote(out_send, layer_out.at[row], 31, at_y)

    def act(name):
        start, kind, rest = name[0] == "S", name[1], [int(c) for c in name[2:]]
        if kind == "r":
            (reduce_start if start else reduce_end)(*rest)
        elif kind == "g":
            (gather_start if start else gather_end)(*rest)
        elif kind == "t":
            twin_copy(*rest).start() if start else twin_copy(*rest).wait()
        elif kind == "s":
            (small_start if start else small_end)(*rest)
        elif kind == "d":
            igrad_step()
        elif kind == "i":
            igrad_copy().start() if start else igrad_end()
        elif kind == "o":
            out_copy().start() if start else out_copy().wait()
        elif kind == "f":
            factors_on()
        elif kind == "H":
            hidden_make()
        elif kind == "h":
            hidden_end()

    def act_on(name):
        for each in PLAN.get(name, ()):
            act(each)

    gb = gb_both[...].reshape(count, model)
    gctx = dot(gb, wo_t[...]).astype(BF16)
    grads[0] = dot_tn(gb, context[...]).astype(BF16)
    act_on("G0")
    for pair in range(pairs):
        lanes = slice(pair * 128, pair * 128 + 128)
        pair_keys, pair_values, pair_queries = keys[:, lanes], values_t[lanes, :], queries[:, lanes]
        pair_gctx = gctx[:, lanes]
        dqs, dks, dvs = [], [], []
        for side in range(2):
            keep = lane_is((count, 128), side * 64, side * 64 + 64)
            head_gctx = jnp.where(keep, pair_gctx.astype(F32), 0.0).astype(BF16)
            low_share = probs[pair * 2 + side]
            share = low_share.astype(F32)
            gp = dot(head_gctx, pair_values)
            spread = jnp.sum(share * gp, axis=-1, keepdims=True)
            gs = (share * (gp - spread)).astype(BF16)
            dqs.append(dot(gs, pair_keys))
            dks.append(dot_tn(gs, pair_queries))
            dvs.append(dot_tn(low_share, pair_gctx))
        first = lane_is((count, 128), 0, 64)
        dq = (jnp.where(first, dqs[0], dqs[1]) * 0.125).astype(BF16)
        dq_low[:, lanes] = dq
        first = lane_is((full, 128), 0, 64)
        dk = (jnp.where(first, dks[0], dks[1]) * 0.125).astype(BF16)
        dv = jnp.where(first, dvs[0], dvs[1]).astype(BF16)
        both = slice(pair * 256, pair * 256 + 256)
        dkv_low[:, pair * 256 : pair * 256 + 128] = dk
        dkv_low[:, pair * 256 + 128 : pair * 256 + 256] = dv
        grads[1 + pair, :, :128] = dot_tn(picked[...], dq).astype(BF16)
        grads[1 + pair, :, 128:] = dot(xs_t[...], dkv_low[:, both]).astype(BF16)
        act_on("p" + str(pair))
        there = pl.ds(pl.multiple_of(core * width + pair * 128, 128), 128)
        small_in[0, parts + 6 : parts + 7, there] = jnp.sum(dq.astype(F32), axis=0, keepdims=True)
        small_in[0, parts + 7 : parts + 8, there] = jnp.sum(dv.astype(F32), axis=0, keepdims=True)

    spread_rows = dot(dq_low[...], wq_t[...])
    zero = jnp.zeros((masks, model), F32)
    is_first = core == 0
    gh1 = grad_h1[...]
    spread_rows = spread_rows + jnp.concatenate([jnp.where(is_first, gh1, zero), jnp.where(is_first, zero, gh1)], axis=0)
    high = spread_rows.astype(BF16)
    rest = (spread_rows - high.astype(F32)).astype(BF16)
    for start in (half, half + stretch, 0, stretch):
        here = slice(start, start + stretch)
        value = dot_tn(chosen[:, here], high) + dot_tn(chosen[:, here], rest)
        value = value + dot(dkv_low[here, :], wkv_t[...])
        if start < half:
            input_grad[row if start == 0 else 1 - row] = value
        else:
            dx_send[start - half : start - half + stretch, :] = value.astype(BF16)
            if start > half:
                push(dx_send, dx_in, 28, twin)

    act_on("dx")

    def hooks(step, prefix, count):
        for at in range(count):
            if prefix + str(at) in PLAN:
                @pl.when(step == at)
                def _(at=at):
                    act_on(prefix + str(at))

    def ctx_copy():
        return remote(all_context.at[pl.ds(half, half)], ctx_in, 30, twin)

    def attend_step(step, carry):
        tile, pair = (step // pairs + 2) % 4, step % pairs
        here = pl.ds(pl.multiple_of(tile * stretch, stretch), stretch)
        lanes = pl.ds(pl.multiple_of(pair * 128, 128), 128)
        block = 2 * (y + (tile % 2) * (1 - 2 * y)) + core + (tile // 2) * (1 - 2 * core)
        place = lax.broadcasted_iota(jnp.int32, (stretch, 1), 0) + block * stretch
        seg_col = jnp.where(place.astype(F32) >= split, 1.0, 0.0)
        same_here = seg_col == seg_row
        pair_queries = all_queries[here, lanes].astype(F32)
        pair_keys, pair_values = keys_t[lanes, :], values[:, lanes]
        found = []
        for side in range(2):
            keep = lane_is((stretch, 128), side * 64, side * 64 + 64)
            head_queries = jnp.where(keep, pair_queries, 0.0).astype(BF16)
            scores = jnp.where(same_here, dot(head_queries, pair_keys), MASKED_SCORE)
            weights = jnp.exp(scores - jnp.max(scores, axis=-1, keepdims=True))
            found.append(dot(weights.astype(BF16), pair_values) / jnp.sum(weights, axis=-1, keepdims=True))
        first = lane_is((stretch, 128), 0, 64)
        all_context[here, lanes] = jnp.where(first, found[0], found[1]).astype(BF16)

        @pl.when(step == 2 * pairs - 1)
        def _():
            ctx_copy().start()

        hooks(step, "a", 4 * pairs)
        return carry

    lax.fori_loop(0, 4 * pairs, attend_step, 0)
    ctx_copy().wait()

    def feed_step(step, carry):
        tile, part = 1 - step // parts, step % parts
        here = pl.ds(pl.multiple_of(tile * stretch, stretch), stretch)

        @pl.when(part == 0)
        def _():
            left = jnp.where(is_first, all_context[here, :], ctx_in[here, :])
            right = jnp.where(is_first, ctx_in[here, :], all_context[here, :])
            here_branch = dot(left, wo_v[:width, :]) + dot(right, wo_v[width:, :]) + vector(6)
            normed, _ = norm_parts(xs[here, :].astype(F32) + here_branch)
            value = normed * vector(7) + vector(8)
            y1_keep[...] = value.astype(BF16)
            total[...] = value + vector(9)

        there = pl.ds(pl.multiple_of(part * model, model), model)
        pre = dot(y1_keep[...], wup_v[:, there]) + vecs[pl.ds(part, 1), :]
        total[...] += dot(gelu_only(pre).astype(BF16), wdown_v[there, :])

        @pl.when(part == parts - 1)
        def _():
            normed, _ = norm_parts(total[...])
            value = (normed * vector(10) + vector(11)).astype(BF16)

            @pl.when(tile == 1)
            def _():
                out_send[...] = value

            @pl.when(tile == 0)
            def _():
                layer_out[row] = value

        hooks(step, "f", 2 * parts)
        return carry

    lax.fori_loop(0, 2 * parts, feed_step, 0)
    act_on("end")
    for copy in pending:
        copy.wait_send()


def vmem(count):
    return [pl.BlockSpec(memory_space=pltpu.VMEM)] * count


def local_call(body, outs, name, scratch=()):
    def call(core, *operands):
        return pl.pallas_call(
            body,
            out_shape=outs,
            in_specs=[pl.BlockSpec(memory_space=pltpu.SMEM)] + vmem(len(operands)),
            out_specs=vmem(len(outs)),
            scratch_shapes=list(scratch),
            compiler_params=pltpu.CompilerParams(vmem_limit_bytes=VMEM_LIMIT),
            name=name,
        )(core, *operands)

    return call


def finish_kernel(parts, go, g0, g1, g2, layer_in, igrad_in, up_in, down_in, small, wq, wk, wv, wo, layer_out, igrad, up, down, up_bias, *vectors):
    wo[...] = go[...].T.astype(F32)
    for pair, ref in enumerate((g0, g1, g2)):
        for core in range(2):
            at = core * 384 + pair * 128
            for place, out in enumerate((wq, wk, wv)):
                begin = core * 384 + place * 128
                out[:, at : at + 128] = ref[:, begin : begin + 128].astype(F32)
    layer_out[...] = layer_in[...]
    igrad[...] = igrad_in[...]
    up[...] = up_in[...]
    down[...] = down_in[...]

    @pl.when(pl.program_id(0) == 0)
    def _():
        model = small.shape[1]
        for part in range(parts):
            up_bias[part * model : (part + 1) * model] = small[part]
        for place, out in enumerate(vectors):
            out[...] = small[parts + place]


def finish(layer_output, input_grad, go, g0, g1, g2, up_part, down_part, small, hidden):
    model = go.shape[0]
    stretch, units, parts = layer_output.shape[1], up_part.shape[0], hidden // model
    shaped = jax.ShapeDtypeStruct
    rows = pl.BlockSpec((128, model), lambda i: (i, 0))
    columns = pl.BlockSpec((model, 128), lambda i: (0, i))
    tokens = pl.BlockSpec((2, stretch, 128), lambda i: (0, 0, i))
    unit = pl.BlockSpec((units, 128), lambda i: (0, i))
    line = pl.BlockSpec((model,), lambda i: (0,))
    square, vector = shaped((model, model), F32), shaped((model,), F32)
    found = pl.pallas_call(
        functools.partial(finish_kernel, parts),
        grid=(model // 128,),
        out_shape=(square,) * 4
        + (shaped(layer_output.shape, BF16), shaped(input_grad.shape, F32), shaped(up_part.shape, F32), shaped(down_part.shape, F32))
        + (shaped((hidden,), F32),)
        + (vector,) * 8,
        in_specs=[columns, rows, rows, rows, tokens, tokens, unit, unit, pl.BlockSpec(small.shape, lambda i: (0, 0))],
        out_specs=[rows] * 4 + [tokens, tokens, unit, unit, pl.BlockSpec((hidden,), lambda i: (0,))] + [line] * 8,
        compiler_params=pltpu.CompilerParams(vmem_limit_bytes=VMEM_LIMIT),
        name="finish",
    )(go, g0, g1, g2, layer_output, input_grad, up_part, down_part, small)
    wq, wk, wv, wo, layer_output, input_grad, up_part, down_part, up_bias, g1, s1, g2, s2, ob, db, qb, vb = found
    return layer_output, input_grad, wq, qb, wk, wv, vb, wo, ob, g1, s1, up_part.T, up_bias, down_part, db, g2, s2


def outputs(layer_output, input_grad, grad_wq, grad_wk, grad_wv, grad_wo, up_part, down_part, small):
    model = grad_wq.shape[0]
    base = small.shape[0] - 12
    vector = lambda index: small[index]
    return (
        layer_output,
        input_grad,
        grad_wq.astype(F32),
        vector(base + 6),
        grad_wk.astype(F32),
        grad_wv.astype(F32),
        vector(base + 7),
        grad_wo.astype(F32),
        vector(base + 4),
        vector(base),
        vector(base + 1),
        up_part.T,
        small[:base].reshape(-1),
        down_part,
        vector(base + 5),
        vector(base + 2),
        vector(base + 3),
    )


def layer_call(tokens, cotangent, segment_ids, mask_positions, vectors, weights):
    _, stretch, model = tokens.shape
    hidden = weights[4].shape[1]
    masks = mask_positions.shape[2]
    count, half, full, width = 2 * masks, 2 * stretch, 4 * stretch, model // 2
    units = hidden // 32
    shaped = jax.ShapeDtypeStruct
    low = lambda *shape: pltpu.VMEM(shape, BF16)
    wide = lambda *shape: pltpu.VMEM(shape, F32)
    scratch = [pltpu.VMEM(small.shape, small.dtype) for small in (segment_ids, mask_positions) + vectors]
    scratch += [
        wide(hidden // model + 8, model), low(width, model), low(model, model), low(model, width), low(width, full), low(width, full),
        low(full, model), low(model, full), low(2, stretch, model), low(2, 2, masks, model), low(2, masks, model), low(2, masks, model),
        low(masks, model), low(half, model), low(half, model), low(model, width), low(model, width), low(model, width), low(model, model),
        low(model, hidden), low(hidden, model), low(full, width), low(full, width), low(count, width), low(count, width),
        low(HEADS // 2, count, full), low(count, model), low(count, full), low(2, masks, width), low(2, masks, model),
        wide(hidden // model, masks, model), low(count, width), low(full, model), low(4, model, width),
        low(4 * units, 2 * model), low(4, units, 2 * model), low(2, 4, masks, model), low(2, 4, masks, model),
        wide(masks, model), wide(7, 16, model), wide(4, 16, model),
        low(full, width), low(full, width), low(half, width), wide(stretch, model), low(stretch, model), low(stretch, model),
        low(stretch, model), low(stretch, model),
    ]
    for order in ORDERS:
        size, at = model, 0
        for dim in order:
            ways = 4 if dim == "z" else 2
            size //= ways
            at += size * (ways - 1)
        scratch.append(low(at, width))
    scratch += [pltpu.SemaphoreType.DMA((8 + 2 + len(vectors),)), pltpu.SemaphoreType.DMA((120,)), pltpu.SemaphoreType.DMA((120,))]
    anywhere = [pl.BlockSpec(memory_space=pltpu.HBM)]
    return pl.pallas_call(
        layer_kernel,
        out_shape=(
            shaped((2, stretch, model), BF16),
            shaped((2, stretch, model), F32),
            shaped((model, model), BF16),
            shaped((model, model), BF16),
            shaped((model, model), BF16),
            shaped((model, model), BF16),
            shaped((units, model), F32),
            shaped((units, model), F32),
            shaped((16, model), F32),
        ),
        in_specs=anywhere * (4 + len(vectors) + len(weights)),
        out_specs=vmem(9),
        scratch_shapes=scratch,
        compiler_params=pltpu.CompilerParams(collective_id=0, has_side_effects=True, vmem_limit_bytes=62 * 2**20),
        name="layer",
    )(tokens, cotangent, segment_ids, mask_positions, *vectors, *weights)


def on_device(
    rows_total,
    tokens,
    cotangent,
    segment_ids,
    mask_positions,
    query_weight,
    query_bias,
    key_weight,
    value_weight,
    value_bias,
    output_weight,
    output_bias,
    first_gain,
    first_shift,
    up_weight,
    up_bias,
    down_weight,
    down_bias,
    second_gain,
    second_shift,
):
    if rows_total == 8:
        vectors = (up_bias, query_bias, value_bias, output_bias, first_gain, first_shift, down_bias, second_gain, second_shift)
        weights = (query_weight, key_weight, value_weight, output_weight, up_weight, down_weight)
        found = layer_call(
            tokens, cotangent, segment_ids, mask_positions, vectors, weights
        )
        return finish(*found, up_weight.shape[1])
    _, stretch, model = tokens.shape
    hidden = up_weight.shape[1]
    width = model // 2
    heads = HEADS // 2
    masks = mask_positions.shape[2]
    seq = lax.axis_index("seq")
    row = seq // 2
    core = seq % 2
    across = [(i, (i + 2) % 4) for i in range(4)]
    beside = [(i, i + 1 - 2 * (i % 2)) for i in range(4)]

    def swap(value):
        return lax.ppermute(value, "seq", across)

    def trade(value):
        return lax.ppermute(value, "seq", beside)

    def take(array, index):
        return lax.dynamic_index_in_dim(array, index, 0, keepdims=False)

    half = jnp.concatenate([take(tokens, row), swap(take(tokens, 1 - row))], axis=0)
    peer = trade(half)
    cot_half = jnp.concatenate([take(cotangent, row), swap(take(cotangent, 1 - row))], axis=0)
    cot_peer = trade(cot_half)
    blocks = jnp.stack([2 * row + core, 2 * (1 - row) + core, 2 * row + 1 - core, 2 * (1 - row) + 1 - core])
    positions = (blocks[:, None] * stretch + jnp.arange(stretch, dtype=jnp.int32)[None, :]).reshape(-1)
    segments = jnp.take(take(segment_ids, row).reshape(4, stretch), blocks, axis=0).reshape(-1)
    slots = take(mask_positions, row).reshape(-1)
    pos, seg, slot_col = positions[None, :], segments[None, :], slots[:, None]
    pos_col, seg_col, slot_row = positions[:, None], segments[:, None], slots[None, :]
    core_scalar = core.reshape(1).astype(jnp.int32)
    line = lambda value: value.reshape(1, -1)
    full = 4 * stretch
    count = 2 * masks
    shaped = jax.ShapeDtypeStruct

    keys, values, queries, context, probs, picked = local_call(
        project_kernel,
        (
            shaped((full, width), BF16),
            shaped((full, width), BF16),
            shaped((count, width), BF16),
            shaped((count, width), BF16),
            shaped((heads, count, full), F32),
            shaped((count, model), BF16),
        ),
        "project",
    )(core_scalar, half, peer, pos, seg, slot_col, query_weight, line(query_bias), key_weight, value_weight, line(value_bias))

    two = context.reshape(2, masks, width)
    ctx_peer = trade(take(two, 1 - core))
    normed_low, feed, branch_low, grad_h1, small = local_call(
        masked_kernel,
        (
            shaped((masks, model), BF16),
            shaped((masks, model), BF16),
            shaped((masks, model), BF16),
            shaped((masks, model), F32),
            shaped((16, model), F32),
        ),
        "masked",
    )(
        core_scalar, take(two, core), ctx_peer, picked, cot_half, cot_peer, pos, slot_col, output_weight, line(output_bias),
        line(first_gain), line(first_shift), up_weight, line(up_bias), down_weight, line(down_bias), line(second_gain), line(second_shift),
    )
    branch_peer = trade(branch_low)
    grads, igrad_own, igrad_peer, bias = local_call(
        back_kernel,
        (
            shaped((4, model, width), BF16),
            shaped((2 * stretch, model), F32),
            shaped((2 * stretch, model), BF16),
            shaped((2, width), F32),
        ),
        "back",
        [pltpu.VMEM((count, width), BF16), pltpu.VMEM((full, width), BF16), pltpu.VMEM((full, width), BF16)],
    )(
        core_scalar, keys, values, queries, context, probs, picked, branch_low, branch_peer, grad_h1, half, peer, pos_col, slot_row,
        query_weight, key_weight, value_weight, output_weight,
    )
    igrad = igrad_own + trade(igrad_peer).astype(F32)
    igrad_other = swap(igrad[stretch:].astype(BF16)).astype(F32)
    igrad_mine = igrad[:stretch]
    input_grad = jnp.where(row == 0, jnp.stack([igrad_mine, igrad_other]), jnp.stack([igrad_other, igrad_mine]))

    ctx_own, ctx_other = local_call(
        attend_kernel, (shaped((2 * stretch, width), BF16), shaped((2 * stretch, width), BF16)), "attend"
    )(core_scalar, half, peer, seg, seg_col, keys, values, query_weight, line(query_bias))
    out_mine, out_other = local_call(
        feed_kernel, (shaped((stretch, model), BF16), shaped((stretch, model), BF16)), "feed"
    )(
        core_scalar, ctx_own, trade(ctx_other), half, output_weight, line(output_bias), line(first_gain), line(first_shift),
        up_weight, line(up_bias), down_weight, line(down_bias), line(second_gain), line(second_shift),
    )
    out_other = swap(out_other)
    layer_output = jnp.where(row == 0, jnp.stack([out_mine, out_other]), jnp.stack([out_other, out_mine]))

    wide = jnp.zeros((2, model), F32)
    bias_rows = lax.dynamic_update_slice(wide, bias, (0, core * width))
    base = hidden // model + 6
    small = jnp.concatenate([small[:base], bias_rows, small[base + 2 :]], axis=0)

    both = ("rows", "seq")
    small = lax.psum(small, both)
    zero = jnp.zeros((model, model), F32)
    wide_grads = [lax.dynamic_update_slice(zero, grads[k].astype(F32), (0, core * width)) for k in (1, 2, 3)]
    rows_wo = grads[0].reshape(2, width, width).transpose(1, 0, 2).reshape(width, model).astype(F32)
    wide_grads.append(lax.dynamic_update_slice(zero, rows_wo, (core * width, 0)))
    grad_wq, grad_wk, grad_wv, grad_wo = lax.psum(tuple(wide_grads), both)
    pieces = []
    units = hidden // 8
    for part in range(8):
        (piece,) = local_call(hidden_kernel, (shaped((units, 2 * model), BF16),), "hidden")(
            jnp.full((1,), part, jnp.int32), normed_low, feed, up_weight, line(up_bias), down_weight
        )
        pieces.append(piece.astype(F32))
    hidden_grads = lax.psum_scatter(jnp.concatenate(pieces, axis=0), both, scatter_dimension=0, tiled=True)

    up_part, down_part = hidden_grads[:, :model], hidden_grads[:, model:]
    return outputs(layer_output, input_grad, grad_wq, grad_wk, grad_wv, grad_wo, up_part, down_part, small)


def solution(mesh):
    split = P("rows", "seq", None)
    in_specs = (split, split, P("rows", None), P("rows", None, None)) + (P(),) * 15
    out_specs = (split, split) + (P(),) * 9 + (P(None, ("rows", "seq")), P(), P(("rows", "seq"), None), P(), P(), P())
    return jax.shard_map(
        functools.partial(on_device, mesh.shape["rows"]), mesh=mesh, in_specs=in_specs, out_specs=out_specs, check_vma=False
    )
```

```python
import functools

import jax
import jax.numpy as jnp
from jax import lax
from jax.experimental import pallas as pl
from jax.experimental.pallas import tpu as pltpu
from jax.sharding import PartitionSpec as P

HEADS = 12
EPSILON = 1e-12
MASKED_SCORE = -1000000000.0
F32 = jnp.float32
BF16 = jnp.bfloat16
MESH = pl.DeviceIdType.MESH
VMEM_LIMIT = 56 * 2**20
ORDERS = ("xyz", "yxz", "xyz", "xyz")
PLAN = {
    "G0": ("Sr00", "Sr01"),
    "p0": ("Sr10", "Sr11"),
    "p1": ("Sr20", "Sr21"),
    "p2": ("Sr30", "Sr31", "Er00", "Sr02"),
    "dx": ("Ss0", "Er10", "Sr12", "Er01", "Er11", "Er20", "Sr22"),
    "a1": ("Ed", "Si0", "Ef", "Es0", "Ss1", "Er21", "Er02", "Sr03"),
    "a2": ("Er22", "Sr23", "Er30", "Sr32", "EH", "Si1", "Sh0", "Es1", "Ss2", "Ei0", "Er12", "Sr13", "Er03", "Sg03", "Er31", "Er23", "Sg23", "Er32", "Sr33"),
    "a4": ("Sh1",),
    "a5": ("Er13", "Sg13", "Ei1"),
    "a6": ("Es2", "Ss3", "Eg03", "Sg00", "Sg02"),
    "a9": ("Eg23", "Sg20", "Sg22"),
    "a11": ("Er33", "Sg33"),
    "f0": ("Eg00",),
    "f1": ("Eg13", "Sg10", "Sg12", "Eh"),
    "f2": ("Es3", "Eg20", "Eg02", "St00", "Sg01"),
    "f4": ("So0", "Eg22", "St20", "Sg21", "Eg33", "Sg30", "Sg32", "Et00", "Eg12", "St10", "Sg11"),
    "f6": ("Et20", "Eg10", "Eg01", "St01", "Et10"),
    "end": ("Eg21", "St21", "Et01", "Eo0", "So1", "Et21", "Eg30", "Eg32", "St30", "Sg31", "Et30", "Eg11", "St11", "Eg31", "St31", "Et11", "Eo1", "Et31"),
}


def dot(left, right):
    return lax.dot_general(left, right, (((1,), (0,)), ((), ())), preferred_element_type=F32)


def dot_nt(left, right):
    return lax.dot_general(left, right, (((1,), (1,)), ((), ())), preferred_element_type=F32)


def dot_tn(left, right):
    return lax.dot_general(left, right, (((0,), (0,)), ((), ())), preferred_element_type=F32)


def norm_parts(hidden):
    centred = hidden - jnp.mean(hidden, axis=-1, keepdims=True)
    variance = jnp.mean(centred * centred, axis=-1, keepdims=True)
    scale = lax.rsqrt(variance + EPSILON)
    return centred * scale, scale


def norm_back(grad, normed, scale, gain):
    scaled = grad * gain
    along = jnp.mean(scaled * normed, axis=-1, keepdims=True)
    return (scaled - jnp.mean(scaled, axis=-1, keepdims=True) - normed * along) * scale


GELU_A = 0.7978845608028654
GELU_B = 0.044715


def gelu_parts(value):
    square = value * value
    bent = jnp.tanh(GELU_A * value * (1.0 + GELU_B * square))
    half = 0.5 * (1.0 + bent)
    slope = half + 0.5 * value * (1.0 - bent * bent) * (GELU_A * (1.0 + 3.0 * GELU_B * square))
    return value * half, slope


def gelu_only(value):
    bent = jnp.tanh(GELU_A * value * (1.0 + GELU_B * value * value))
    return 0.5 * value * (1.0 + bent)


def lane_is(shape, low, high):
    lane = lax.broadcasted_iota(jnp.int32, shape, len(shape) - 1)
    return (lane >= low) & (lane < high)


def project_kernel(core, half, peer, pos, seg, slots, wq, bq, wk, wv, bv, keys, values, queries, context, probs, picked):
    width = keys.shape[1]
    mine = pl.ds(pl.multiple_of(core[0] * width, 128), width)
    count = slots.shape[0]
    tokens_half = half.shape[0]
    chosen = jnp.where(slots[...] == pos[...], 1.0, 0.0).astype(BF16)
    rows = dot(chosen[:, :tokens_half], half[...]) + dot(chosen[:, tokens_half:], peer[...])
    rows = rows.astype(BF16)
    picked[...] = rows
    queries[...] = (dot(rows, wq[:, mine]) + bq[:, mine]).astype(BF16)
    for place, part in ((0, half), (tokens_half, peer)):
        for start in range(0, tokens_half, 256):
            block = part[start : start + 256, :]
            there = slice(place + start, place + start + 256)
            keys[there, :] = dot(block, wk[:, mine]).astype(BF16)
            values[there, :] = (dot(block, wv[:, mine]) + bv[:, mine]).astype(BF16)
    sequence = lax.broadcasted_iota(jnp.int32, (count, 1), 0) // (count // 2)
    same = seg[...] == sequence
    for pair in range(width // 128):
        lanes = slice(pair * 128, pair * 128 + 128)
        pair_queries = queries[:, lanes].astype(F32) * 0.125
        pair_keys, pair_values = keys[:, lanes], values[:, lanes]
        outs = []
        for side in range(2):
            keep = lane_is((count, 128), side * 64, side * 64 + 64)
            head_queries = jnp.where(keep, pair_queries, 0.0).astype(BF16)
            scores = jnp.where(same, dot_nt(head_queries, pair_keys), MASKED_SCORE)
            weights = jnp.exp(scores - jnp.max(scores, axis=-1, keepdims=True))
            share = weights / jnp.sum(weights, axis=-1, keepdims=True)
            probs[pair * 2 + side] = share
            outs.append(dot(share.astype(BF16), pair_values))
        first = lane_is((count, 128), 0, 64)
        context[:, lanes] = jnp.where(first, outs[0], outs[1]).astype(BF16)


def masked_kernel(core, ctx_own, ctx_peer, picked, cot_half, cot_peer, pos, slots, wo, bo, g1, s1, wup, bup, wdown, bdown, g2, s2, normed_low, feed, branch_low, grad_h1, small):
    count, width = ctx_own.shape
    hidden = wup.shape[1]
    model = wup.shape[0]
    tokens_half = cot_half.shape[0]
    mine = pl.multiple_of(core[0] * count, 16)
    is_first = core[0] == 0
    left = jnp.where(is_first, ctx_own[...], ctx_peer[...])
    right = jnp.where(is_first, ctx_peer[...], ctx_own[...])
    branch = dot(left, wo[:width, :]) + dot(right, wo[width:, :]) + bo[...]
    h1 = picked[pl.ds(mine, count), :].astype(F32) + branch
    n1, r1 = norm_parts(h1)
    y1 = n1 * g1[...] + s1[...]
    y1_low = y1.astype(BF16)
    normed_low[...] = y1_low
    total = y1 + bdown[...]
    slopes = []
    step = model
    for start in range(0, hidden, step):
        pre = dot(y1_low, wup[:, start : start + step]) + bup[:, start : start + step]
        act, slope = gelu_parts(pre)
        slopes.append(slope)
        total = total + dot(act.astype(BF16), wdown[start : start + step, :])
    n2, r2 = norm_parts(total)
    chosen = jnp.where(slots[pl.ds(mine, count), :] == pos[...], 1.0, 0.0).astype(BF16)
    grad = dot(chosen[:, :tokens_half], cot_half[...]) + dot(chosen[:, tokens_half:], cot_peer[...])
    gh2 = norm_back(grad, n2, r2, g2[...])
    gf = gh2.astype(BF16)
    feed[...] = gf
    gy1 = gh2
    small[...] = jnp.zeros_like(small)
    for place, start in enumerate(range(0, hidden, step)):
        ga = dot_nt(gf, wdown[start : start + step, :])
        gp = (ga * slopes[place]).astype(BF16)
        small[place : place + 1, :] = jnp.sum(gp.astype(F32), axis=0, keepdims=True)
        gy1 = gy1 + dot_nt(gp, wup[:, start : start + step])
    gh1 = norm_back(gy1, n1, r1, g1[...])
    grad_h1[...] = gh1
    gb = gh1.astype(BF16)
    branch_low[...] = gb
    base = hidden // step
    for place, value in enumerate((gy1 * n1, gy1, grad * n2, grad, gb.astype(F32), gf.astype(F32))):
        small[base + place : base + place + 1, :] = jnp.sum(value, axis=0, keepdims=True)


def back_kernel(core, keys, values, queries, context, probs, picked, gb_own, gb_peer, gh1, half, peer, pos_col, slots_row, wq, wk, wv, wo, grads, igrad_own, igrad_peer, bias, dq_low, dk_low, dv_low):
    width = keys.shape[1]
    count = queries.shape[0]
    own = gb_own.shape[0]
    tokens_half = half.shape[0]
    is_first = core[0] == 0
    mine = pl.ds(pl.multiple_of(core[0] * width, 128), width)
    mine_rows = pl.ds(pl.multiple_of(core[0] * width, 128), width)
    top = jnp.where(is_first, gb_own[...], gb_peer[...])
    low = jnp.where(is_first, gb_peer[...], gb_own[...])
    gb = jnp.concatenate([top, low], axis=0)
    gctx = dot_nt(gb, wo[mine_rows, :]).astype(BF16)
    for pair in range(width // 128):
        lanes = slice(pair * 128, pair * 128 + 128)
        pair_keys, pair_values, pair_queries = keys[:, lanes], values[:, lanes], queries[:, lanes]
        pair_gctx = gctx[:, lanes]
        dqs, dks, dvs = [], [], []
        for side in range(2):
            keep = lane_is((count, 128), side * 64, side * 64 + 64)
            head_gctx = jnp.where(keep, pair_gctx.astype(F32), 0.0).astype(BF16)
            share = probs[pair * 2 + side]
            gp = dot_nt(head_gctx, pair_values)
            spread = jnp.sum(share * gp, axis=-1, keepdims=True)
            gs = (share * (gp - spread)).astype(BF16)
            dqs.append(dot(gs, pair_keys))
            dks.append(dot_tn(gs, pair_queries))
            dvs.append(dot_tn(share.astype(BF16), pair_gctx))
        first = lane_is((count, 128), 0, 64)
        dq_low[:, lanes] = (jnp.where(first, dqs[0], dqs[1]) * 0.125).astype(BF16)
        first = lane_is((2 * tokens_half, 128), 0, 64)
        dk_low[:, lanes] = (jnp.where(first, dks[0], dks[1]) * 0.125).astype(BF16)
        dv_low[:, lanes] = jnp.where(first, dvs[0], dvs[1]).astype(BF16)
    grads[1] = dot_tn(picked[...], dq_low[...]).astype(BF16)
    gwo = dot_tn(context[...], gb).astype(BF16)
    grads[0, :width, :] = gwo[:, :width]
    grads[0, width:, :] = gwo[:, width:]
    for place, part in ((2, dk_low), (3, dv_low)):
        total = dot_tn(half[...], part[:tokens_half, :]) + dot_tn(peer[...], part[tokens_half:, :])
        grads[place] = total.astype(BF16)
    bias[0:1, :] = jnp.sum(dq_low[...].astype(F32), axis=0, keepdims=True)
    bias[1:2, :] = jnp.sum(dv_low[...].astype(F32), axis=0, keepdims=True)
    spread_rows = dot_nt(dq_low[...], wq[:, mine])
    zero = jnp.zeros((own, wq.shape[0]), F32)
    spread_rows = spread_rows + jnp.concatenate(
        [jnp.where(is_first, gh1[...], zero), jnp.where(is_first, zero, gh1[...])], axis=0
    )
    high = spread_rows.astype(BF16)
    rest = (spread_rows - high.astype(F32)).astype(BF16)
    for start in range(0, 2 * tokens_half, 256):
        here = slice(start, start + 256)
        chosen = jnp.where(pos_col[here, :] == slots_row[...], 1.0, 0.0).astype(BF16)
        total = dot(chosen, high) + dot(chosen, rest)
        total = total + dot_nt(dk_low[here, :], wk[:, mine]) + dot_nt(dv_low[here, :], wv[:, mine])
        if start < tokens_half:
            igrad_own[here, :] = total
        else:
            igrad_peer[start - tokens_half : start - tokens_half + 256, :] = total.astype(BF16)


def attend_kernel(core, half, peer, seg, seg_col, keys, values, wq, bq, own, other):
    width = keys.shape[1]
    mine = pl.ds(pl.multiple_of(core[0] * width, 128), width)
    tile = 256
    for part, out in ((half, own), (peer, other)):
        place = 0 if part is half else half.shape[0]

        def body(step, carry, part=part, out=out, place=place):
            here = pl.ds(pl.multiple_of(step * tile, tile), tile)
            queries = (dot(part[here, :], wq[:, mine]) + bq[:, mine]).astype(BF16).astype(F32) * 0.125
            same = seg_col[pl.ds(pl.multiple_of(place + step * tile, tile), tile), :] == seg[...]
            for pair in range(width // 128):
                lanes = slice(pair * 128, pair * 128 + 128)
                outs = []
                for side in range(2):
                    keep = lane_is((tile, 128), side * 64, side * 64 + 64)
                    head_queries = jnp.where(keep, queries[:, lanes], 0.0).astype(BF16)
                    scores = jnp.where(same, dot_nt(head_queries, keys[:, lanes]), MASKED_SCORE)
                    weights = jnp.exp(scores - jnp.max(scores, axis=-1, keepdims=True))
                    total = jnp.sum(weights, axis=-1, keepdims=True)
                    outs.append(dot(weights.astype(BF16), values[:, lanes]) / total)
                first = lane_is((tile, 128), 0, 64)
                out[here, lanes] = jnp.where(first, outs[0], outs[1]).astype(BF16)
            return carry

        lax.fori_loop(0, part.shape[0] // tile, body, 0)


def feed_kernel(core, ctx_own, ctx_peer, half, wo, bo, g1, s1, wup, bup, wdown, bdown, g2, s2, own, other):
    width = ctx_own.shape[1]
    hidden, model = wdown.shape
    is_first = core[0] == 0
    tile = own.shape[0]
    for start, out in ((0, own), (tile, other)):
        here = slice(start, start + tile)
        left = jnp.where(is_first, ctx_own[here, :], ctx_peer[here, :])
        right = jnp.where(is_first, ctx_peer[here, :], ctx_own[here, :])
        branch = dot(left, wo[:width, :]) + dot(right, wo[width:, :]) + bo[...]
        n1, _ = norm_parts(half[here, :].astype(F32) + branch)
        y1 = n1 * g1[...] + s1[...]
        y1_low = y1.astype(BF16)
        total = y1 + bdown[...]
        for place in range(0, hidden, model):
            pre = dot(y1_low, wup[:, place : place + model]) + bup[:, place : place + model]
            total = total + dot(gelu_only(pre).astype(BF16), wdown[place : place + model, :])
        n2, _ = norm_parts(total)
        out[...] = (n2 * g2[...] + s2[...]).astype(BF16)


def hidden_kernel(slot, normed, feed, wup, bup, wdown, out):
    units = out.shape[0]
    model = normed.shape[1]
    mine = pl.ds(pl.multiple_of(slot[0] * units, 128), units)
    pre = dot(normed[...], wup[:, mine]) + bup[:, mine]
    act, slope = gelu_parts(pre)
    ga = dot_nt(feed[...], wdown[mine, :])
    gp = (ga * slope).astype(BF16)
    out[:, :model] = dot_tn(gp, normed[...]).astype(BF16)
    out[:, model:] = dot_tn(act.astype(BF16), feed[...]).astype(BF16)


def place_here():
    row, seq = lax.axis_index("rows"), lax.axis_index("seq")
    return row // 2, row % 2, seq // 2, seq % 2


def device(z, x, y, core):
    return (z * 2 + x, y * 2 + core)


def layer_kernel(
    tokens, cotangent, segments_in, slots_in, up_bias_in, bq_in, bv_in, bo_in, g1_in, s1_in, bdown_in, g2_in, s2_in, wq, wk, wv, wo, wup, wdown,
    layer_hbm, igrad_hbm, hbm_o, hbm_0, hbm_1, hbm_2, up_hbm, down_hbm, small_hbm,
    layer_out, input_grad, out_o, out_0, out_1, out_2, up_out, down_out, small_out,
    segments, slots, up_bias, bq, bv, bo, g1, s1, bdown, g2, s2, vecs, wq_t, wkv_t, wo_t, keys_t, values_t,
    xs, xs_t, cots, cot_part, cot_in, cot_sum, cot_far, dx_send, dx_in, wq_v, wk_v, wv_v, wo_v, wup_v, wdown_v, keys, values, queries, context, probs, picked, chosen, ctx_both, gb_both,
    slopes, dq_low, dkv_low, grads, hidden_grads, hidden_in, fac_normed, fac_feed, grad_h1, small_in, small_z,
    all_queries, all_context, ctx_in, total, y1_keep, out_send, igrad_send, igrad_in,
    in_o, in_0, in_1, in_2, local_sem, send_sem, recv_sem,
):
    z, x, y, core = place_here()
    row = y
    stretch, model = tokens.shape[1:]
    half = 2 * stretch
    full = 2 * half
    width = wq_v.shape[1]
    masks = slots.shape[2]
    count = 2 * masks
    hidden = wup.shape[1]
    parts = hidden // model
    units = down_out.shape[0]
    others = [(z + k) % 4 for k in (1, 2, 3)]
    at_y, at_x, twin = device(z, x, 1 - y, core), device(z, 1 - x, y, core), device(z, x, y, 1 - core)
    columns = [device(o, x, y, core) for o in others]
    mine = pl.ds(pl.multiple_of(core * width, 128), width)
    my_slots = pl.ds(pl.multiple_of(core * masks, 16), masks)
    twin_slots = pl.ds(pl.multiple_of((1 - core) * masks, 16), masks)
    pending = []

    def local(src, dst, index):
        copy = pltpu.make_async_copy(src, dst, local_sem.at[index])
        copy.start()
        return copy

    def remote(src, dst, index, target):
        return pltpu.make_async_remote_copy(
            src_ref=src, dst_ref=dst, send_sem=send_sem.at[index], recv_sem=recv_sem.at[index],
            device_id=target, device_id_type=MESH,
        )

    def push(src, dst, index, target):
        copy = remote(src, dst, index, target)
        copy.start()
        pending.append(copy)
        return copy

    def vector(index):
        return vecs[index : index + 1, :]

    def half_vector(index):
        return vecs[index : index + 1, mine]

    small_pairs = (
        (segments_in, segments), (slots_in, slots), (up_bias_in, up_bias), (bq_in, bq), (bv_in, bv), (bo_in, bo), (g1_in, g1),
        (s1_in, s1), (bdown_in, bdown), (g2_in, g2), (s2_in, s2),
    )
    own_tokens = local(tokens.at[row], xs.at[pl.ds(0, stretch)], 0)
    get_wk = local(wk.at[:, mine], wk_v, 1)
    get_wv = local(wv.at[:, mine], wv_v, 2)
    get_small = [local(src, dst, 8 + k) for k, (src, dst) in enumerate(small_pairs)]
    get_wq = local(wq.at[:, mine], wq_v, 3)
    own_cot = local(cotangent, cots, 4)
    get_wo = local(wo, wo_v, 5)
    get_up = local(wup, wup_v, 6)
    get_down = local(wdown, wdown_v, 7)

    near = [(1 - x, y), (x, 1 - y), (1 - x, 1 - y)]
    greeted = [twin] + columns + [device(z, nx, ny, c) for nx, ny in near for c in range(2)]
    barrier = pltpu.get_barrier_semaphore()
    for target in greeted:
        pl.semaphore_signal(barrier, inc=1, device_id=target, device_id_type=MESH)
    pl.semaphore_wait(barrier, len(greeted))

    piece = stretch // 2
    tok_y = [
        push(tokens.at[1 - row, pl.ds(k * piece, piece)], xs.at[pl.ds(stretch + k * piece, piece)], k, at_y) for k in range(2)
    ]
    tok_c = push(tokens.at[row], xs.at[pl.ds(half, stretch)], 2, twin)

    for copy in get_small:
        copy.wait()
    for part in range(parts):
        vecs[part : part + 1, :] = up_bias[part * model : (part + 1) * model].reshape(1, model)
    for place, value in enumerate((bq, bv, bo, g1, s1, bdown, g2, s2)):
        vecs[parts + place : parts + place + 1, :] = value[...].reshape(1, model)

    def key_values(start):
        here = pl.ds(start, stretch)
        block = xs[here, :]
        block_keys = dot(block, wk_v[...]).astype(BF16)
        block_values = (dot(block, wv_v[...]) + half_vector(5)).astype(BF16)
        keys[here, :] = block_keys
        values[here, :] = block_values
        xs_t[:, here] = block.T
        keys_t[:, here] = block_keys.T
        values_t[:, here] = block_values.T

    blocks = [2 * y + core, 2 * (1 - y) + core, 2 * y + 1 - core, 2 * (1 - y) + 1 - core]
    lane = lax.broadcasted_iota(jnp.int32, (1, stretch), 1)
    pos_row = jnp.concatenate([lane + block * stretch for block in blocks], axis=1)
    seg_here = segments[pl.ds(row, 1), :]
    split = jnp.sum((1 - seg_here).astype(F32), axis=1, keepdims=True)
    pos_row = pos_row.astype(F32)
    seg_row = jnp.where(pos_row >= split, 1.0, 0.0)
    diagonal = lax.broadcasted_iota(jnp.int32, (masks, masks), 0) == lax.broadcasted_iota(jnp.int32, (masks, masks), 1)

    def slot_column(which, sequence):
        line = slots[which].astype(F32)[sequence : sequence + 1, :]
        return jnp.sum(jnp.where(diagonal, line, 0.0), axis=1, keepdims=True)

    for sequence in range(2):
        column = slot_column(row, sequence)
        chosen[sequence * masks : (sequence + 1) * masks, :] = jnp.where(column == pos_row, 1.0, 0.0).astype(BF16)
    own_cot.wait()
    for sequence in range(2):
        here = chosen[sequence * masks : (sequence + 1) * masks, :stretch]
        cot_part[0, sequence] = dot(here, cots[row]).astype(BF16)
        there = jnp.where(slot_column(1 - row, sequence) == pos_row[:, :stretch], 1.0, 0.0).astype(BF16)
        cot_part[1, sequence] = dot(there, cots[1 - row]).astype(BF16)
    cot_c = push(cot_part.at[:, 1 - core], cot_in, 4, twin)

    own_tokens.wait()
    get_wk.wait()
    get_wv.wait()
    key_values(0)
    tok_c.wait_recv()
    key_values(half)
    get_wq.wait()
    for pair in range(width // 128):
        lanes = slice(pair * 128, pair * 128 + 128)
        wkv_t[pair * 256 : pair * 256 + 128, :] = wk_v[:, lanes].T
        wkv_t[pair * 256 + 128 : pair * 256 + 256, :] = wv_v[:, lanes].T
    wq_t[...] = wq_v[...].T
    forward = []
    for k in range(2):
        tok_y[k].wait_recv()
        src = xs.at[pl.ds(stretch + k * piece, piece)]
        forward.append(push(src, xs.at[pl.ds(half + stretch + k * piece, piece)], 5 + k, twin))
    cot_c.wait_recv()
    cot_sum[...] = cot_part[:, core] + cot_in[...]
    cot_y = push(cot_sum.at[1], cot_far, 3, at_y)
    key_values(stretch)
    for copy in forward:
        copy.wait_recv()
    key_values(half + stretch)

    rows = dot(chosen[...], xs[...]).astype(BF16)
    picked[...] = rows
    queries[...] = (dot(rows, wq_v[...]) + half_vector(4)).astype(BF16)
    sequence = lax.broadcasted_iota(jnp.int32, (count, 1), 0) // masks
    same = seg_row == sequence.astype(F32)
    pairs = width // 128
    for pair in range(pairs):
        lanes = slice(pair * 128, pair * 128 + 128)
        pair_queries = queries[:, lanes].astype(F32) * 0.125
        pair_keys, pair_values = keys_t[lanes, :], values[:, lanes]
        outs = []
        for side in range(2):
            keep = lane_is((count, 128), side * 64, side * 64 + 64)
            head_queries = jnp.where(keep, pair_queries, 0.0).astype(BF16)
            scores = jnp.where(same, dot(head_queries, pair_keys), MASKED_SCORE)
            weights = jnp.exp(scores - jnp.max(scores, axis=-1, keepdims=True))
            share = weights / jnp.sum(weights, axis=-1, keepdims=True)
            share = share.astype(BF16)
            probs[pair * 2 + side] = share
            outs.append(dot(share, pair_values))
        first = lane_is((count, 128), 0, 64)
        context[:, lanes] = jnp.where(first, outs[0], outs[1]).astype(BF16)
    ctx_both[core] = context[my_slots, :]
    ctx_c = push(context.at[twin_slots], ctx_both.at[core], 7, twin)

    for start in range(0, full, stretch):
        value = (dot(xs[start : start + stretch, :], wq_v[...]) + half_vector(4)).astype(BF16)
        all_queries[start : start + stretch, :] = (value.astype(F32) * 0.125).astype(BF16)
    get_wo.wait()
    wo_t[...] = wo_v[mine, :].T
    ctx_c.wait_recv()

    branch = dot(ctx_both[0], wo_v[:width, :]) + dot(ctx_both[1], wo_v[width:, :]) + vector(6)
    n1, r1 = norm_parts(picked[my_slots, :].astype(F32) + branch)
    y1 = n1 * vector(7) + vector(8)
    y1_low = y1.astype(BF16)
    fac_normed[core, z] = y1_low
    spot = fac_normed.at[core, z]
    norm_z = [push(spot, spot, 9 + k, columns[k]) for k in range(3)]
    get_up.wait()
    get_down.wait()
    sum2 = y1 + vector(9)
    for part in range(parts):
        there = slice(part * model, (part + 1) * model)
        act, slope = gelu_parts(dot(y1_low, wup_v[:, there]) + vector(part))
        slopes[part] = slope
        sum2 = sum2 + dot(act.astype(BF16), wdown_v[there, :])
    n2, r2 = norm_parts(sum2)
    cot_y.wait_recv()
    grad = cot_sum[0].astype(F32) + cot_far[...].astype(F32)
    gh2 = norm_back(grad, n2, r2, vector(10))
    gf = gh2.astype(BF16)
    fac_feed[core, z] = gf
    spot = fac_feed.at[core, z]
    feed_z = [push(spot, spot, 12 + k, columns[k]) for k in range(3)]
    gf_t = gf.T
    gy1_t = jnp.zeros((model, masks), F32)
    small_in[0] = jnp.zeros(small_in.shape[1:], F32)
    for part in range(parts):
        there = slice(part * model, (part + 1) * model)
        gp = (dot(wdown_v[there, :], gf_t).T * slopes[part]).astype(BF16)
        small_in[0, part : part + 1, :] = jnp.sum(gp.astype(F32), axis=0, keepdims=True)
        gy1_t = gy1_t + dot(wup_v[:, there], gp.T)
    gy1 = gh2 + gy1_t.T
    gh1 = norm_back(gy1, n1, r1, vector(7))
    grad_h1[...] = gh1
    gb = gh1.astype(BF16)
    gb_both[core] = gb
    gb_c = push(gb_both.at[core], gb_both.at[core], 15, twin)
    for place, value in enumerate((gy1 * n1, gy1, grad * n2, grad, gb.astype(F32), gf.astype(F32))):
        small_in[0, parts + place : parts + place + 1, :] = jnp.sum(value, axis=0, keepdims=True)
    gb_c.wait_recv()

    spots = {"x": x, "y": y}
    neighbours = {"x": at_x, "y": at_y}
    ins = [in_o, in_0, in_1, in_2]
    outs = [out_o, out_0, out_1, out_2]
    half_rows, quarter, chunk = model // 2, model // 4, model // 16

    def rows_of(job):
        p1, p2 = (spots[dim] for dim in ORDERS[job][:2])
        kept, gone = p1 * half_rows, (1 - p1) * half_rows
        return kept, kept + p2 * quarter, kept + (1 - p2) * quarter, kept + p2 * quarter + z * chunk, gone + (1 - p2) * quarter, gone + p2 * quarter

    def at(start, size):
        return pl.ds(pl.multiple_of(start, 16), size)

    def job_copies(kind, job, stage):
        first, second = (neighbours[dim] for dim in ORDERS[job][:2])
        kept, mine_at, pass_at, own, gone_pass, gone_keep = rows_of(job)
        source, arrive, out = grads.at[job], ins[job], outs[job]
        base = 40 + job * 16

        def spread(start, size, index, target):
            spot = out.at[at(start, size), mine]
            return remote(spot, spot, base + index, target)

        if kind == "r" and stage == 0:
            return [remote(source.at[at(gone_pass, quarter)], arrive.at[pl.ds(0, quarter)], base, first)]
        if kind == "r" and stage == 1:
            return [remote(source.at[at(gone_keep, quarter)], arrive.at[pl.ds(quarter, quarter)], base + 1, first)]
        if kind == "r" and stage == 2:
            return [remote(source.at[at(pass_at, quarter)], arrive.at[pl.ds(2 * quarter, quarter)], base + 2, second)]
        if kind == "r":
            return [
                remote(
                    source.at[at(mine_at + others[k] * chunk, chunk)], arrive.at[pl.ds(3 * quarter + k * chunk, chunk)], base + 3 + k, columns[k]
                )
                for k in range(3)
            ]
        if kind == "g" and stage == 3:
            return [spread(own, chunk, 6 + k, columns[k]) for k in range(3)]
        if kind == "g" and stage == 2:
            return [spread(mine_at, quarter, 9, second)]
        if kind == "g" and stage == 0:
            return [spread(mine_at, quarter, 10, first)]
        if kind == "g":
            return [spread(pass_at, quarter, 11, first)]
        return [spread(kept if stage == 0 else half_rows - kept, half_rows, 12 + stage, twin)]

    def job_start(kind, job, stage):
        for copy in job_copies(kind, job, stage):
            copy.start()

    def job_end(kind, job, stage):
        for copy in job_copies(kind, job, stage):
            copy.wait()
        if kind != "r":
            return
        _, mine_at, pass_at, own, _, _ = rows_of(job)
        arrive = ins[job]
        if stage == 0:
            here = at(pass_at, quarter)
            grads[job, here] = (grads[job, here].astype(F32) + arrive[:quarter].astype(F32)).astype(BF16)
        elif stage == 2:
            here = at(mine_at, quarter)
            value = grads[job, here].astype(F32) + arrive[quarter : 2 * quarter].astype(F32)
            grads[job, here] = (value + arrive[2 * quarter : 3 * quarter].astype(F32)).astype(BF16)
        elif stage == 3:
            value = grads[job, at(own, chunk)].astype(F32)
            for k in range(3):
                value = value + arrive[3 * quarter + k * chunk : 3 * quarter + (k + 1) * chunk].astype(F32)
            outs[job][at(own, chunk), mine] = value.astype(BF16)

    def small_copies(stage):
        if stage < 3:
            target = (twin, at_y, at_x)[stage]
            return [remote(small_in.at[2 * stage], small_in.at[2 * stage + 1], 16 + stage, target)]
        return [remote(small_in.at[6], small_z.at[z], 19 + k, target) for k, target in enumerate(columns)]

    def small_start(stage):
        for copy in small_copies(stage):
            copy.start()

    def small_end(stage):
        for copy in small_copies(stage):
            copy.wait()
        if stage < 3:
            small_in[2 * stage + 2] = small_in[2 * stage] + small_in[2 * stage + 1]
            if stage == 2:
                small_z[z] = small_in[6]
        else:
            small_out[...] = (small_z[0] + small_z[1]) + (small_z[2] + small_z[3])

    source = x * 2 + y

    def factor_copies():
        return [remote(ref.at[core], ref.at[core], 22 + k, twin) for k, ref in enumerate((fac_normed, fac_feed))]

    def factors_on():
        for copy in norm_z + feed_z:
            copy.wait_recv()
        for copy in factor_copies():
            copy.start()

    def is_me(cy, cc):
        return (core == x) & (cy == y) & (cc == core)

    def hidden_copy(cy, cc):
        part = hidden_grads.at[pl.ds((cy * 2 + cc) * units, units)]
        return pltpu.make_async_remote_copy(
            src_ref=part, dst_ref=hidden_in.at[source], send_sem=send_sem.at[24 + cy * 2 + cc], recv_sem=recv_sem.at[24 + source],
            device_id=device(z, core, cy, cc), device_id_type=MESH,
        )

    def hidden_make():
        for copy in factor_copies():
            copy.wait()
        slot = z * 2 + core
        size = hidden_grads.shape[0]
        normed = fac_normed[...].reshape(8 * masks, model)
        feed = fac_feed[...].reshape(8 * masks, model)
        at = pl.ds(pl.multiple_of(slot * size, 128), size)
        act, slope = gelu_parts(dot(normed, wup_v[:, at]) + vecs[pl.ds(z, 1), mine])
        gp = (dot_nt(feed, wdown_v[at, :]) * slope).astype(BF16)
        hidden_grads[:, :model] = dot_tn(gp, normed).astype(BF16)
        hidden_grads[:, model:] = dot_tn(act.astype(BF16), feed).astype(BF16)
        for cy in range(2):
            for cc in range(2):
                @pl.when(is_me(cy, cc))
                def _(cy=cy, cc=cc):
                    hidden_in[source] = hidden_grads[pl.ds((cy * 2 + cc) * units, units)]

    def hidden_start(cc):
        for cy in range(2):
            @pl.when(jnp.logical_not(is_me(cy, cc)))
            def _(cy=cy):
                hidden_copy(cy, cc).start()

    def hidden_end():
        for cy in range(2):
            for cc in range(2):
                @pl.when(jnp.logical_not(is_me(cy, cc)))
                def _(cy=cy, cc=cc):
                    hidden_copy(cy, cc).wait_send()
        for cx in range(2):
            for cy in range(2):
                @pl.when(jnp.logical_not((cx == x) & (cy == y) & (core == x)))
                def _(cx=cx, cy=cy):
                    slot = hidden_in.at[cx * 2 + cy]
                    pltpu.make_async_remote_copy(
                        src_ref=slot, dst_ref=slot, send_sem=send_sem.at[24], recv_sem=recv_sem.at[24 + cx * 2 + cy],
                        device_id=twin, device_id_type=MESH,
                    ).wait_recv()
        value = hidden_in[0].astype(F32)
        for k in range(1, 4):
            value = value + hidden_in[k].astype(F32)
        up_out[...] = value[:, :model]
        down_out[...] = value[:, model:]

    def piece_of(index):
        return pl.ds(index * piece, piece)

    def igrad_copy(index):
        return remote(igrad_send.at[piece_of(index)], igrad_in.at[piece_of(index)], 29 + index, at_y)

    def igrad_step():
        remote(dx_send, dx_in, 28, twin).wait_recv()
        input_grad[row] = input_grad[row] + dx_in[:stretch, :].astype(F32)
        igrad_send[...] = (input_grad[1 - row] + dx_in[stretch:, :].astype(F32)).astype(BF16)

    def igrad_end(index):
        igrad_copy(index).wait()
        input_grad[1 - row, piece_of(index)] = igrad_in[piece_of(index), :].astype(F32)

    def out_copy(index):
        return remote(out_send.at[piece_of(index)], layer_out.at[row, piece_of(index)], 32 + index, at_y)

    results = [
        (layer_out, layer_hbm), (input_grad, igrad_hbm), (out_o, hbm_o), (out_0, hbm_0), (out_1, hbm_1), (out_2, hbm_2),
        (up_out, up_hbm), (down_out, down_hbm), (small_out, small_hbm),
    ]

    def result_copy(index):
        src, dst = results[index]
        return pltpu.make_async_copy(src, dst, local_sem.at[20 + index])

    ended = []

    def act(name):
        start, kind, rest = name[0] == "S", name[1], [int(c) for c in name[2:]]
        ended.append(name)
        if kind in "rgt":
            (job_start if start else job_end)(kind, *rest)
            if kind == "t" and not start and {"Et%d0" % rest[0], "Et%d1" % rest[0]} <= set(ended):
                result_copy(2 + rest[0]).start()
        elif kind == "s":
            (small_start if start else small_end)(*rest)
            if not start and rest[0] == 3:
                result_copy(8).start()
        elif kind == "d":
            igrad_step()
        elif kind == "i":
            if start:
                igrad_copy(*rest).start()
            else:
                igrad_end(*rest)
                if {"Ei0", "Ei1"} <= set(ended):
                    result_copy(1).start()
        elif kind == "o":
            if start:
                out_copy(*rest).start()
            else:
                out_copy(*rest).wait()
                if {"Eo0", "Eo1"} <= set(ended):
                    result_copy(0).start()
        elif kind == "f":
            factors_on()
        elif kind == "H":
            hidden_make()
        elif kind == "h" and start:
            hidden_start(*rest)
        elif kind == "h":
            hidden_end()
            result_copy(6).start()
            result_copy(7).start()

    def act_on(name):
        for each in PLAN.get(name, ()):
            act(each)

    gb = gb_both[...].reshape(count, model)
    gctx = dot(gb, wo_t[...]).astype(BF16)
    grads[0] = dot_tn(gb, context[...]).astype(BF16)
    act_on("G0")
    for pair in range(pairs):
        lanes = slice(pair * 128, pair * 128 + 128)
        pair_keys, pair_values, pair_queries = keys[:, lanes], values_t[lanes, :], queries[:, lanes]
        pair_gctx = gctx[:, lanes]
        dqs, dks, dvs = [], [], []
        for side in range(2):
            keep = lane_is((count, 128), side * 64, side * 64 + 64)
            head_gctx = jnp.where(keep, pair_gctx.astype(F32), 0.0).astype(BF16)
            low_share = probs[pair * 2 + side]
            share = low_share.astype(F32)
            gp = dot(head_gctx, pair_values)
            spread = jnp.sum(share * gp, axis=-1, keepdims=True)
            gs = (share * (gp - spread)).astype(BF16)
            dqs.append(dot(gs, pair_keys))
            dks.append(dot_tn(gs, pair_queries))
            dvs.append(dot_tn(low_share, pair_gctx))
        first = lane_is((count, 128), 0, 64)
        dq = (jnp.where(first, dqs[0], dqs[1]) * 0.125).astype(BF16)
        dq_low[:, lanes] = dq
        first = lane_is((full, 128), 0, 64)
        dk = (jnp.where(first, dks[0], dks[1]) * 0.125).astype(BF16)
        dv = jnp.where(first, dvs[0], dvs[1]).astype(BF16)
        both = slice(pair * 256, pair * 256 + 256)
        dkv_low[:, pair * 256 : pair * 256 + 128] = dk
        dkv_low[:, pair * 256 + 128 : pair * 256 + 256] = dv
        grads[1 + pair, :, :128] = dot_tn(picked[...], dq).astype(BF16)
        grads[1 + pair, :, 128:] = dot(xs_t[...], dkv_low[:, both]).astype(BF16)
        act_on("p" + str(pair))
        there = pl.ds(pl.multiple_of(core * width + pair * 128, 128), 128)
        small_in[0, parts + 6 : parts + 7, there] = jnp.sum(dq.astype(F32), axis=0, keepdims=True)
        small_in[0, parts + 7 : parts + 8, there] = jnp.sum(dv.astype(F32), axis=0, keepdims=True)

    spread_rows = dot(dq_low[...], wq_t[...])
    zero = jnp.zeros((masks, model), F32)
    is_first = core == 0
    gh1 = grad_h1[...]
    spread_rows = spread_rows + jnp.concatenate([jnp.where(is_first, gh1, zero), jnp.where(is_first, zero, gh1)], axis=0)
    high = spread_rows.astype(BF16)
    rest = (spread_rows - high.astype(F32)).astype(BF16)
    for start in (half, half + stretch, 0, stretch):
        here = slice(start, start + stretch)
        value = dot_tn(chosen[:, here], high) + dot_tn(chosen[:, here], rest)
        value = value + dot(dkv_low[here, :], wkv_t[...])
        if start < half:
            input_grad[row if start == 0 else 1 - row] = value
        else:
            dx_send[start - half : start - half + stretch, :] = value.astype(BF16)
            if start > half:
                push(dx_send, dx_in, 28, twin)

    act_on("dx")

    def hooks(step, prefix, count):
        for at in range(count):
            if prefix + str(at) in PLAN:
                @pl.when(step == at)
                def _(at=at):
                    act_on(prefix + str(at))

    def ctx_copy():
        return remote(all_context.at[pl.ds(half, half)], ctx_in, 31, twin)

    def attend_step(step, carry):
        tile, pair = (step // pairs + 2) % 4, step % pairs
        here = pl.ds(pl.multiple_of(tile * stretch, stretch), stretch)
        lanes = pl.ds(pl.multiple_of(pair * 128, 128), 128)
        block = 2 * (y + (tile % 2) * (1 - 2 * y)) + core + (tile // 2) * (1 - 2 * core)
        place = lax.broadcasted_iota(jnp.int32, (stretch, 1), 0) + block * stretch
        seg_col = jnp.where(place.astype(F32) >= split, 1.0, 0.0)
        same_here = seg_col == seg_row
        pair_queries = all_queries[here, lanes].astype(F32)
        pair_keys, pair_values = keys_t[lanes, :], values[:, lanes]
        found = []
        for side in range(2):
            keep = lane_is((stretch, 128), side * 64, side * 64 + 64)
            head_queries = jnp.where(keep, pair_queries, 0.0).astype(BF16)
            scores = jnp.where(same_here, dot(head_queries, pair_keys), MASKED_SCORE)
            weights = jnp.exp(scores - jnp.max(scores, axis=-1, keepdims=True))
            found.append(dot(weights.astype(BF16), pair_values) / jnp.sum(weights, axis=-1, keepdims=True))
        first = lane_is((stretch, 128), 0, 64)
        all_context[here, lanes] = jnp.where(first, found[0], found[1]).astype(BF16)

        @pl.when(step == 2 * pairs - 1)
        def _():
            ctx_copy().start()

        hooks(step, "a", 4 * pairs)
        return carry

    lax.fori_loop(0, 4 * pairs, attend_step, 0)
    ctx_copy().wait()

    def feed_step(step, carry):
        tile, part = 1 - step // parts, step % parts
        here = pl.ds(pl.multiple_of(tile * stretch, stretch), stretch)

        @pl.when(part == 0)
        def _():
            left = jnp.where(is_first, all_context[here, :], ctx_in[here, :])
            right = jnp.where(is_first, ctx_in[here, :], all_context[here, :])
            here_branch = dot(left, wo_v[:width, :]) + dot(right, wo_v[width:, :]) + vector(6)
            normed, _ = norm_parts(xs[here, :].astype(F32) + here_branch)
            value = normed * vector(7) + vector(8)
            y1_keep[...] = value.astype(BF16)
            total[...] = value + vector(9)

        there = pl.ds(pl.multiple_of(part * model, model), model)
        pre = dot(y1_keep[...], wup_v[:, there]) + vecs[pl.ds(part, 1), :]
        total[...] += dot(gelu_only(pre).astype(BF16), wdown_v[there, :])

        @pl.when(part == parts - 1)
        def _():
            normed, _ = norm_parts(total[...])
            value = (normed * vector(10) + vector(11)).astype(BF16)

            @pl.when(tile == 1)
            def _():
                out_send[...] = value

            @pl.when(tile == 0)
            def _():
                layer_out[row] = value

        hooks(step, "f", 2 * parts)
        return carry

    lax.fori_loop(0, 2 * parts, feed_step, 0)
    act_on("end")
    for index in range(len(results)):
        result_copy(index).wait()
    for copy in pending:
        copy.wait_send()


def vmem(count):
    return [pl.BlockSpec(memory_space=pltpu.VMEM)] * count


def local_call(body, outs, name, scratch=()):
    def call(core, *operands):
        return pl.pallas_call(
            body,
            out_shape=outs,
            in_specs=[pl.BlockSpec(memory_space=pltpu.SMEM)] + vmem(len(operands)),
            out_specs=vmem(len(outs)),
            scratch_shapes=list(scratch),
            compiler_params=pltpu.CompilerParams(vmem_limit_bytes=VMEM_LIMIT),
            name=name,
        )(core, *operands)

    return call


def finish_kernel(parts, go, g0, g1, g2, layer_in, igrad_in, up_in, down_in, small, wq, wk, wv, wo, layer_out, igrad, up, down, up_bias, *vectors):
    wo[...] = go[...].T.astype(F32)
    for pair, ref in enumerate((g0, g1, g2)):
        for core in range(2):
            at = core * 384 + pair * 128
            for place, out in enumerate((wq, wk, wv)):
                begin = core * 384 + place * 128
                out[:, at : at + 128] = ref[:, begin : begin + 128].astype(F32)
    layer_out[...] = layer_in[...]
    igrad[...] = igrad_in[...]
    up[...] = up_in[...]
    down[...] = down_in[...]

    @pl.when(pl.program_id(0) == 0)
    def _():
        model = small.shape[1]
        for part in range(parts):
            up_bias[part * model : (part + 1) * model] = small[part]
        for place, out in enumerate(vectors):
            out[...] = small[parts + place]


def finish(layer_output, input_grad, go, g0, g1, g2, up_part, down_part, small, hidden):
    model = go.shape[0]
    stretch, units, parts = layer_output.shape[1], up_part.shape[0], hidden // model
    shaped = jax.ShapeDtypeStruct
    rows = pl.BlockSpec((128, model), lambda i: (i, 0))
    columns = pl.BlockSpec((model, 128), lambda i: (0, i))
    tokens = pl.BlockSpec((2, stretch, 128), lambda i: (0, 0, i))
    unit = pl.BlockSpec((units, 128), lambda i: (0, i))
    line = pl.BlockSpec((model,), lambda i: (0,))
    square, vector = shaped((model, model), F32), shaped((model,), F32)
    found = pl.pallas_call(
        functools.partial(finish_kernel, parts),
        grid=(model // 128,),
        out_shape=(square,) * 4
        + (shaped(layer_output.shape, BF16), shaped(input_grad.shape, F32), shaped(up_part.shape, F32), shaped(down_part.shape, F32))
        + (shaped((hidden,), F32),)
        + (vector,) * 8,
        in_specs=[columns, rows, rows, rows, tokens, tokens, unit, unit, pl.BlockSpec(small.shape, lambda i: (0, 0))],
        out_specs=[rows] * 4 + [tokens, tokens, unit, unit, pl.BlockSpec((hidden,), lambda i: (0,))] + [line] * 8,
        compiler_params=pltpu.CompilerParams(vmem_limit_bytes=VMEM_LIMIT),
        name="finish",
    )(go, g0, g1, g2, layer_output, input_grad, up_part, down_part, small)
    wq, wk, wv, wo, layer_output, input_grad, up_part, down_part, up_bias, g1, s1, g2, s2, ob, db, qb, vb = found
    return layer_output, input_grad, wq, qb, wk, wv, vb, wo, ob, g1, s1, up_part.T, up_bias, down_part, db, g2, s2


def outputs(layer_output, input_grad, grad_wq, grad_wk, grad_wv, grad_wo, up_part, down_part, small):
    model = grad_wq.shape[0]
    base = small.shape[0] - 12
    vector = lambda index: small[index]
    return (
        layer_output,
        input_grad,
        grad_wq.astype(F32),
        vector(base + 6),
        grad_wk.astype(F32),
        grad_wv.astype(F32),
        vector(base + 7),
        grad_wo.astype(F32),
        vector(base + 4),
        vector(base),
        vector(base + 1),
        up_part.T,
        small[:base].reshape(-1),
        down_part,
        vector(base + 5),
        vector(base + 2),
        vector(base + 3),
    )


def layer_call(tokens, cotangent, segment_ids, mask_positions, vectors, weights):
    _, stretch, model = tokens.shape
    hidden = weights[4].shape[1]
    masks = mask_positions.shape[2]
    count, half, full, width = 2 * masks, 2 * stretch, 4 * stretch, model // 2
    units = hidden // 32
    shaped = jax.ShapeDtypeStruct
    low = lambda *shape: pltpu.VMEM(shape, BF16)
    wide = lambda *shape: pltpu.VMEM(shape, F32)
    results = [low(2, stretch, model), wide(2, stretch, model)] + [low(model, model)] * 4
    results += [wide(units, model), wide(units, model), wide(16, model)]
    scratch = results + [pltpu.VMEM(small.shape, small.dtype) for small in (segment_ids, mask_positions) + vectors]
    scratch += [
        wide(hidden // model + 8, model), low(width, model), low(model, model), low(model, width), low(width, full), low(width, full),
        low(full, model), low(model, full), low(2, stretch, model), low(2, 2, masks, model), low(2, masks, model), low(2, masks, model),
        low(masks, model), low(half, model), low(half, model), low(model, width), low(model, width), low(model, width), low(model, model),
        low(model, hidden), low(hidden, model), low(full, width), low(full, width), low(count, width), low(count, width),
        low(HEADS // 2, count, full), low(count, model), low(count, full), low(2, masks, width), low(2, masks, model),
        wide(hidden // model, masks, model), low(count, width), low(full, model), low(4, model, width),
        low(4 * units, 2 * model), low(4, units, 2 * model), low(2, 4, masks, model), low(2, 4, masks, model),
        wide(masks, model), wide(7, 16, model), wide(4, 16, model),
        low(full, width), low(full, width), low(half, width), wide(stretch, model), low(stretch, model), low(stretch, model),
        low(stretch, model), low(stretch, model),
    ]
    scratch += [low(model - model // 16, width)] * 4
    scratch += [pltpu.SemaphoreType.DMA((32,)), pltpu.SemaphoreType.DMA((120,)), pltpu.SemaphoreType.DMA((120,))]
    anywhere = [pl.BlockSpec(memory_space=pltpu.HBM)]
    return pl.pallas_call(
        layer_kernel,
        out_shape=(
            shaped((2, stretch, model), BF16),
            shaped((2, stretch, model), F32),
            shaped((model, model), BF16),
            shaped((model, model), BF16),
            shaped((model, model), BF16),
            shaped((model, model), BF16),
            shaped((units, model), F32),
            shaped((units, model), F32),
            shaped((16, model), F32),
        ),
        in_specs=anywhere * (4 + len(vectors) + len(weights)),
        out_specs=anywhere * 9,
        scratch_shapes=scratch,
        compiler_params=pltpu.CompilerParams(collective_id=0, has_side_effects=True, vmem_limit_bytes=62 * 2**20),
        name="layer",
    )(tokens, cotangent, segment_ids, mask_positions, *vectors, *weights)


def on_device(
    rows_total,
    tokens,
    cotangent,
    segment_ids,
    mask_positions,
    query_weight,
    query_bias,
    key_weight,
    value_weight,
    value_bias,
    output_weight,
    output_bias,
    first_gain,
    first_shift,
    up_weight,
    up_bias,
    down_weight,
    down_bias,
    second_gain,
    second_shift,
):
    if rows_total == 8:
        vectors = (up_bias, query_bias, value_bias, output_bias, first_gain, first_shift, down_bias, second_gain, second_shift)
        weights = (query_weight, key_weight, value_weight, output_weight, up_weight, down_weight)
        found = layer_call(
            tokens, cotangent, segment_ids, mask_positions, vectors, weights
        )
        return finish(*found, up_weight.shape[1])
    _, stretch, model = tokens.shape
    hidden = up_weight.shape[1]
    width = model // 2
    heads = HEADS // 2
    masks = mask_positions.shape[2]
    seq = lax.axis_index("seq")
    row = seq // 2
    core = seq % 2
    across = [(i, (i + 2) % 4) for i in range(4)]
    beside = [(i, i + 1 - 2 * (i % 2)) for i in range(4)]

    def swap(value):
        return lax.ppermute(value, "seq", across)

    def trade(value):
        return lax.ppermute(value, "seq", beside)

    def take(array, index):
        return lax.dynamic_index_in_dim(array, index, 0, keepdims=False)

    half = jnp.concatenate([take(tokens, row), swap(take(tokens, 1 - row))], axis=0)
    peer = trade(half)
    cot_half = jnp.concatenate([take(cotangent, row), swap(take(cotangent, 1 - row))], axis=0)
    cot_peer = trade(cot_half)
    blocks = jnp.stack([2 * row + core, 2 * (1 - row) + core, 2 * row + 1 - core, 2 * (1 - row) + 1 - core])
    positions = (blocks[:, None] * stretch + jnp.arange(stretch, dtype=jnp.int32)[None, :]).reshape(-1)
    segments = jnp.take(take(segment_ids, row).reshape(4, stretch), blocks, axis=0).reshape(-1)
    slots = take(mask_positions, row).reshape(-1)
    pos, seg, slot_col = positions[None, :], segments[None, :], slots[:, None]
    pos_col, seg_col, slot_row = positions[:, None], segments[:, None], slots[None, :]
    core_scalar = core.reshape(1).astype(jnp.int32)
    line = lambda value: value.reshape(1, -1)
    full = 4 * stretch
    count = 2 * masks
    shaped = jax.ShapeDtypeStruct

    keys, values, queries, context, probs, picked = local_call(
        project_kernel,
        (
            shaped((full, width), BF16),
            shaped((full, width), BF16),
            shaped((count, width), BF16),
            shaped((count, width), BF16),
            shaped((heads, count, full), F32),
            shaped((count, model), BF16),
        ),
        "project",
    )(core_scalar, half, peer, pos, seg, slot_col, query_weight, line(query_bias), key_weight, value_weight, line(value_bias))

    two = context.reshape(2, masks, width)
    ctx_peer = trade(take(two, 1 - core))
    normed_low, feed, branch_low, grad_h1, small = local_call(
        masked_kernel,
        (
            shaped((masks, model), BF16),
            shaped((masks, model), BF16),
            shaped((masks, model), BF16),
            shaped((masks, model), F32),
            shaped((16, model), F32),
        ),
        "masked",
    )(
        core_scalar, take(two, core), ctx_peer, picked, cot_half, cot_peer, pos, slot_col, output_weight, line(output_bias),
        line(first_gain), line(first_shift), up_weight, line(up_bias), down_weight, line(down_bias), line(second_gain), line(second_shift),
    )
    branch_peer = trade(branch_low)
    grads, igrad_own, igrad_peer, bias = local_call(
        back_kernel,
        (
            shaped((4, model, width), BF16),
            shaped((2 * stretch, model), F32),
            shaped((2 * stretch, model), BF16),
            shaped((2, width), F32),
        ),
        "back",
        [pltpu.VMEM((count, width), BF16), pltpu.VMEM((full, width), BF16), pltpu.VMEM((full, width), BF16)],
    )(
        core_scalar, keys, values, queries, context, probs, picked, branch_low, branch_peer, grad_h1, half, peer, pos_col, slot_row,
        query_weight, key_weight, value_weight, output_weight,
    )
    igrad = igrad_own + trade(igrad_peer).astype(F32)
    igrad_other = swap(igrad[stretch:].astype(BF16)).astype(F32)
    igrad_mine = igrad[:stretch]
    input_grad = jnp.where(row == 0, jnp.stack([igrad_mine, igrad_other]), jnp.stack([igrad_other, igrad_mine]))

    ctx_own, ctx_other = local_call(
        attend_kernel, (shaped((2 * stretch, width), BF16), shaped((2 * stretch, width), BF16)), "attend"
    )(core_scalar, half, peer, seg, seg_col, keys, values, query_weight, line(query_bias))
    out_mine, out_other = local_call(
        feed_kernel, (shaped((stretch, model), BF16), shaped((stretch, model), BF16)), "feed"
    )(
        core_scalar, ctx_own, trade(ctx_other), half, output_weight, line(output_bias), line(first_gain), line(first_shift),
        up_weight, line(up_bias), down_weight, line(down_bias), line(second_gain), line(second_shift),
    )
    out_other = swap(out_other)
    layer_output = jnp.where(row == 0, jnp.stack([out_mine, out_other]), jnp.stack([out_other, out_mine]))

    wide = jnp.zeros((2, model), F32)
    bias_rows = lax.dynamic_update_slice(wide, bias, (0, core * width))
    base = hidden // model + 6
    small = jnp.concatenate([small[:base], bias_rows, small[base + 2 :]], axis=0)

    both = ("rows", "seq")
    small = lax.psum(small, both)
    zero = jnp.zeros((model, model), F32)
    wide_grads = [lax.dynamic_update_slice(zero, grads[k].astype(F32), (0, core * width)) for k in (1, 2, 3)]
    rows_wo = grads[0].reshape(2, width, width).transpose(1, 0, 2).reshape(width, model).astype(F32)
    wide_grads.append(lax.dynamic_update_slice(zero, rows_wo, (core * width, 0)))
    grad_wq, grad_wk, grad_wv, grad_wo = lax.psum(tuple(wide_grads), both)
    pieces = []
    units = hidden // 8
    for part in range(8):
        (piece,) = local_call(hidden_kernel, (shaped((units, 2 * model), BF16),), "hidden")(
            jnp.full((1,), part, jnp.int32), normed_low, feed, up_weight, line(up_bias), down_weight
        )
        pieces.append(piece.astype(F32))
    hidden_grads = lax.psum_scatter(jnp.concatenate(pieces, axis=0), both, scatter_dimension=0, tiled=True)

    up_part, down_part = hidden_grads[:, :model], hidden_grads[:, model:]
    return outputs(layer_output, input_grad, grad_wq, grad_wk, grad_wv, grad_wo, up_part, down_part, small)


def solution(mesh):
    split = P("rows", "seq", None)
    in_specs = (split, split, P("rows", None), P("rows", None, None)) + (P(),) * 15
    out_specs = (split, split) + (P(),) * 9 + (P(None, ("rows", "seq")), P(), P(("rows", "seq"), None), P(), P(), P())
    return jax.shard_map(
        functools.partial(on_device, mesh.shape["rows"]), mesh=mesh, in_specs=in_specs, out_specs=out_specs, check_vma=False
    )
```

```python
import functools

import jax
import jax.numpy as jnp
from jax import lax
from jax.experimental import pallas as pl
from jax.experimental.pallas import tpu as pltpu
from jax.sharding import PartitionSpec as P

HEADS = 12
EPSILON = 1e-12
MASKED_SCORE = -1000000000.0
F32 = jnp.float32
BF16 = jnp.bfloat16
MESH = pl.DeviceIdType.MESH
VMEM_LIMIT = 56 * 2**20
ORDERS = ("xyz", "yxz", "xyz", "xyz")
PLAN = {
    "G0": ("Sr00", "Sr01"),
    "p0": ("Sr10", "Sr11"),
    "p1": ("Sr20", "Sr21"),
    "p2": ("Sr30", "Sr31", "Er00", "Sr02"),
    "dx": ("Ss0", "Er10", "Sr12", "Er01"),
    "a0": ("Er11",),
    "a1": ("Er20", "Sr22"),
    "a2": ("Ed", "Si0", "Es0", "Ss1", "Er02", "Sr03"),
    "a3": ("Ef", "Er21"),
    "a5": ("Er30", "Sr32", "Er22", "Sr23"),
    "a6": ("Er03", "Sg03", "EH", "Si1", "Sh0", "Es1", "Ss2", "Er12", "Sr13", "Er31", "Er23", "Sg23", "Ei0"),
    "a7": ("Er32", "Sr33"),
    "a8": ("Eg03", "Sg00", "Sg02"),
    "a11": ("Er13", "Sg13", "Sh1", "Ei1"),
    "f0": ("Es2", "Ss3", "Eg02", "St00", "Sg01", "Eg23", "Sg20", "Sg22", "Eh0"),
    "f2": ("Et00", "Eg00", "Er33", "Sg33"),
    "f4": ("Eg13", "Sg10", "Sg12", "Eg22", "St20", "Sg21"),
    "f6": ("Es3", "Et20", "Eh1"),
    "f7": ("So0",),
    "end": ("Eg33", "Sg30", "Sg32", "Eg01", "St01", "Ek", "Et01", "Eg20", "Eg10", "Em", "So1", "Eg12", "St10", "Sg11", "Eo0", "Et10", "Eg21", "St21", "Eg32", "St30", "Sg31", "Et21", "Eg30", "Et30", "Eo1", "Eg31", "St31", "Eg11", "St11", "Et31", "Et11"),
}


def dot(left, right):
    return lax.dot_general(left, right, (((1,), (0,)), ((), ())), preferred_element_type=F32)


def dot_nt(left, right):
    return lax.dot_general(left, right, (((1,), (1,)), ((), ())), preferred_element_type=F32)


def dot_tn(left, right):
    return lax.dot_general(left, right, (((0,), (0,)), ((), ())), preferred_element_type=F32)


def norm_parts(hidden):
    centred = hidden - jnp.mean(hidden, axis=-1, keepdims=True)
    variance = jnp.mean(centred * centred, axis=-1, keepdims=True)
    scale = lax.rsqrt(variance + EPSILON)
    return centred * scale, scale


def norm_back(grad, normed, scale, gain):
    scaled = grad * gain
    along = jnp.mean(scaled * normed, axis=-1, keepdims=True)
    return (scaled - jnp.mean(scaled, axis=-1, keepdims=True) - normed * along) * scale


GELU_A = 0.7978845608028654
GELU_B = 0.044715


def gelu_parts(value):
    square = value * value
    bent = jnp.tanh(GELU_A * value * (1.0 + GELU_B * square))
    half = 0.5 * (1.0 + bent)
    slope = half + 0.5 * value * (1.0 - bent * bent) * (GELU_A * (1.0 + 3.0 * GELU_B * square))
    return value * half, slope


def gelu_only(value):
    bent = jnp.tanh(GELU_A * value * (1.0 + GELU_B * value * value))
    return 0.5 * value * (1.0 + bent)


def lane_is(shape, low, high):
    lane = lax.broadcasted_iota(jnp.int32, shape, len(shape) - 1)
    return (lane >= low) & (lane < high)


def project_kernel(core, half, peer, pos, seg, slots, wq, bq, wk, wv, bv, keys, values, queries, context, probs, picked):
    width = keys.shape[1]
    mine = pl.ds(pl.multiple_of(core[0] * width, 128), width)
    count = slots.shape[0]
    tokens_half = half.shape[0]
    chosen = jnp.where(slots[...] == pos[...], 1.0, 0.0).astype(BF16)
    rows = dot(chosen[:, :tokens_half], half[...]) + dot(chosen[:, tokens_half:], peer[...])
    rows = rows.astype(BF16)
    picked[...] = rows
    queries[...] = (dot(rows, wq[:, mine]) + bq[:, mine]).astype(BF16)
    for place, part in ((0, half), (tokens_half, peer)):
        for start in range(0, tokens_half, 256):
            block = part[start : start + 256, :]
            there = slice(place + start, place + start + 256)
            keys[there, :] = dot(block, wk[:, mine]).astype(BF16)
            values[there, :] = (dot(block, wv[:, mine]) + bv[:, mine]).astype(BF16)
    sequence = lax.broadcasted_iota(jnp.int32, (count, 1), 0) // (count // 2)
    same = seg[...] == sequence
    for pair in range(width // 128):
        lanes = slice(pair * 128, pair * 128 + 128)
        pair_queries = queries[:, lanes].astype(F32) * 0.125
        pair_keys, pair_values = keys[:, lanes], values[:, lanes]
        outs = []
        for side in range(2):
            keep = lane_is((count, 128), side * 64, side * 64 + 64)
            head_queries = jnp.where(keep, pair_queries, 0.0).astype(BF16)
            scores = jnp.where(same, dot_nt(head_queries, pair_keys), MASKED_SCORE)
            weights = jnp.exp(scores - jnp.max(scores, axis=-1, keepdims=True))
            share = weights / jnp.sum(weights, axis=-1, keepdims=True)
            probs[pair * 2 + side] = share
            outs.append(dot(share.astype(BF16), pair_values))
        first = lane_is((count, 128), 0, 64)
        context[:, lanes] = jnp.where(first, outs[0], outs[1]).astype(BF16)


def masked_kernel(core, ctx_own, ctx_peer, picked, cot_half, cot_peer, pos, slots, wo, bo, g1, s1, wup, bup, wdown, bdown, g2, s2, normed_low, feed, branch_low, grad_h1, small):
    count, width = ctx_own.shape
    hidden = wup.shape[1]
    model = wup.shape[0]
    tokens_half = cot_half.shape[0]
    mine = pl.multiple_of(core[0] * count, 16)
    is_first = core[0] == 0
    left = jnp.where(is_first, ctx_own[...], ctx_peer[...])
    right = jnp.where(is_first, ctx_peer[...], ctx_own[...])
    branch = dot(left, wo[:width, :]) + dot(right, wo[width:, :]) + bo[...]
    h1 = picked[pl.ds(mine, count), :].astype(F32) + branch
    n1, r1 = norm_parts(h1)
    y1 = n1 * g1[...] + s1[...]
    y1_low = y1.astype(BF16)
    normed_low[...] = y1_low
    total = y1 + bdown[...]
    slopes = []
    step = model
    for start in range(0, hidden, step):
        pre = dot(y1_low, wup[:, start : start + step]) + bup[:, start : start + step]
        act, slope = gelu_parts(pre)
        slopes.append(slope)
        total = total + dot(act.astype(BF16), wdown[start : start + step, :])
    n2, r2 = norm_parts(total)
    chosen = jnp.where(slots[pl.ds(mine, count), :] == pos[...], 1.0, 0.0).astype(BF16)
    grad = dot(chosen[:, :tokens_half], cot_half[...]) + dot(chosen[:, tokens_half:], cot_peer[...])
    gh2 = norm_back(grad, n2, r2, g2[...])
    gf = gh2.astype(BF16)
    feed[...] = gf
    gy1 = gh2
    small[...] = jnp.zeros_like(small)
    for place, start in enumerate(range(0, hidden, step)):
        ga = dot_nt(gf, wdown[start : start + step, :])
        gp = (ga * slopes[place]).astype(BF16)
        small[place : place + 1, :] = jnp.sum(gp.astype(F32), axis=0, keepdims=True)
        gy1 = gy1 + dot_nt(gp, wup[:, start : start + step])
    gh1 = norm_back(gy1, n1, r1, g1[...])
    grad_h1[...] = gh1
    gb = gh1.astype(BF16)
    branch_low[...] = gb
    base = hidden // step
    for place, value in enumerate((gy1 * n1, gy1, grad * n2, grad, gb.astype(F32), gf.astype(F32))):
        small[base + place : base + place + 1, :] = jnp.sum(value, axis=0, keepdims=True)


def back_kernel(core, keys, values, queries, context, probs, picked, gb_own, gb_peer, gh1, half, peer, pos_col, slots_row, wq, wk, wv, wo, grads, igrad_own, igrad_peer, bias, dq_low, dk_low, dv_low):
    width = keys.shape[1]
    count = queries.shape[0]
    own = gb_own.shape[0]
    tokens_half = half.shape[0]
    is_first = core[0] == 0
    mine = pl.ds(pl.multiple_of(core[0] * width, 128), width)
    mine_rows = pl.ds(pl.multiple_of(core[0] * width, 128), width)
    top = jnp.where(is_first, gb_own[...], gb_peer[...])
    low = jnp.where(is_first, gb_peer[...], gb_own[...])
    gb = jnp.concatenate([top, low], axis=0)
    gctx = dot_nt(gb, wo[mine_rows, :]).astype(BF16)
    for pair in range(width // 128):
        lanes = slice(pair * 128, pair * 128 + 128)
        pair_keys, pair_values, pair_queries = keys[:, lanes], values[:, lanes], queries[:, lanes]
        pair_gctx = gctx[:, lanes]
        dqs, dks, dvs = [], [], []
        for side in range(2):
            keep = lane_is((count, 128), side * 64, side * 64 + 64)
            head_gctx = jnp.where(keep, pair_gctx.astype(F32), 0.0).astype(BF16)
            share = probs[pair * 2 + side]
            gp = dot_nt(head_gctx, pair_values)
            spread = jnp.sum(share * gp, axis=-1, keepdims=True)
            gs = (share * (gp - spread)).astype(BF16)
            dqs.append(dot(gs, pair_keys))
            dks.append(dot_tn(gs, pair_queries))
            dvs.append(dot_tn(share.astype(BF16), pair_gctx))
        first = lane_is((count, 128), 0, 64)
        dq_low[:, lanes] = (jnp.where(first, dqs[0], dqs[1]) * 0.125).astype(BF16)
        first = lane_is((2 * tokens_half, 128), 0, 64)
        dk_low[:, lanes] = (jnp.where(first, dks[0], dks[1]) * 0.125).astype(BF16)
        dv_low[:, lanes] = jnp.where(first, dvs[0], dvs[1]).astype(BF16)
    grads[1] = dot_tn(picked[...], dq_low[...]).astype(BF16)
    gwo = dot_tn(context[...], gb).astype(BF16)
    grads[0, :width, :] = gwo[:, :width]
    grads[0, width:, :] = gwo[:, width:]
    for place, part in ((2, dk_low), (3, dv_low)):
        total = dot_tn(half[...], part[:tokens_half, :]) + dot_tn(peer[...], part[tokens_half:, :])
        grads[place] = total.astype(BF16)
    bias[0:1, :] = jnp.sum(dq_low[...].astype(F32), axis=0, keepdims=True)
    bias[1:2, :] = jnp.sum(dv_low[...].astype(F32), axis=0, keepdims=True)
    spread_rows = dot_nt(dq_low[...], wq[:, mine])
    zero = jnp.zeros((own, wq.shape[0]), F32)
    spread_rows = spread_rows + jnp.concatenate(
        [jnp.where(is_first, gh1[...], zero), jnp.where(is_first, zero, gh1[...])], axis=0
    )
    high = spread_rows.astype(BF16)
    rest = (spread_rows - high.astype(F32)).astype(BF16)
    for start in range(0, 2 * tokens_half, 256):
        here = slice(start, start + 256)
        chosen = jnp.where(pos_col[here, :] == slots_row[...], 1.0, 0.0).astype(BF16)
        total = dot(chosen, high) + dot(chosen, rest)
        total = total + dot_nt(dk_low[here, :], wk[:, mine]) + dot_nt(dv_low[here, :], wv[:, mine])
        if start < tokens_half:
            igrad_own[here, :] = total
        else:
            igrad_peer[start - tokens_half : start - tokens_half + 256, :] = total.astype(BF16)


def attend_kernel(core, half, peer, seg, seg_col, keys, values, wq, bq, own, other):
    width = keys.shape[1]
    mine = pl.ds(pl.multiple_of(core[0] * width, 128), width)
    tile = 256
    for part, out in ((half, own), (peer, other)):
        place = 0 if part is half else half.shape[0]

        def body(step, carry, part=part, out=out, place=place):
            here = pl.ds(pl.multiple_of(step * tile, tile), tile)
            queries = (dot(part[here, :], wq[:, mine]) + bq[:, mine]).astype(BF16).astype(F32) * 0.125
            same = seg_col[pl.ds(pl.multiple_of(place + step * tile, tile), tile), :] == seg[...]
            for pair in range(width // 128):
                lanes = slice(pair * 128, pair * 128 + 128)
                outs = []
                for side in range(2):
                    keep = lane_is((tile, 128), side * 64, side * 64 + 64)
                    head_queries = jnp.where(keep, queries[:, lanes], 0.0).astype(BF16)
                    scores = jnp.where(same, dot_nt(head_queries, keys[:, lanes]), MASKED_SCORE)
                    weights = jnp.exp(scores - jnp.max(scores, axis=-1, keepdims=True))
                    total = jnp.sum(weights, axis=-1, keepdims=True)
                    outs.append(dot(weights.astype(BF16), values[:, lanes]) / total)
                first = lane_is((tile, 128), 0, 64)
                out[here, lanes] = jnp.where(first, outs[0], outs[1]).astype(BF16)
            return carry

        lax.fori_loop(0, part.shape[0] // tile, body, 0)


def feed_kernel(core, ctx_own, ctx_peer, half, wo, bo, g1, s1, wup, bup, wdown, bdown, g2, s2, own, other):
    width = ctx_own.shape[1]
    hidden, model = wdown.shape
    is_first = core[0] == 0
    tile = own.shape[0]
    for start, out in ((0, own), (tile, other)):
        here = slice(start, start + tile)
        left = jnp.where(is_first, ctx_own[here, :], ctx_peer[here, :])
        right = jnp.where(is_first, ctx_peer[here, :], ctx_own[here, :])
        branch = dot(left, wo[:width, :]) + dot(right, wo[width:, :]) + bo[...]
        n1, _ = norm_parts(half[here, :].astype(F32) + branch)
        y1 = n1 * g1[...] + s1[...]
        y1_low = y1.astype(BF16)
        total = y1 + bdown[...]
        for place in range(0, hidden, model):
            pre = dot(y1_low, wup[:, place : place + model]) + bup[:, place : place + model]
            total = total + dot(gelu_only(pre).astype(BF16), wdown[place : place + model, :])
        n2, _ = norm_parts(total)
        out[...] = (n2 * g2[...] + s2[...]).astype(BF16)


def hidden_kernel(slot, normed, feed, wup, bup, wdown, out):
    units = out.shape[0]
    model = normed.shape[1]
    mine = pl.ds(pl.multiple_of(slot[0] * units, 128), units)
    pre = dot(normed[...], wup[:, mine]) + bup[:, mine]
    act, slope = gelu_parts(pre)
    ga = dot_nt(feed[...], wdown[mine, :])
    gp = (ga * slope).astype(BF16)
    out[:, :model] = dot_tn(gp, normed[...]).astype(BF16)
    out[:, model:] = dot_tn(act.astype(BF16), feed[...]).astype(BF16)


def place_here():
    row, seq = lax.axis_index("rows"), lax.axis_index("seq")
    return row // 2, row % 2, seq // 2, seq % 2


def device(z, x, y, core):
    return (z * 2 + x, y * 2 + core)


def layer_kernel(
    tokens, cotangent, segments_in, slots_in, up_bias_in, bq_in, bv_in, bo_in, g1_in, s1_in, bdown_in, g2_in, s2_in, wq, wk, wv, wo, wup, wdown,
    layer_hbm, igrad_hbm, hbm_o, hbm_0, hbm_1, hbm_2, up_hbm, down_hbm, small_hbm,
    layer_out, input_grad, out_o, out_0, out_1, out_2, up_out, down_out, small_out,
    segments, slots, up_bias, bq, bv, bo, g1, s1, bdown, g2, s2, vecs, wq_t, wkv_t, wo_t, keys_t, values_t,
    xs, xs_t, cots, cot_part, cot_in, cot_sum, cot_far, dx_send, dx_in, wq_v, wk_v, wv_v, wo_v, wup_v, wdown_v, keys, values, queries, context, probs, picked, chosen, ctx_both, gb_both,
    slopes, dq_low, dkv_low, grads, hidden_grads, hidden_in, hidden_far, hidden_share, hidden_got, fac_normed, fac_feed, grad_h1, small_in, small_z,
    all_queries, all_context, ctx_in, total, y1_keep, out_send, igrad_send, igrad_in,
    in_o, in_0, in_1, in_2, local_sem, send_sem, recv_sem,
):
    z, x, y, core = place_here()
    row = y
    stretch, model = tokens.shape[1:]
    half = 2 * stretch
    full = 2 * half
    width = wq_v.shape[1]
    masks = slots.shape[2]
    count = 2 * masks
    hidden = wup.shape[1]
    parts = hidden // model
    units = down_out.shape[0]
    others = [(z + k) % 4 for k in (1, 2, 3)]
    at_y, at_x, twin = device(z, x, 1 - y, core), device(z, 1 - x, y, core), device(z, x, y, 1 - core)
    columns = [device(o, x, y, core) for o in others]
    mine = pl.ds(pl.multiple_of(core * width, 128), width)
    my_slots = pl.ds(pl.multiple_of(core * masks, 16), masks)
    twin_slots = pl.ds(pl.multiple_of((1 - core) * masks, 16), masks)
    pending = []

    def local(src, dst, index):
        copy = pltpu.make_async_copy(src, dst, local_sem.at[index])
        copy.start()
        return copy

    def remote(src, dst, index, target):
        return pltpu.make_async_remote_copy(
            src_ref=src, dst_ref=dst, send_sem=send_sem.at[index], recv_sem=recv_sem.at[index],
            device_id=target, device_id_type=MESH,
        )

    def push(src, dst, index, target):
        copy = remote(src, dst, index, target)
        copy.start()
        pending.append(copy)
        return copy

    def vector(index):
        return vecs[index : index + 1, :]

    def half_vector(index):
        return vecs[index : index + 1, mine]

    small_pairs = (
        (segments_in, segments), (slots_in, slots), (up_bias_in, up_bias), (bq_in, bq), (bv_in, bv), (bo_in, bo), (g1_in, g1),
        (s1_in, s1), (bdown_in, bdown), (g2_in, g2), (s2_in, s2),
    )
    own_tokens = local(tokens.at[row], xs.at[pl.ds(0, stretch)], 0)
    get_wk = local(wk.at[:, mine], wk_v, 1)
    get_wv = local(wv.at[:, mine], wv_v, 2)
    get_small = [local(src, dst, 8 + k) for k, (src, dst) in enumerate(small_pairs)]
    get_wq = local(wq.at[:, mine], wq_v, 3)
    own_cot = local(cotangent, cots, 4)
    get_wo = local(wo, wo_v, 5)
    get_up = local(wup, wup_v, 6)
    get_down = local(wdown, wdown_v, 7)

    greeted = [twin, at_x, at_y] + columns
    barrier = pltpu.get_barrier_semaphore()
    for target in greeted:
        pl.semaphore_signal(barrier, inc=1, device_id=target, device_id_type=MESH)
    pl.semaphore_wait(barrier, len(greeted))

    piece = stretch // 2
    tok_y = [
        push(tokens.at[1 - row, pl.ds(k * piece, piece)], xs.at[pl.ds(stretch + k * piece, piece)], k, at_y) for k in range(2)
    ]
    tok_c = push(tokens.at[row], xs.at[pl.ds(half, stretch)], 2, twin)

    for copy in get_small:
        copy.wait()
    for part in range(parts):
        vecs[part : part + 1, :] = up_bias[part * model : (part + 1) * model].reshape(1, model)
    for place, value in enumerate((bq, bv, bo, g1, s1, bdown, g2, s2)):
        vecs[parts + place : parts + place + 1, :] = value[...].reshape(1, model)

    def key_values(start):
        here = pl.ds(start, stretch)
        block = xs[here, :]
        block_keys = dot(block, wk_v[...]).astype(BF16)
        block_values = (dot(block, wv_v[...]) + half_vector(5)).astype(BF16)
        keys[here, :] = block_keys
        values[here, :] = block_values
        xs_t[:, here] = block.T
        keys_t[:, here] = block_keys.T
        values_t[:, here] = block_values.T

    blocks = [2 * y + core, 2 * (1 - y) + core, 2 * y + 1 - core, 2 * (1 - y) + 1 - core]
    lane = lax.broadcasted_iota(jnp.int32, (1, stretch), 1)
    pos_row = jnp.concatenate([lane + block * stretch for block in blocks], axis=1)
    seg_here = segments[pl.ds(row, 1), :]
    split = jnp.sum((1 - seg_here).astype(F32), axis=1, keepdims=True)
    pos_row = pos_row.astype(F32)
    seg_row = jnp.where(pos_row >= split, 1.0, 0.0)
    diagonal = lax.broadcasted_iota(jnp.int32, (masks, masks), 0) == lax.broadcasted_iota(jnp.int32, (masks, masks), 1)

    def slot_column(which, sequence):
        line = slots[which].astype(F32)[sequence : sequence + 1, :]
        return jnp.sum(jnp.where(diagonal, line, 0.0), axis=1, keepdims=True)

    for sequence in range(2):
        column = slot_column(row, sequence)
        chosen[sequence * masks : (sequence + 1) * masks, :] = jnp.where(column == pos_row, 1.0, 0.0).astype(BF16)
    own_cot.wait()
    for sequence in range(2):
        here = chosen[sequence * masks : (sequence + 1) * masks, :stretch]
        cot_part[0, sequence] = dot(here, cots[row]).astype(BF16)
        there = jnp.where(slot_column(1 - row, sequence) == pos_row[:, :stretch], 1.0, 0.0).astype(BF16)
        cot_part[1, sequence] = dot(there, cots[1 - row]).astype(BF16)
    cot_c = push(cot_part.at[:, 1 - core], cot_in, 4, twin)

    own_tokens.wait()
    get_wk.wait()
    get_wv.wait()
    key_values(0)
    tok_c.wait_recv()
    key_values(half)
    get_wq.wait()
    for pair in range(width // 128):
        lanes = slice(pair * 128, pair * 128 + 128)
        wkv_t[pair * 256 : pair * 256 + 128, :] = wk_v[:, lanes].T
        wkv_t[pair * 256 + 128 : pair * 256 + 256, :] = wv_v[:, lanes].T
    wq_t[...] = wq_v[...].T
    forward = []
    for k in range(2):
        tok_y[k].wait_recv()
        src = xs.at[pl.ds(stretch + k * piece, piece)]
        forward.append(push(src, xs.at[pl.ds(half + stretch + k * piece, piece)], 5 + k, twin))
    cot_c.wait_recv()
    cot_sum[...] = cot_part[:, core] + cot_in[...]
    cot_y = push(cot_sum.at[1], cot_far, 3, at_y)
    key_values(stretch)
    for copy in forward:
        copy.wait_recv()
    key_values(half + stretch)

    rows = dot(chosen[...], xs[...]).astype(BF16)
    picked[...] = rows
    queries[...] = (dot(rows, wq_v[...]) + half_vector(4)).astype(BF16)
    sequence = lax.broadcasted_iota(jnp.int32, (count, 1), 0) // masks
    same = seg_row == sequence.astype(F32)
    pairs = width // 128
    for pair in range(pairs):
        lanes = slice(pair * 128, pair * 128 + 128)
        pair_queries = queries[:, lanes].astype(F32) * 0.125
        pair_keys, pair_values = keys_t[lanes, :], values[:, lanes]
        outs = []
        for side in range(2):
            keep = lane_is((count, 128), side * 64, side * 64 + 64)
            head_queries = jnp.where(keep, pair_queries, 0.0).astype(BF16)
            scores = jnp.where(same, dot(head_queries, pair_keys), MASKED_SCORE)
            weights = jnp.exp(scores - jnp.max(scores, axis=-1, keepdims=True))
            share = weights / jnp.sum(weights, axis=-1, keepdims=True)
            share = share.astype(BF16)
            probs[pair * 2 + side] = share
            outs.append(dot(share, pair_values))
        first = lane_is((count, 128), 0, 64)
        context[:, lanes] = jnp.where(first, outs[0], outs[1]).astype(BF16)
    ctx_both[core] = context[my_slots, :]
    ctx_c = push(context.at[twin_slots], ctx_both.at[core], 7, twin)

    for start in range(0, full, stretch):
        value = (dot(xs[start : start + stretch, :], wq_v[...]) + half_vector(4)).astype(BF16)
        all_queries[start : start + stretch, :] = (value.astype(F32) * 0.125).astype(BF16)
    get_wo.wait()
    wo_t[...] = wo_v[mine, :].T
    ctx_c.wait_recv()

    branch = dot(ctx_both[0], wo_v[:width, :]) + dot(ctx_both[1], wo_v[width:, :]) + vector(6)
    n1, r1 = norm_parts(picked[my_slots, :].astype(F32) + branch)
    y1 = n1 * vector(7) + vector(8)
    y1_low = y1.astype(BF16)
    fac_normed[core, z] = y1_low
    spot = fac_normed.at[core, z]
    norm_z = [push(spot, spot, 9 + k, columns[k]) for k in range(3)]
    get_up.wait()
    get_down.wait()
    sum2 = y1 + vector(9)
    for part in range(parts):
        there = slice(part * model, (part + 1) * model)
        act, slope = gelu_parts(dot(y1_low, wup_v[:, there]) + vector(part))
        slopes[part] = slope
        sum2 = sum2 + dot(act.astype(BF16), wdown_v[there, :])
    n2, r2 = norm_parts(sum2)
    cot_y.wait_recv()
    grad = cot_sum[0].astype(F32) + cot_far[...].astype(F32)
    gh2 = norm_back(grad, n2, r2, vector(10))
    gf = gh2.astype(BF16)
    fac_feed[core, z] = gf
    spot = fac_feed.at[core, z]
    feed_z = [push(spot, spot, 12 + k, columns[k]) for k in range(3)]
    gf_t = gf.T
    gy1_t = jnp.zeros((model, masks), F32)
    small_in[0] = jnp.zeros(small_in.shape[1:], F32)
    for part in range(parts):
        there = slice(part * model, (part + 1) * model)
        gp = (dot(wdown_v[there, :], gf_t).T * slopes[part]).astype(BF16)
        small_in[0, part : part + 1, :] = jnp.sum(gp.astype(F32), axis=0, keepdims=True)
        gy1_t = gy1_t + dot(wup_v[:, there], gp.T)
    gy1 = gh2 + gy1_t.T
    gh1 = norm_back(gy1, n1, r1, vector(7))
    grad_h1[...] = gh1
    gb = gh1.astype(BF16)
    gb_both[core] = gb
    gb_c = push(gb_both.at[core], gb_both.at[core], 15, twin)
    for place, value in enumerate((gy1 * n1, gy1, grad * n2, grad, gb.astype(F32), gf.astype(F32))):
        small_in[0, parts + place : parts + place + 1, :] = jnp.sum(value, axis=0, keepdims=True)
    gb_c.wait_recv()

    spots = {"x": x, "y": y}
    neighbours = {"x": at_x, "y": at_y}
    ins = [in_o, in_0, in_1, in_2]
    outs = [out_o, out_0, out_1, out_2]
    half_rows, quarter, chunk = model // 2, model // 4, model // 16

    def rows_of(job):
        p1, p2 = (spots[dim] for dim in ORDERS[job][:2])
        kept, gone = p1 * half_rows, (1 - p1) * half_rows
        return kept, kept + p2 * quarter, kept + (1 - p2) * quarter, kept + p2 * quarter + z * chunk, gone + (1 - p2) * quarter, gone + p2 * quarter

    def at(start, size):
        return pl.ds(pl.multiple_of(start, 16), size)

    def job_copies(kind, job, stage):
        first, second = (neighbours[dim] for dim in ORDERS[job][:2])
        kept, mine_at, pass_at, own, gone_pass, gone_keep = rows_of(job)
        source, arrive, out = grads.at[job], ins[job], outs[job]
        base = 40 + job * 16

        def spread(start, size, index, target):
            spot = out.at[at(start, size), mine]
            return remote(spot, spot, base + index, target)

        if kind == "r" and stage == 0:
            return [remote(source.at[at(gone_pass, quarter)], arrive.at[pl.ds(0, quarter)], base, first)]
        if kind == "r" and stage == 1:
            return [remote(source.at[at(gone_keep, quarter)], arrive.at[pl.ds(quarter, quarter)], base + 1, first)]
        if kind == "r" and stage == 2:
            return [remote(source.at[at(pass_at, quarter)], arrive.at[pl.ds(2 * quarter, quarter)], base + 2, second)]
        if kind == "r":
            return [
                remote(
                    source.at[at(mine_at + others[k] * chunk, chunk)], arrive.at[pl.ds(3 * quarter + k * chunk, chunk)], base + 3 + k, columns[k]
                )
                for k in range(3)
            ]
        if kind == "g" and stage == 3:
            return [spread(own, chunk, 6 + k, columns[k]) for k in range(3)]
        if kind == "g" and stage == 2:
            return [spread(mine_at, quarter, 9, second)]
        if kind == "g" and stage == 0:
            return [spread(mine_at, quarter, 10, first)]
        if kind == "g":
            return [spread(pass_at, quarter, 11, first)]
        return [spread(kept if stage == 0 else half_rows - kept, half_rows, 12 + stage, twin)]

    def job_start(kind, job, stage):
        for copy in job_copies(kind, job, stage):
            copy.start()

    def job_end(kind, job, stage):
        for copy in job_copies(kind, job, stage):
            copy.wait()
        if kind != "r":
            return
        _, mine_at, pass_at, own, _, _ = rows_of(job)
        arrive = ins[job]
        if stage == 0:
            here = at(pass_at, quarter)
            grads[job, here] = (grads[job, here].astype(F32) + arrive[:quarter].astype(F32)).astype(BF16)
        elif stage == 2:
            here = at(mine_at, quarter)
            value = grads[job, here].astype(F32) + arrive[quarter : 2 * quarter].astype(F32)
            grads[job, here] = (value + arrive[2 * quarter : 3 * quarter].astype(F32)).astype(BF16)
        elif stage == 3:
            value = grads[job, at(own, chunk)].astype(F32)
            for k in range(3):
                value = value + arrive[3 * quarter + k * chunk : 3 * quarter + (k + 1) * chunk].astype(F32)
            outs[job][at(own, chunk), mine] = value.astype(BF16)

    def small_copies(stage):
        if stage < 3:
            target = (twin, at_y, at_x)[stage]
            return [remote(small_in.at[2 * stage], small_in.at[2 * stage + 1], 16 + stage, target)]
        return [remote(small_in.at[6], small_z.at[z], 19 + k, target) for k, target in enumerate(columns)]

    def small_start(stage):
        for copy in small_copies(stage):
            copy.start()

    def small_end(stage):
        for copy in small_copies(stage):
            copy.wait()
        if stage < 3:
            small_in[2 * stage + 2] = small_in[2 * stage] + small_in[2 * stage + 1]
            if stage == 2:
                small_z[z] = small_in[6]
        else:
            small_out[...] = (small_z[0] + small_z[1]) + (small_z[2] + small_z[3])

    def factor_copies():
        return [remote(ref.at[core], ref.at[core], 22 + k, twin) for k, ref in enumerate((fac_normed, fac_feed))]

    def factors_on():
        for copy in norm_z + feed_z:
            copy.wait_recv()
        for copy in factor_copies():
            copy.start()

    two = 2 * units
    summing = core == x

    def part_at(which):
        return pl.ds(pl.multiple_of(which * two, 16), two)

    def across_copy(k):
        return remote(hidden_grads.at[part_at(y if k else 1 - y)], hidden_in.at[k], 24 + k, at_x)

    def along_copy():
        return remote(hidden_grads.at[part_at(1 - y)], hidden_far, 26, at_y)

    def share_copy():
        return remote(hidden_share, hidden_got, 27, twin)

    def hidden_make():
        for copy in factor_copies():
            copy.wait()
        slot = z * 2 + core
        size = hidden_grads.shape[0]
        normed = fac_normed[...].reshape(8 * masks, model)
        feed = fac_feed[...].reshape(8 * masks, model)
        at = pl.ds(pl.multiple_of(slot * size, 128), size)
        act, slope = gelu_parts(dot(normed, wup_v[:, at]) + vecs[pl.ds(z, 1), mine])
        gp = (dot_nt(feed, wdown_v[at, :]) * slope).astype(BF16)
        hidden_grads[:, :model] = dot_tn(gp, normed).astype(BF16)
        hidden_grads[:, model:] = dot_tn(act.astype(BF16), feed).astype(BF16)

    def hidden_start(k):
        @pl.when(jnp.logical_not(summing))
        def _():
            across_copy(k).start()

    def hidden_arrive(k):
        @pl.when(jnp.logical_not(summing))
        def _():
            across_copy(k).wait_send()

        @pl.when(summing)
        def _():
            across_copy(k).wait_recv()
            if k == 0:
                here = part_at(1 - y)
                hidden_grads[here] = (hidden_grads[here].astype(F32) + hidden_in[0].astype(F32)).astype(BF16)
                along_copy().start()

    def hidden_sum():
        @pl.when(summing)
        def _():
            along_copy().wait()
            value = hidden_grads[part_at(y)].astype(F32) + hidden_in[1].astype(F32) + hidden_far[...].astype(F32)
            low_part, high_part = value[:units], value[units:]
            own = jnp.where(core == 0, low_part, high_part)
            hidden_share[...] = jnp.where(core == 0, high_part, low_part).astype(BF16)
            share_copy().start()
            up_out[...] = own[:, :model]
            down_out[...] = own[:, model:]

    def hidden_end():
        @pl.when(summing)
        def _():
            share_copy().wait_send()

        @pl.when(jnp.logical_not(summing))
        def _():
            share_copy().wait_recv()
            value = hidden_got[...].astype(F32)
            up_out[...] = value[:, :model]
            down_out[...] = value[:, model:]

    def piece_of(index):
        return pl.ds(index * piece, piece)

    def igrad_copy(index):
        return remote(igrad_send.at[piece_of(index)], igrad_in.at[piece_of(index)], 29 + index, at_y)

    def igrad_step():
        remote(dx_send, dx_in, 28, twin).wait_recv()
        input_grad[row] = input_grad[row] + dx_in[:stretch, :].astype(F32)
        igrad_send[...] = (input_grad[1 - row] + dx_in[stretch:, :].astype(F32)).astype(BF16)

    def igrad_end(index):
        igrad_copy(index).wait()
        input_grad[1 - row, piece_of(index)] = igrad_in[piece_of(index), :].astype(F32)

    def out_copy(index):
        return remote(out_send.at[piece_of(index)], layer_out.at[row, piece_of(index)], 32 + index, at_y)

    results = [
        (layer_out, layer_hbm), (input_grad, igrad_hbm), (out_o, hbm_o), (out_0, hbm_0), (out_1, hbm_1), (out_2, hbm_2),
        (up_out, up_hbm), (down_out, down_hbm), (small_out, small_hbm),
    ]

    def result_copy(index):
        src, dst = results[index]
        return pltpu.make_async_copy(src, dst, local_sem.at[20 + index])

    ended = []

    def act(name):
        start, kind, rest = name[0] == "S", name[1], [int(c) for c in name[2:]]
        ended.append(name)
        if kind in "rgt":
            (job_start if start else job_end)(kind, *rest)
            if kind == "t" and not start and {"Et%d0" % rest[0], "Et%d1" % rest[0]} <= set(ended):
                result_copy(2 + rest[0]).start()
        elif kind == "s":
            (small_start if start else small_end)(*rest)
            if not start and rest[0] == 3:
                result_copy(8).start()
        elif kind == "d":
            igrad_step()
        elif kind == "i":
            if start:
                igrad_copy(*rest).start()
            else:
                igrad_end(*rest)
                if {"Ei0", "Ei1"} <= set(ended):
                    result_copy(1).start()
        elif kind == "o":
            if start:
                out_copy(*rest).start()
            else:
                out_copy(*rest).wait()
                if {"Eo0", "Eo1"} <= set(ended):
                    result_copy(0).start()
        elif kind == "f":
            factors_on()
        elif kind == "H":
            hidden_make()
        elif kind == "h":
            (hidden_start if start else hidden_arrive)(*rest)
        elif kind == "k":
            hidden_sum()
        elif kind == "m":
            hidden_end()
            result_copy(6).start()
            result_copy(7).start()

    def act_on(name):
        for each in PLAN.get(name, ()):
            act(each)

    gb = gb_both[...].reshape(count, model)
    gctx = dot(gb, wo_t[...]).astype(BF16)
    grads[0] = dot_tn(gb, context[...]).astype(BF16)
    act_on("G0")
    for pair in range(pairs):
        lanes = slice(pair * 128, pair * 128 + 128)
        pair_keys, pair_values, pair_queries = keys[:, lanes], values_t[lanes, :], queries[:, lanes]
        pair_gctx = gctx[:, lanes]
        dqs, dks, dvs = [], [], []
        for side in range(2):
            keep = lane_is((count, 128), side * 64, side * 64 + 64)
            head_gctx = jnp.where(keep, pair_gctx.astype(F32), 0.0).astype(BF16)
            low_share = probs[pair * 2 + side]
            share = low_share.astype(F32)
            gp = dot(head_gctx, pair_values)
            spread = jnp.sum(share * gp, axis=-1, keepdims=True)
            gs = (share * (gp - spread)).astype(BF16)
            dqs.append(dot(gs, pair_keys))
            dks.append(dot_tn(gs, pair_queries))
            dvs.append(dot_tn(low_share, pair_gctx))
        first = lane_is((count, 128), 0, 64)
        dq = (jnp.where(first, dqs[0], dqs[1]) * 0.125).astype(BF16)
        dq_low[:, lanes] = dq
        first = lane_is((full, 128), 0, 64)
        dk = (jnp.where(first, dks[0], dks[1]) * 0.125).astype(BF16)
        dv = jnp.where(first, dvs[0], dvs[1]).astype(BF16)
        both = slice(pair * 256, pair * 256 + 256)
        dkv_low[:, pair * 256 : pair * 256 + 128] = dk
        dkv_low[:, pair * 256 + 128 : pair * 256 + 256] = dv
        grads[1 + pair, :, :128] = dot_tn(picked[...], dq).astype(BF16)
        grads[1 + pair, :, 128:] = dot(xs_t[...], dkv_low[:, both]).astype(BF16)
        act_on("p" + str(pair))
        there = pl.ds(pl.multiple_of(core * width + pair * 128, 128), 128)
        small_in[0, parts + 6 : parts + 7, there] = jnp.sum(dq.astype(F32), axis=0, keepdims=True)
        small_in[0, parts + 7 : parts + 8, there] = jnp.sum(dv.astype(F32), axis=0, keepdims=True)

    spread_rows = dot(dq_low[...], wq_t[...])
    zero = jnp.zeros((masks, model), F32)
    is_first = core == 0
    gh1 = grad_h1[...]
    spread_rows = spread_rows + jnp.concatenate([jnp.where(is_first, gh1, zero), jnp.where(is_first, zero, gh1)], axis=0)
    high = spread_rows.astype(BF16)
    rest = (spread_rows - high.astype(F32)).astype(BF16)
    for start in (half, half + stretch, 0, stretch):
        here = slice(start, start + stretch)
        value = dot_tn(chosen[:, here], high) + dot_tn(chosen[:, here], rest)
        value = value + dot(dkv_low[here, :], wkv_t[...])
        if start < half:
            input_grad[row if start == 0 else 1 - row] = value
        else:
            dx_send[start - half : start - half + stretch, :] = value.astype(BF16)
            if start > half:
                push(dx_send, dx_in, 28, twin)

    act_on("dx")

    def hooks(step, prefix, count):
        for at in range(count):
            if prefix + str(at) in PLAN:
                @pl.when(step == at)
                def _(at=at):
                    act_on(prefix + str(at))

    def ctx_copy():
        return remote(all_context.at[pl.ds(half, half)], ctx_in, 31, twin)

    def attend_step(step, carry):
        tile, pair = (step // pairs + 2) % 4, step % pairs
        here = pl.ds(pl.multiple_of(tile * stretch, stretch), stretch)
        lanes = pl.ds(pl.multiple_of(pair * 128, 128), 128)
        block = 2 * (y + (tile % 2) * (1 - 2 * y)) + core + (tile // 2) * (1 - 2 * core)
        place = lax.broadcasted_iota(jnp.int32, (stretch, 1), 0) + block * stretch
        seg_col = jnp.where(place.astype(F32) >= split, 1.0, 0.0)
        same_here = seg_col == seg_row
        pair_queries = all_queries[here, lanes].astype(F32)
        pair_keys, pair_values = keys_t[lanes, :], values[:, lanes]
        found = []
        for side in range(2):
            keep = lane_is((stretch, 128), side * 64, side * 64 + 64)
            head_queries = jnp.where(keep, pair_queries, 0.0).astype(BF16)
            scores = jnp.where(same_here, dot(head_queries, pair_keys), MASKED_SCORE)
            weights = jnp.exp(scores - jnp.max(scores, axis=-1, keepdims=True))
            found.append(dot(weights.astype(BF16), pair_values) / jnp.sum(weights, axis=-1, keepdims=True))
        first = lane_is((stretch, 128), 0, 64)
        all_context[here, lanes] = jnp.where(first, found[0], found[1]).astype(BF16)

        @pl.when(step == 2 * pairs - 1)
        def _():
            ctx_copy().start()

        hooks(step, "a", 4 * pairs)
        return carry

    lax.fori_loop(0, 4 * pairs, attend_step, 0)
    ctx_copy().wait()

    def feed_step(step, carry):
        tile, part = 1 - step // parts, step % parts
        here = pl.ds(pl.multiple_of(tile * stretch, stretch), stretch)

        @pl.when(part == 0)
        def _():
            left = jnp.where(is_first, all_context[here, :], ctx_in[here, :])
            right = jnp.where(is_first, ctx_in[here, :], all_context[here, :])
            here_branch = dot(left, wo_v[:width, :]) + dot(right, wo_v[width:, :]) + vector(6)
            normed, _ = norm_parts(xs[here, :].astype(F32) + here_branch)
            value = normed * vector(7) + vector(8)
            y1_keep[...] = value.astype(BF16)
            total[...] = value + vector(9)

        there = pl.ds(pl.multiple_of(part * model, model), model)
        pre = dot(y1_keep[...], wup_v[:, there]) + vecs[pl.ds(part, 1), :]
        total[...] += dot(gelu_only(pre).astype(BF16), wdown_v[there, :])

        @pl.when(part == parts - 1)
        def _():
            normed, _ = norm_parts(total[...])
            value = (normed * vector(10) + vector(11)).astype(BF16)

            @pl.when(tile == 1)
            def _():
                out_send[...] = value

            @pl.when(tile == 0)
            def _():
                layer_out[row] = value

        hooks(step, "f", 2 * parts)
        return carry

    lax.fori_loop(0, 2 * parts, feed_step, 0)
    act_on("end")
    for index in range(len(results)):
        result_copy(index).wait()
    for copy in pending:
        copy.wait_send()


def vmem(count):
    return [pl.BlockSpec(memory_space=pltpu.VMEM)] * count


def local_call(body, outs, name, scratch=()):
    def call(core, *operands):
        return pl.pallas_call(
            body,
            out_shape=outs,
            in_specs=[pl.BlockSpec(memory_space=pltpu.SMEM)] + vmem(len(operands)),
            out_specs=vmem(len(outs)),
            scratch_shapes=list(scratch),
            compiler_params=pltpu.CompilerParams(vmem_limit_bytes=VMEM_LIMIT),
            name=name,
        )(core, *operands)

    return call


def finish_kernel(parts, go, g0, g1, g2, layer_in, igrad_in, up_in, down_in, small_in, wq, wk, wv, wo, layer_out, igrad, up, down, up_bias, *rest):
    vectors, (go_v, pair_v, small, wide, wo_v, *through, in_sem, out_sem) = rest[:8], rest[8:]
    model = go_v.shape[0]
    width, tile = model // 2, 128
    steps = model // tile
    loads = [pltpu.make_async_copy(small_in, small, in_sem.at[0])]
    for step in range(steps):
        rows = pl.ds(step * tile, tile)
        for pair, ref in enumerate((g0, g1, g2)):
            loads.append(pltpu.make_async_copy(ref.at[rows], pair_v.at[pair, rows], in_sem.at[1 + step * 3 + pair]))
    loads.append(pltpu.make_async_copy(go, go_v, in_sem.at[1 + 3 * steps]))
    passed = tuple(zip((igrad_in, layer_in, up_in, down_in), through, (igrad, layer_out, up, down)))
    for index, (src, held, _) in enumerate(passed):
        loads.append(pltpu.make_async_copy(src, held, in_sem.at[2 + 3 * steps + index]))
    for copy in loads:
        copy.start()
    stores = []

    def store(src, dst):
        copy = pltpu.make_async_copy(src, dst, out_sem.at[len(stores)])
        copy.start()
        stores.append(copy)

    loads[0].wait()
    for part in range(parts):
        up_bias[part * model : (part + 1) * model] = small[part]
    for place, out in enumerate(vectors):
        out[...] = small[parts + place]
    for step in range(steps):
        rows = pl.ds(step * tile, tile)
        for pair in range(3):
            loads[1 + step * 3 + pair].wait()
            for core in range(2):
                to = core * width + pair * 128
                for place in range(3):
                    begin = core * width + place * 128
                    wide[place, rows, to : to + 128] = pair_v[pair, rows, begin : begin + 128].astype(F32)
        for place, out in enumerate((wq, wk, wv)):
            store(wide.at[place, rows], out.at[rows])
    for index, (_, held, dst) in enumerate(passed):
        loads[2 + 3 * steps + index].wait()
        store(held, dst)
    loads[1 + 3 * steps].wait()
    for step in range(steps):
        rows = pl.ds(step * tile, tile)
        wo_v[rows, :] = go_v[:, step * tile : (step + 1) * tile].T.astype(F32)
        store(wo_v.at[rows], wo.at[rows])
    for copy in stores:
        copy.wait()


def finish(layer_output, input_grad, go, g0, g1, g2, up_part, down_part, small, hidden):
    model = go.shape[0]
    parts, steps = hidden // model, model // 128
    shaped = jax.ShapeDtypeStruct
    square, vector = shaped((model, model), F32), shaped((model,), F32)
    far = pl.BlockSpec(memory_space=pltpu.HBM)
    found = pl.pallas_call(
        functools.partial(finish_kernel, parts),
        out_shape=(square,) * 4
        + (shaped(layer_output.shape, BF16), shaped(input_grad.shape, F32), shaped(up_part.shape, F32), shaped(down_part.shape, F32))
        + (shaped((hidden,), F32),)
        + (vector,) * 8,
        in_specs=[far] * 9,
        out_specs=[far] * 8 + vmem(9),
        scratch_shapes=[
            pltpu.VMEM((model, model), BF16),
            pltpu.VMEM((3, model, model), BF16),
            pltpu.VMEM(small.shape, F32),
            pltpu.VMEM((3, model, model), F32),
            pltpu.VMEM((model, model), F32),
            pltpu.VMEM(input_grad.shape, F32),
            pltpu.VMEM(layer_output.shape, BF16),
            pltpu.VMEM(up_part.shape, F32),
            pltpu.VMEM(down_part.shape, F32),
            pltpu.SemaphoreType.DMA((6 + 3 * steps,)),
            pltpu.SemaphoreType.DMA((4 + 4 * steps,)),
        ],
        compiler_params=pltpu.CompilerParams(vmem_limit_bytes=VMEM_LIMIT),
        name="finish",
    )(go, g0, g1, g2, layer_output, input_grad, up_part, down_part, small)
    wq, wk, wv, wo, layer_output, input_grad, up_part, down_part, up_bias, g1, s1, g2, s2, ob, db, qb, vb = found
    return layer_output, input_grad, wq, qb, wk, wv, vb, wo, ob, g1, s1, up_part.T, up_bias, down_part, db, g2, s2


def outputs(layer_output, input_grad, grad_wq, grad_wk, grad_wv, grad_wo, up_part, down_part, small):
    model = grad_wq.shape[0]
    base = small.shape[0] - 12
    vector = lambda index: small[index]
    return (
        layer_output,
        input_grad,
        grad_wq.astype(F32),
        vector(base + 6),
        grad_wk.astype(F32),
        grad_wv.astype(F32),
        vector(base + 7),
        grad_wo.astype(F32),
        vector(base + 4),
        vector(base),
        vector(base + 1),
        up_part.T,
        small[:base].reshape(-1),
        down_part,
        vector(base + 5),
        vector(base + 2),
        vector(base + 3),
    )


def layer_call(tokens, cotangent, segment_ids, mask_positions, vectors, weights):
    _, stretch, model = tokens.shape
    hidden = weights[4].shape[1]
    masks = mask_positions.shape[2]
    count, half, full, width = 2 * masks, 2 * stretch, 4 * stretch, model // 2
    units = hidden // 32
    shaped = jax.ShapeDtypeStruct
    low = lambda *shape: pltpu.VMEM(shape, BF16)
    wide = lambda *shape: pltpu.VMEM(shape, F32)
    results = [low(2, stretch, model), wide(2, stretch, model)] + [low(model, model)] * 4
    results += [wide(units, model), wide(units, model), wide(16, model)]
    scratch = results + [pltpu.VMEM(small.shape, small.dtype) for small in (segment_ids, mask_positions) + vectors]
    scratch += [
        wide(hidden // model + 8, model), low(width, model), low(model, model), low(model, width), low(width, full), low(width, full),
        low(full, model), low(model, full), low(2, stretch, model), low(2, 2, masks, model), low(2, masks, model), low(2, masks, model),
        low(masks, model), low(half, model), low(half, model), low(model, width), low(model, width), low(model, width), low(model, model),
        low(model, hidden), low(hidden, model), low(full, width), low(full, width), low(count, width), low(count, width),
        low(HEADS // 2, count, full), low(count, model), low(count, full), low(2, masks, width), low(2, masks, model),
        wide(hidden // model, masks, model), low(count, width), low(full, model), low(4, model, width),
        low(4 * units, 2 * model), low(2, 2 * units, 2 * model), low(2 * units, 2 * model), low(units, 2 * model), low(units, 2 * model), low(2, 4, masks, model), low(2, 4, masks, model),
        wide(masks, model), wide(7, 16, model), wide(4, 16, model),
        low(full, width), low(full, width), low(half, width), wide(stretch, model), low(stretch, model), low(stretch, model),
        low(stretch, model), low(stretch, model),
    ]
    scratch += [low(model - model // 16, width)] * 4
    scratch += [pltpu.SemaphoreType.DMA((32,)), pltpu.SemaphoreType.DMA((120,)), pltpu.SemaphoreType.DMA((120,))]
    anywhere = [pl.BlockSpec(memory_space=pltpu.HBM)]
    return pl.pallas_call(
        layer_kernel,
        out_shape=(
            shaped((2, stretch, model), BF16),
            shaped((2, stretch, model), F32),
            shaped((model, model), BF16),
            shaped((model, model), BF16),
            shaped((model, model), BF16),
            shaped((model, model), BF16),
            shaped((units, model), F32),
            shaped((units, model), F32),
            shaped((16, model), F32),
        ),
        in_specs=anywhere * (4 + len(vectors) + len(weights)),
        out_specs=anywhere * 9,
        scratch_shapes=scratch,
        compiler_params=pltpu.CompilerParams(collective_id=0, has_side_effects=True, vmem_limit_bytes=62 * 2**20),
        name="layer",
    )(tokens, cotangent, segment_ids, mask_positions, *vectors, *weights)


def on_device(
    rows_total,
    tokens,
    cotangent,
    segment_ids,
    mask_positions,
    query_weight,
    query_bias,
    key_weight,
    value_weight,
    value_bias,
    output_weight,
    output_bias,
    first_gain,
    first_shift,
    up_weight,
    up_bias,
    down_weight,
    down_bias,
    second_gain,
    second_shift,
):
    if rows_total == 8:
        vectors = (up_bias, query_bias, value_bias, output_bias, first_gain, first_shift, down_bias, second_gain, second_shift)
        weights = (query_weight, key_weight, value_weight, output_weight, up_weight, down_weight)
        found = layer_call(
            tokens, cotangent, segment_ids, mask_positions, vectors, weights
        )
        return finish(*found, up_weight.shape[1])
    _, stretch, model = tokens.shape
    hidden = up_weight.shape[1]
    width = model // 2
    heads = HEADS // 2
    masks = mask_positions.shape[2]
    seq = lax.axis_index("seq")
    row = seq // 2
    core = seq % 2
    across = [(i, (i + 2) % 4) for i in range(4)]
    beside = [(i, i + 1 - 2 * (i % 2)) for i in range(4)]

    def swap(value):
        return lax.ppermute(value, "seq", across)

    def trade(value):
        return lax.ppermute(value, "seq", beside)

    def take(array, index):
        return lax.dynamic_index_in_dim(array, index, 0, keepdims=False)

    half = jnp.concatenate([take(tokens, row), swap(take(tokens, 1 - row))], axis=0)
    peer = trade(half)
    cot_half = jnp.concatenate([take(cotangent, row), swap(take(cotangent, 1 - row))], axis=0)
    cot_peer = trade(cot_half)
    blocks = jnp.stack([2 * row + core, 2 * (1 - row) + core, 2 * row + 1 - core, 2 * (1 - row) + 1 - core])
    positions = (blocks[:, None] * stretch + jnp.arange(stretch, dtype=jnp.int32)[None, :]).reshape(-1)
    segments = jnp.take(take(segment_ids, row).reshape(4, stretch), blocks, axis=0).reshape(-1)
    slots = take(mask_positions, row).reshape(-1)
    pos, seg, slot_col = positions[None, :], segments[None, :], slots[:, None]
    pos_col, seg_col, slot_row = positions[:, None], segments[:, None], slots[None, :]
    core_scalar = core.reshape(1).astype(jnp.int32)
    line = lambda value: value.reshape(1, -1)
    full = 4 * stretch
    count = 2 * masks
    shaped = jax.ShapeDtypeStruct

    keys, values, queries, context, probs, picked = local_call(
        project_kernel,
        (
            shaped((full, width), BF16),
            shaped((full, width), BF16),
            shaped((count, width), BF16),
            shaped((count, width), BF16),
            shaped((heads, count, full), F32),
            shaped((count, model), BF16),
        ),
        "project",
    )(core_scalar, half, peer, pos, seg, slot_col, query_weight, line(query_bias), key_weight, value_weight, line(value_bias))

    two = context.reshape(2, masks, width)
    ctx_peer = trade(take(two, 1 - core))
    normed_low, feed, branch_low, grad_h1, small = local_call(
        masked_kernel,
        (
            shaped((masks, model), BF16),
            shaped((masks, model), BF16),
            shaped((masks, model), BF16),
            shaped((masks, model), F32),
            shaped((16, model), F32),
        ),
        "masked",
    )(
        core_scalar, take(two, core), ctx_peer, picked, cot_half, cot_peer, pos, slot_col, output_weight, line(output_bias),
        line(first_gain), line(first_shift), up_weight, line(up_bias), down_weight, line(down_bias), line(second_gain), line(second_shift),
    )
    branch_peer = trade(branch_low)
    grads, igrad_own, igrad_peer, bias = local_call(
        back_kernel,
        (
            shaped((4, model, width), BF16),
            shaped((2 * stretch, model), F32),
            shaped((2 * stretch, model), BF16),
            shaped((2, width), F32),
        ),
        "back",
        [pltpu.VMEM((count, width), BF16), pltpu.VMEM((full, width), BF16), pltpu.VMEM((full, width), BF16)],
    )(
        core_scalar, keys, values, queries, context, probs, picked, branch_low, branch_peer, grad_h1, half, peer, pos_col, slot_row,
        query_weight, key_weight, value_weight, output_weight,
    )
    igrad = igrad_own + trade(igrad_peer).astype(F32)
    igrad_other = swap(igrad[stretch:].astype(BF16)).astype(F32)
    igrad_mine = igrad[:stretch]
    input_grad = jnp.where(row == 0, jnp.stack([igrad_mine, igrad_other]), jnp.stack([igrad_other, igrad_mine]))

    ctx_own, ctx_other = local_call(
        attend_kernel, (shaped((2 * stretch, width), BF16), shaped((2 * stretch, width), BF16)), "attend"
    )(core_scalar, half, peer, seg, seg_col, keys, values, query_weight, line(query_bias))
    out_mine, out_other = local_call(
        feed_kernel, (shaped((stretch, model), BF16), shaped((stretch, model), BF16)), "feed"
    )(
        core_scalar, ctx_own, trade(ctx_other), half, output_weight, line(output_bias), line(first_gain), line(first_shift),
        up_weight, line(up_bias), down_weight, line(down_bias), line(second_gain), line(second_shift),
    )
    out_other = swap(out_other)
    layer_output = jnp.where(row == 0, jnp.stack([out_mine, out_other]), jnp.stack([out_other, out_mine]))

    wide = jnp.zeros((2, model), F32)
    bias_rows = lax.dynamic_update_slice(wide, bias, (0, core * width))
    base = hidden // model + 6
    small = jnp.concatenate([small[:base], bias_rows, small[base + 2 :]], axis=0)

    both = ("rows", "seq")
    small = lax.psum(small, both)
    zero = jnp.zeros((model, model), F32)
    wide_grads = [lax.dynamic_update_slice(zero, grads[k].astype(F32), (0, core * width)) for k in (1, 2, 3)]
    rows_wo = grads[0].reshape(2, width, width).transpose(1, 0, 2).reshape(width, model).astype(F32)
    wide_grads.append(lax.dynamic_update_slice(zero, rows_wo, (core * width, 0)))
    grad_wq, grad_wk, grad_wv, grad_wo = lax.psum(tuple(wide_grads), both)
    pieces = []
    units = hidden // 8
    for part in range(8):
        (piece,) = local_call(hidden_kernel, (shaped((units, 2 * model), BF16),), "hidden")(
            jnp.full((1,), part, jnp.int32), normed_low, feed, up_weight, line(up_bias), down_weight
        )
        pieces.append(piece.astype(F32))
    hidden_grads = lax.psum_scatter(jnp.concatenate(pieces, axis=0), both, scatter_dimension=0, tiled=True)

    up_part, down_part = hidden_grads[:, :model], hidden_grads[:, model:]
    return outputs(layer_output, input_grad, grad_wq, grad_wk, grad_wv, grad_wo, up_part, down_part, small)


def solution(mesh):
    split = P("rows", "seq", None)
    in_specs = (split, split, P("rows", None), P("rows", None, None)) + (P(),) * 15
    out_specs = (split, split) + (P(),) * 9 + (P(None, ("rows", "seq")), P(), P(("rows", "seq"), None), P(), P(), P())
    return jax.shard_map(
        functools.partial(on_device, mesh.shape["rows"]), mesh=mesh, in_specs=in_specs, out_specs=out_specs, check_vma=False
    )
```

```python
import functools

import jax
import jax.numpy as jnp
from jax import lax
from jax.experimental import pallas as pl
from jax.experimental.pallas import tpu as pltpu
from jax.sharding import PartitionSpec as P

HEADS = 12
EPSILON = 1e-12
MASKED_SCORE = -1000000000.0
F32 = jnp.float32
BF16 = jnp.bfloat16
MESH = pl.DeviceIdType.MESH
VMEM_LIMIT = 56 * 2**20
ORDERS = ("xyz", "yxz", "xyz", "xyz")
PLAN = {
    "p0": ("Sr10", "Sr11"),
    "p1": ("Sr20", "Sr21"),
    "G0": ("Sr02",),
    "p2": ("Sr30", "Sr31", "Er10", "Sr12"),
    "dx": ("Ss0", "Er11", "Er20", "Sr22"),
    "a0": ("Er21", "Er02", "Sr03"),
    "a1": ("Ed", "Si0", "Es0", "Ss1", "Ef", "Er30", "Sr32"),
    "a2": ("Er22", "Sr23"),
    "a3": ("Er31", "Er03", "Sg03", "EH", "Sh0", "Si1", "Es1", "Ss2", "Er12", "Sr13", "Er23", "Sg23", "Ei0"),
    "a4": ("Er32", "Sr33", "Eg03", "Sg00", "Sg02"),
    "a6": ("Er13", "Sg13"),
    "a7": ("Ei1",),
    "a8": ("Sh1", "Es2", "Ss3", "Eh0", "Eg23", "Sg20", "Sg22"),
    "a9": ("Eg02", "St00", "Sg01"),
    "a10": ("Er33", "Sg33", "Eg00", "Et00"),
    "f0": ("Eg13", "Sg10", "Sg12"),
    "f2": ("Es3", "Eh1", "Ek"),
    "f3": ("So0", "Eg22", "St20", "Sg21"),
    "f4": ("Em", "Eg33", "Sg30", "Sg32", "Et20", "Eg20"),
    "f5": ("Eg10",),
    "f6": ("Eg01", "St01"),
    "end": ("Et01", "So1", "Eo0", "Eg12", "St10", "Sg11", "Et10", "Eg32", "St30", "Sg31", "Eg21", "St21", "Et30", "Et21", "Eg30", "Eo1", "Eg31", "St31", "Eg11", "St11", "Et31", "Et11"),
}


def dot(left, right):
    return lax.dot_general(left, right, (((1,), (0,)), ((), ())), preferred_element_type=F32)


def dot_nt(left, right):
    return lax.dot_general(left, right, (((1,), (1,)), ((), ())), preferred_element_type=F32)


def dot_tn(left, right):
    return lax.dot_general(left, right, (((0,), (0,)), ((), ())), preferred_element_type=F32)


def norm_parts(hidden):
    centred = hidden - jnp.mean(hidden, axis=-1, keepdims=True)
    variance = jnp.mean(centred * centred, axis=-1, keepdims=True)
    scale = lax.rsqrt(variance + EPSILON)
    return centred * scale, scale


def norm_back(grad, normed, scale, gain):
    scaled = grad * gain
    along = jnp.mean(scaled * normed, axis=-1, keepdims=True)
    return (scaled - jnp.mean(scaled, axis=-1, keepdims=True) - normed * along) * scale


GELU_A = 0.7978845608028654
GELU_B = 0.044715


def gelu_parts(value):
    square = value * value
    bent = jnp.tanh(GELU_A * value * (1.0 + GELU_B * square))
    half = 0.5 * (1.0 + bent)
    slope = half + 0.5 * value * (1.0 - bent * bent) * (GELU_A * (1.0 + 3.0 * GELU_B * square))
    return value * half, slope


def gelu_only(value):
    bent = jnp.tanh(GELU_A * value * (1.0 + GELU_B * value * value))
    return 0.5 * value * (1.0 + bent)


def lane_is(shape, low, high):
    lane = lax.broadcasted_iota(jnp.int32, shape, len(shape) - 1)
    return (lane >= low) & (lane < high)


def project_kernel(core, half, peer, pos, seg, slots, wq, bq, wk, wv, bv, keys, values, queries, context, probs, picked):
    width = keys.shape[1]
    mine = pl.ds(pl.multiple_of(core[0] * width, 128), width)
    count = slots.shape[0]
    tokens_half = half.shape[0]
    chosen = jnp.where(slots[...] == pos[...], 1.0, 0.0).astype(BF16)
    rows = dot(chosen[:, :tokens_half], half[...]) + dot(chosen[:, tokens_half:], peer[...])
    rows = rows.astype(BF16)
    picked[...] = rows
    queries[...] = (dot(rows, wq[:, mine]) + bq[:, mine]).astype(BF16)
    for place, part in ((0, half), (tokens_half, peer)):
        for start in range(0, tokens_half, 256):
            block = part[start : start + 256, :]
            there = slice(place + start, place + start + 256)
            keys[there, :] = dot(block, wk[:, mine]).astype(BF16)
            values[there, :] = (dot(block, wv[:, mine]) + bv[:, mine]).astype(BF16)
    sequence = lax.broadcasted_iota(jnp.int32, (count, 1), 0) // (count // 2)
    same = seg[...] == sequence
    for pair in range(width // 128):
        lanes = slice(pair * 128, pair * 128 + 128)
        pair_queries = queries[:, lanes].astype(F32) * 0.125
        pair_keys, pair_values = keys[:, lanes], values[:, lanes]
        outs = []
        for side in range(2):
            keep = lane_is((count, 128), side * 64, side * 64 + 64)
            head_queries = jnp.where(keep, pair_queries, 0.0).astype(BF16)
            scores = jnp.where(same, dot_nt(head_queries, pair_keys), MASKED_SCORE)
            weights = jnp.exp(scores - jnp.max(scores, axis=-1, keepdims=True))
            share = weights / jnp.sum(weights, axis=-1, keepdims=True)
            probs[pair * 2 + side] = share
            outs.append(dot(share.astype(BF16), pair_values))
        first = lane_is((count, 128), 0, 64)
        context[:, lanes] = jnp.where(first, outs[0], outs[1]).astype(BF16)


def masked_kernel(core, ctx_own, ctx_peer, picked, cot_half, cot_peer, pos, slots, wo, bo, g1, s1, wup, bup, wdown, bdown, g2, s2, normed_low, feed, branch_low, grad_h1, small):
    count, width = ctx_own.shape
    hidden = wup.shape[1]
    model = wup.shape[0]
    tokens_half = cot_half.shape[0]
    mine = pl.multiple_of(core[0] * count, 16)
    is_first = core[0] == 0
    left = jnp.where(is_first, ctx_own[...], ctx_peer[...])
    right = jnp.where(is_first, ctx_peer[...], ctx_own[...])
    branch = dot(left, wo[:width, :]) + dot(right, wo[width:, :]) + bo[...]
    h1 = picked[pl.ds(mine, count), :].astype(F32) + branch
    n1, r1 = norm_parts(h1)
    y1 = n1 * g1[...] + s1[...]
    y1_low = y1.astype(BF16)
    normed_low[...] = y1_low
    total = y1 + bdown[...]
    slopes = []
    step = model
    for start in range(0, hidden, step):
        pre = dot(y1_low, wup[:, start : start + step]) + bup[:, start : start + step]
        act, slope = gelu_parts(pre)
        slopes.append(slope)
        total = total + dot(act.astype(BF16), wdown[start : start + step, :])
    n2, r2 = norm_parts(total)
    chosen = jnp.where(slots[pl.ds(mine, count), :] == pos[...], 1.0, 0.0).astype(BF16)
    grad = dot(chosen[:, :tokens_half], cot_half[...]) + dot(chosen[:, tokens_half:], cot_peer[...])
    gh2 = norm_back(grad, n2, r2, g2[...])
    gf = gh2.astype(BF16)
    feed[...] = gf
    gy1 = gh2
    small[...] = jnp.zeros_like(small)
    for place, start in enumerate(range(0, hidden, step)):
        ga = dot_nt(gf, wdown[start : start + step, :])
        gp = (ga * slopes[place]).astype(BF16)
        small[place : place + 1, :] = jnp.sum(gp.astype(F32), axis=0, keepdims=True)
        gy1 = gy1 + dot_nt(gp, wup[:, start : start + step])
    gh1 = norm_back(gy1, n1, r1, g1[...])
    grad_h1[...] = gh1
    gb = gh1.astype(BF16)
    branch_low[...] = gb
    base = hidden // step
    for place, value in enumerate((gy1 * n1, gy1, grad * n2, grad, gb.astype(F32), gf.astype(F32))):
        small[base + place : base + place + 1, :] = jnp.sum(value, axis=0, keepdims=True)


def back_kernel(core, keys, values, queries, context, probs, picked, gb_own, gb_peer, gh1, half, peer, pos_col, slots_row, wq, wk, wv, wo, grads, igrad_own, igrad_peer, bias, dq_low, dk_low, dv_low):
    width = keys.shape[1]
    count = queries.shape[0]
    own = gb_own.shape[0]
    tokens_half = half.shape[0]
    is_first = core[0] == 0
    mine = pl.ds(pl.multiple_of(core[0] * width, 128), width)
    mine_rows = pl.ds(pl.multiple_of(core[0] * width, 128), width)
    top = jnp.where(is_first, gb_own[...], gb_peer[...])
    low = jnp.where(is_first, gb_peer[...], gb_own[...])
    gb = jnp.concatenate([top, low], axis=0)
    gctx = dot_nt(gb, wo[mine_rows, :]).astype(BF16)
    for pair in range(width // 128):
        lanes = slice(pair * 128, pair * 128 + 128)
        pair_keys, pair_values, pair_queries = keys[:, lanes], values[:, lanes], queries[:, lanes]
        pair_gctx = gctx[:, lanes]
        dqs, dks, dvs = [], [], []
        for side in range(2):
            keep = lane_is((count, 128), side * 64, side * 64 + 64)
            head_gctx = jnp.where(keep, pair_gctx.astype(F32), 0.0).astype(BF16)
            share = probs[pair * 2 + side]
            gp = dot_nt(head_gctx, pair_values)
            spread = jnp.sum(share * gp, axis=-1, keepdims=True)
            gs = (share * (gp - spread)).astype(BF16)
            dqs.append(dot(gs, pair_keys))
            dks.append(dot_tn(gs, pair_queries))
            dvs.append(dot_tn(share.astype(BF16), pair_gctx))
        first = lane_is((count, 128), 0, 64)
        dq_low[:, lanes] = (jnp.where(first, dqs[0], dqs[1]) * 0.125).astype(BF16)
        first = lane_is((2 * tokens_half, 128), 0, 64)
        dk_low[:, lanes] = (jnp.where(first, dks[0], dks[1]) * 0.125).astype(BF16)
        dv_low[:, lanes] = jnp.where(first, dvs[0], dvs[1]).astype(BF16)
    grads[1] = dot_tn(picked[...], dq_low[...]).astype(BF16)
    gwo = dot_tn(context[...], gb).astype(BF16)
    grads[0, :width, :] = gwo[:, :width]
    grads[0, width:, :] = gwo[:, width:]
    for place, part in ((2, dk_low), (3, dv_low)):
        total = dot_tn(half[...], part[:tokens_half, :]) + dot_tn(peer[...], part[tokens_half:, :])
        grads[place] = total.astype(BF16)
    bias[0:1, :] = jnp.sum(dq_low[...].astype(F32), axis=0, keepdims=True)
    bias[1:2, :] = jnp.sum(dv_low[...].astype(F32), axis=0, keepdims=True)
    spread_rows = dot_nt(dq_low[...], wq[:, mine])
    zero = jnp.zeros((own, wq.shape[0]), F32)
    spread_rows = spread_rows + jnp.concatenate(
        [jnp.where(is_first, gh1[...], zero), jnp.where(is_first, zero, gh1[...])], axis=0
    )
    high = spread_rows.astype(BF16)
    rest = (spread_rows - high.astype(F32)).astype(BF16)
    for start in range(0, 2 * tokens_half, 256):
        here = slice(start, start + 256)
        chosen = jnp.where(pos_col[here, :] == slots_row[...], 1.0, 0.0).astype(BF16)
        total = dot(chosen, high) + dot(chosen, rest)
        total = total + dot_nt(dk_low[here, :], wk[:, mine]) + dot_nt(dv_low[here, :], wv[:, mine])
        if start < tokens_half:
            igrad_own[here, :] = total
        else:
            igrad_peer[start - tokens_half : start - tokens_half + 256, :] = total.astype(BF16)


def attend_kernel(core, half, peer, seg, seg_col, keys, values, wq, bq, own, other):
    width = keys.shape[1]
    mine = pl.ds(pl.multiple_of(core[0] * width, 128), width)
    tile = 256
    for part, out in ((half, own), (peer, other)):
        place = 0 if part is half else half.shape[0]

        def body(step, carry, part=part, out=out, place=place):
            here = pl.ds(pl.multiple_of(step * tile, tile), tile)
            queries = (dot(part[here, :], wq[:, mine]) + bq[:, mine]).astype(BF16).astype(F32) * 0.125
            same = seg_col[pl.ds(pl.multiple_of(place + step * tile, tile), tile), :] == seg[...]
            for pair in range(width // 128):
                lanes = slice(pair * 128, pair * 128 + 128)
                outs = []
                for side in range(2):
                    keep = lane_is((tile, 128), side * 64, side * 64 + 64)
                    head_queries = jnp.where(keep, queries[:, lanes], 0.0).astype(BF16)
                    scores = jnp.where(same, dot_nt(head_queries, keys[:, lanes]), MASKED_SCORE)
                    weights = jnp.exp(scores - jnp.max(scores, axis=-1, keepdims=True))
                    total = jnp.sum(weights, axis=-1, keepdims=True)
                    outs.append(dot(weights.astype(BF16), values[:, lanes]) / total)
                first = lane_is((tile, 128), 0, 64)
                out[here, lanes] = jnp.where(first, outs[0], outs[1]).astype(BF16)
            return carry

        lax.fori_loop(0, part.shape[0] // tile, body, 0)


def feed_kernel(core, ctx_own, ctx_peer, half, wo, bo, g1, s1, wup, bup, wdown, bdown, g2, s2, own, other):
    width = ctx_own.shape[1]
    hidden, model = wdown.shape
    is_first = core[0] == 0
    tile = own.shape[0]
    for start, out in ((0, own), (tile, other)):
        here = slice(start, start + tile)
        left = jnp.where(is_first, ctx_own[here, :], ctx_peer[here, :])
        right = jnp.where(is_first, ctx_peer[here, :], ctx_own[here, :])
        branch = dot(left, wo[:width, :]) + dot(right, wo[width:, :]) + bo[...]
        n1, _ = norm_parts(half[here, :].astype(F32) + branch)
        y1 = n1 * g1[...] + s1[...]
        y1_low = y1.astype(BF16)
        total = y1 + bdown[...]
        for place in range(0, hidden, model):
            pre = dot(y1_low, wup[:, place : place + model]) + bup[:, place : place + model]
            total = total + dot(gelu_only(pre).astype(BF16), wdown[place : place + model, :])
        n2, _ = norm_parts(total)
        out[...] = (n2 * g2[...] + s2[...]).astype(BF16)


def hidden_kernel(slot, normed, feed, wup, bup, wdown, out):
    units = out.shape[0]
    model = normed.shape[1]
    mine = pl.ds(pl.multiple_of(slot[0] * units, 128), units)
    pre = dot(normed[...], wup[:, mine]) + bup[:, mine]
    act, slope = gelu_parts(pre)
    ga = dot_nt(feed[...], wdown[mine, :])
    gp = (ga * slope).astype(BF16)
    out[:, :model] = dot_tn(gp, normed[...]).astype(BF16)
    out[:, model:] = dot_tn(act.astype(BF16), feed[...]).astype(BF16)


def place_here():
    row, seq = lax.axis_index("rows"), lax.axis_index("seq")
    return row // 2, row % 2, seq // 2, seq % 2


def device(z, x, y, core):
    return (z * 2 + x, y * 2 + core)


def layer_kernel(
    tokens, cotangent, segments_in, slots_in, up_bias_in, bq_in, bv_in, bo_in, g1_in, s1_in, bdown_in, g2_in, s2_in, wq, wk, wv, wo, wup, wdown,
    layer_hbm, igrad_hbm, hbm_o, hbm_0, hbm_1, hbm_2, up_hbm, down_hbm, small_hbm,
    layer_out, input_grad, out_o, out_0, out_1, out_2, up_out, down_out, small_out,
    segments, slots, up_bias, bq, bv, bo, g1, s1, bdown, g2, s2, vecs, wq_t, wkv_t, wo_t, keys_t, values_t,
    xs, xs_t, cots, cot_part, cot_in, cot_sum, cot_far, dx_send, dx_in, wq_v, wk_v, wv_v, wo_v, wup_v, wdown_v, keys, values, queries, context, probs, picked, chosen, ctx_both, ctx_far, gb_both, gb_far,
    slopes, dq_low, dkv_low, grads, hidden_grads, hidden_in, hidden_far, hidden_share, hidden_got, fac_normed, fac_feed, grad_h1, small_in, small_z,
    all_queries, all_context, ctx_in, total, y1_keep, out_send, igrad_send, igrad_in,
    in_o, in_0, in_1, in_2, local_sem, send_sem, recv_sem,
):
    z, x, y, core = place_here()
    row = y
    stretch, model = tokens.shape[1:]
    half = 2 * stretch
    full = 2 * half
    width = wq_v.shape[1]
    masks = slots.shape[2]
    count = 2 * masks
    hidden = wup.shape[1]
    parts = hidden // model
    units = down_out.shape[0]
    others = [(z + k) % 4 for k in (1, 2, 3)]
    at_y, at_x, twin = device(z, x, 1 - y, core), device(z, 1 - x, y, core), device(z, x, y, 1 - core)
    columns = [device(o, x, y, core) for o in others]
    mine = pl.ds(pl.multiple_of(core * width, 128), width)
    my_slots = pl.ds(pl.multiple_of(core * masks, 16), masks)
    twin_slots = pl.ds(pl.multiple_of((1 - core) * masks, 16), masks)
    pending = []

    def local(src, dst, index):
        copy = pltpu.make_async_copy(src, dst, local_sem.at[index])
        copy.start()
        return copy

    def remote(src, dst, index, target):
        return pltpu.make_async_remote_copy(
            src_ref=src, dst_ref=dst, send_sem=send_sem.at[index], recv_sem=recv_sem.at[index],
            device_id=target, device_id_type=MESH,
        )

    def push(src, dst, index, target):
        copy = remote(src, dst, index, target)
        copy.start()
        pending.append(copy)
        return copy

    def vector(index):
        return vecs[index : index + 1, :]

    def half_vector(index):
        return vecs[index : index + 1, mine]

    small_pairs = (
        (segments_in, segments), (slots_in, slots), (up_bias_in, up_bias), (bq_in, bq), (bv_in, bv), (bo_in, bo), (g1_in, g1),
        (s1_in, s1), (bdown_in, bdown), (g2_in, g2), (s2_in, s2),
    )
    own_tokens = local(tokens.at[row], xs.at[pl.ds(0, stretch)], 0)
    get_wk = local(wk.at[:, mine], wk_v, 1)
    get_wv = local(wv.at[:, mine], wv_v, 2)
    get_small = [local(src, dst, 8 + k) for k, (src, dst) in enumerate(small_pairs)]
    get_wq = local(wq.at[:, mine], wq_v, 3)
    own_cot = local(cotangent, cots, 4)
    get_wo = local(wo, wo_v, 5)
    get_up = local(wup, wup_v, 6)
    get_down = local(wdown, wdown_v, 7)

    greeted = [twin, at_x, at_y] + columns
    barrier = pltpu.get_barrier_semaphore()
    for target in greeted:
        pl.semaphore_signal(barrier, inc=1, device_id=target, device_id_type=MESH)
    pl.semaphore_wait(barrier, len(greeted))

    piece = stretch // 2
    tok_y = [
        push(tokens.at[1 - row, pl.ds(k * piece, piece)], xs.at[pl.ds(stretch + k * piece, piece)], k, at_y) for k in range(2)
    ]
    tok_c = push(tokens.at[row], xs.at[pl.ds(half, stretch)], 2, twin)

    for copy in get_small:
        copy.wait()
    for part in range(parts):
        vecs[part : part + 1, :] = up_bias[part * model : (part + 1) * model].reshape(1, model)
    for place, value in enumerate((bq, bv, bo, g1, s1, bdown, g2, s2)):
        vecs[parts + place : parts + place + 1, :] = value[...].reshape(1, model)

    def key_values(start):
        here = pl.ds(start, stretch)
        block = xs[here, :]
        block_keys = dot(block, wk_v[...]).astype(BF16)
        block_values = (dot(block, wv_v[...]) + half_vector(5)).astype(BF16)
        keys[here, :] = block_keys
        values[here, :] = block_values
        keys_t[:, here] = block_keys.T

    def turn_tokens(start):
        here = pl.ds(start, stretch)
        xs_t[:, here] = xs[here, :].T
        values_t[:, here] = values[here, :].T

    blocks = [2 * y + core, 2 * (1 - y) + core, 2 * y + 1 - core, 2 * (1 - y) + 1 - core]
    lane = lax.broadcasted_iota(jnp.int32, (1, stretch), 1)
    pos_row = jnp.concatenate([lane + block * stretch for block in blocks], axis=1)
    seg_here = segments[pl.ds(row, 1), :]
    split = jnp.sum((1 - seg_here).astype(F32), axis=1, keepdims=True)
    pos_row = pos_row.astype(F32)
    seg_row = jnp.where(pos_row >= split, 1.0, 0.0)
    diagonal = lax.broadcasted_iota(jnp.int32, (masks, masks), 0) == lax.broadcasted_iota(jnp.int32, (masks, masks), 1)

    def slot_column(which, sequence):
        line = slots[which].astype(F32)[sequence : sequence + 1, :]
        return jnp.sum(jnp.where(diagonal, line, 0.0), axis=1, keepdims=True)

    for sequence in range(2):
        column = slot_column(row, sequence)
        chosen[sequence * masks : (sequence + 1) * masks, :] = jnp.where(column == pos_row, 1.0, 0.0).astype(BF16)
    own_cot.wait()
    for sequence in range(2):
        here = chosen[sequence * masks : (sequence + 1) * masks, :stretch]
        cot_part[0, sequence] = dot(here, cots[row]).astype(BF16)
        there = jnp.where(slot_column(1 - row, sequence) == pos_row[:, :stretch], 1.0, 0.0).astype(BF16)
        cot_part[1, sequence] = dot(there, cots[1 - row]).astype(BF16)
    cot_c = push(cot_part.at[:, 1 - core], cot_in, 4, twin)

    own_tokens.wait()
    get_wk.wait()
    get_wv.wait()
    key_values(0)
    tok_c.wait_recv()
    key_values(half)
    turn_tokens(0)
    turn_tokens(half)
    get_wq.wait()
    for pair in range(width // 128):
        lanes = slice(pair * 128, pair * 128 + 128)
        wkv_t[pair * 256 : pair * 256 + 128, :] = wk_v[:, lanes].T
        wkv_t[pair * 256 + 128 : pair * 256 + 256, :] = wv_v[:, lanes].T
    wq_t[...] = wq_v[...].T
    forward = []
    for k in range(2):
        tok_y[k].wait_recv()
        src = xs.at[pl.ds(stretch + k * piece, piece)]
        forward.append(push(src, xs.at[pl.ds(half + stretch + k * piece, piece)], 5 + k, twin))
    cot_c.wait_recv()
    cot_sum[...] = cot_part[:, core] + cot_in[...]
    cot_y = push(cot_sum.at[1], cot_far, 3, at_y)
    key_values(stretch)
    for copy in forward:
        copy.wait_recv()
    key_values(half + stretch)

    rows = dot(chosen[...], xs[...]).astype(BF16)
    picked[...] = rows
    queries[...] = (dot(rows, wq_v[...]) + half_vector(4)).astype(BF16)
    sequence = lax.broadcasted_iota(jnp.int32, (count, 1), 0) // masks
    same = seg_row == sequence.astype(F32)
    pairs = width // 128
    for pair in range(pairs):
        lanes = slice(pair * 128, pair * 128 + 128)
        pair_queries = queries[:, lanes].astype(F32) * 0.125
        pair_keys, pair_values = keys_t[lanes, :], values[:, lanes]
        outs = []
        for side in range(2):
            keep = lane_is((count, 128), side * 64, side * 64 + 64)
            head_queries = jnp.where(keep, pair_queries, 0.0).astype(BF16)
            scores = jnp.where(same, dot(head_queries, pair_keys), MASKED_SCORE)
            weights = jnp.exp(scores - jnp.max(scores, axis=-1, keepdims=True))
            share = weights / jnp.sum(weights, axis=-1, keepdims=True)
            share = share.astype(BF16)
            probs[pair * 2 + side] = share
            outs.append(dot(share, pair_values))
        first = lane_is((count, 128), 0, 64)
        context[:, lanes] = jnp.where(first, outs[0], outs[1]).astype(BF16)
    ctx_both[core] = context[my_slots, :]
    ctx_c = push(context.at[twin_slots], ctx_both.at[core], 7, twin)
    ctx_x = push(context, ctx_far, 34, at_x)

    turn_tokens(stretch)
    turn_tokens(half + stretch)
    get_wo.wait()
    wo_t[...] = wo_v[mine, :].T
    ctx_c.wait_recv()

    branch = dot(ctx_both[0], wo_v[:width, :]) + dot(ctx_both[1], wo_v[width:, :]) + vector(6)
    n1, r1 = norm_parts(picked[my_slots, :].astype(F32) + branch)
    y1 = n1 * vector(7) + vector(8)
    y1_low = y1.astype(BF16)
    fac_normed[core, z] = y1_low
    spot = fac_normed.at[core, z]
    norm_z = [push(spot, spot, 9 + k, columns[k]) for k in range(3)]
    get_up.wait()
    get_down.wait()
    sum2 = y1 + vector(9)
    for part in range(parts):
        there = slice(part * model, (part + 1) * model)
        act, slope = gelu_parts(dot(y1_low, wup_v[:, there]) + vector(part))
        slopes[part] = slope
        sum2 = sum2 + dot(act.astype(BF16), wdown_v[there, :])
    n2, r2 = norm_parts(sum2)
    cot_y.wait_recv()
    grad = cot_sum[0].astype(F32) + cot_far[...].astype(F32)
    gh2 = norm_back(grad, n2, r2, vector(10))
    gf = gh2.astype(BF16)
    fac_feed[core, z] = gf
    spot = fac_feed.at[core, z]
    feed_z = [push(spot, spot, 12 + k, columns[k]) for k in range(3)]
    gf_t = gf.T
    gy1_t = jnp.zeros((model, masks), F32)
    small_in[0] = jnp.zeros(small_in.shape[1:], F32)
    for part in range(parts):
        there = slice(part * model, (part + 1) * model)
        gp = (dot(wdown_v[there, :], gf_t).T * slopes[part]).astype(BF16)
        small_in[0, part : part + 1, :] = jnp.sum(gp.astype(F32), axis=0, keepdims=True)
        gy1_t = gy1_t + dot(wup_v[:, there], gp.T)
    gy1 = gh2 + gy1_t.T
    gh1 = norm_back(gy1, n1, r1, vector(7))
    grad_h1[...] = gh1
    gb = gh1.astype(BF16)
    gb_both[core] = gb
    gb_c = push(gb_both.at[core], gb_both.at[core], 15, twin)
    for start in range(0, full, stretch):
        value = (dot(xs[start : start + stretch, :], wq_v[...]) + half_vector(4)).astype(BF16)
        all_queries[start : start + stretch, :] = (value.astype(F32) * 0.125).astype(BF16)
    for place, value in enumerate((gy1 * n1, gy1, grad * n2, grad, gb.astype(F32), gf.astype(F32))):
        small_in[0, parts + place : parts + place + 1, :] = jnp.sum(value, axis=0, keepdims=True)
    gb_c.wait_recv()
    far_half = pl.ds(pl.multiple_of((1 - x) * width, 128), width)
    gb_x = push(gb_both.at[:, :, far_half], gb_far, 35, at_x)

    spots = {"x": x, "y": y}
    neighbours = {"x": at_x, "y": at_y}
    ins = [in_o, in_0, in_1, in_2]
    outs = [out_o, out_0, out_1, out_2]
    half_rows, quarter, chunk = model // 2, model // 4, model // 16

    def rows_of(job):
        p1, p2 = (spots[dim] for dim in ORDERS[job][:2])
        kept, gone = p1 * half_rows, (1 - p1) * half_rows
        return kept, kept + p2 * quarter, kept + (1 - p2) * quarter, kept + p2 * quarter + z * chunk, gone + (1 - p2) * quarter, gone + p2 * quarter

    def at(start, size):
        return pl.ds(pl.multiple_of(start, 16), size)

    def job_copies(kind, job, stage):
        first, second = (neighbours[dim] for dim in ORDERS[job][:2])
        kept, mine_at, pass_at, own, gone_pass, gone_keep = rows_of(job)
        source, arrive, out = grads.at[job], ins[job], outs[job]
        base = 40 + job * 16

        def spread(start, size, index, target):
            spot = out.at[at(start, size), mine]
            return remote(spot, spot, base + index, target)

        if kind == "r" and stage == 0:
            return [remote(source.at[at(gone_pass, quarter)], arrive.at[pl.ds(0, quarter)], base, first)]
        if kind == "r" and stage == 1:
            return [remote(source.at[at(gone_keep, quarter)], arrive.at[pl.ds(quarter, quarter)], base + 1, first)]
        if kind == "r" and stage == 2:
            return [remote(source.at[at(pass_at, quarter)], arrive.at[pl.ds(2 * quarter, quarter)], base + 2, second)]
        if kind == "r":
            return [
                remote(
                    source.at[at(mine_at + others[k] * chunk, chunk)], arrive.at[pl.ds(3 * quarter + k * chunk, chunk)], base + 3 + k, columns[k]
                )
                for k in range(3)
            ]
        if kind == "g" and stage == 3:
            return [spread(own, chunk, 6 + k, columns[k]) for k in range(3)]
        if kind == "g" and stage == 2:
            return [spread(mine_at, quarter, 9, second)]
        if kind == "g" and stage == 0:
            return [spread(mine_at, quarter, 10, first)]
        if kind == "g":
            return [spread(pass_at, quarter, 11, first)]
        return [spread(kept if stage == 0 else half_rows - kept, half_rows, 12 + stage, twin)]

    def job_start(kind, job, stage):
        for copy in job_copies(kind, job, stage):
            copy.start()

    def job_end(kind, job, stage):
        for copy in job_copies(kind, job, stage):
            copy.wait()
        if kind != "r":
            return
        _, mine_at, pass_at, own, _, _ = rows_of(job)
        arrive = ins[job]
        if stage == 0:
            here = at(pass_at, quarter)
            grads[job, here] = (grads[job, here].astype(F32) + arrive[:quarter].astype(F32)).astype(BF16)
        elif stage == 2:
            here = at(mine_at, quarter)
            value = grads[job, here].astype(F32)
            if job > 0:
                value = value + arrive[quarter : 2 * quarter].astype(F32)
            grads[job, here] = (value + arrive[2 * quarter : 3 * quarter].astype(F32)).astype(BF16)
        elif stage == 3:
            value = grads[job, at(own, chunk)].astype(F32)
            for k in range(3):
                value = value + arrive[3 * quarter + k * chunk : 3 * quarter + (k + 1) * chunk].astype(F32)
            outs[job][at(own, chunk), mine] = value.astype(BF16)

    def small_copies(stage):
        if stage < 3:
            target = (twin, at_y, at_x)[stage]
            return [remote(small_in.at[2 * stage], small_in.at[2 * stage + 1], 16 + stage, target)]
        return [remote(small_in.at[6], small_z.at[z], 19 + k, target) for k, target in enumerate(columns)]

    def small_start(stage):
        for copy in small_copies(stage):
            copy.start()

    def small_end(stage):
        for copy in small_copies(stage):
            copy.wait()
        if stage < 3:
            small_in[2 * stage + 2] = small_in[2 * stage] + small_in[2 * stage + 1]
            if stage == 2:
                small_z[z] = small_in[6]
        else:
            small_out[...] = (small_z[0] + small_z[1]) + (small_z[2] + small_z[3])

    def factor_copies():
        return [remote(ref.at[core], ref.at[core], 22 + k, twin) for k, ref in enumerate((fac_normed, fac_feed))]

    def factors_on():
        for copy in norm_z + feed_z:
            copy.wait_recv()
        for copy in factor_copies():
            copy.start()

    two = 2 * units
    summing = core == x

    def part_at(which):
        return pl.ds(pl.multiple_of(which * two, 16), two)

    def across_copy(k):
        return remote(hidden_grads.at[part_at(y if k else 1 - y)], hidden_in.at[k], 24 + k, at_x)

    def along_copy():
        return remote(hidden_grads.at[part_at(1 - y)], hidden_far, 26, at_y)

    def share_copy():
        return remote(hidden_share, hidden_got, 27, twin)

    def hidden_make():
        for copy in factor_copies():
            copy.wait()
        slot = z * 2 + core
        size = hidden_grads.shape[0]
        normed = fac_normed[...].reshape(8 * masks, model)
        feed = fac_feed[...].reshape(8 * masks, model)
        at = pl.ds(pl.multiple_of(slot * size, 128), size)
        act, slope = gelu_parts(dot(normed, wup_v[:, at]) + vecs[pl.ds(z, 1), mine])
        gp = (dot_nt(feed, wdown_v[at, :]) * slope).astype(BF16)
        hidden_grads[:, :model] = dot_tn(gp, normed).astype(BF16)
        hidden_grads[:, model:] = dot_tn(act.astype(BF16), feed).astype(BF16)

    def hidden_start(k):
        @pl.when(jnp.logical_not(summing))
        def _():
            across_copy(k).start()

    def hidden_arrive(k):
        @pl.when(jnp.logical_not(summing))
        def _():
            across_copy(k).wait_send()

        @pl.when(summing)
        def _():
            across_copy(k).wait_recv()
            if k == 0:
                here = part_at(1 - y)
                hidden_grads[here] = (hidden_grads[here].astype(F32) + hidden_in[0].astype(F32)).astype(BF16)
                along_copy().start()

    def hidden_sum():
        @pl.when(summing)
        def _():
            along_copy().wait()
            value = hidden_grads[part_at(y)].astype(F32) + hidden_in[1].astype(F32) + hidden_far[...].astype(F32)
            low_part, high_part = value[:units], value[units:]
            own = jnp.where(core == 0, low_part, high_part)
            hidden_share[...] = jnp.where(core == 0, high_part, low_part).astype(BF16)
            share_copy().start()
            up_out[...] = own[:, :model]
            down_out[...] = own[:, model:]

    def hidden_end():
        @pl.when(summing)
        def _():
            share_copy().wait_send()

        @pl.when(jnp.logical_not(summing))
        def _():
            share_copy().wait_recv()
            value = hidden_got[...].astype(F32)
            up_out[...] = value[:, :model]
            down_out[...] = value[:, model:]

    def piece_of(index):
        return pl.ds(index * piece, piece)

    def igrad_copy(index):
        return remote(igrad_send.at[piece_of(index)], igrad_in.at[piece_of(index)], 29 + index, at_y)

    def igrad_step():
        remote(dx_send, dx_in, 28, twin).wait_recv()
        input_grad[row] = input_grad[row] + dx_in[:stretch, :].astype(F32)
        igrad_send[...] = (input_grad[1 - row] + dx_in[stretch:, :].astype(F32)).astype(BF16)

    def igrad_end(index):
        igrad_copy(index).wait()
        input_grad[1 - row, piece_of(index)] = igrad_in[piece_of(index), :].astype(F32)

    def out_copy(index):
        return remote(out_send.at[piece_of(index)], layer_out.at[row, piece_of(index)], 32 + index, at_y)

    results = [
        (layer_out, layer_hbm), (input_grad, igrad_hbm), (out_o, hbm_o), (out_0, hbm_0), (out_1, hbm_1), (out_2, hbm_2),
        (up_out, up_hbm), (down_out, down_hbm), (small_out, small_hbm),
    ]

    def result_copy(index):
        src, dst = results[index]
        return pltpu.make_async_copy(src, dst, local_sem.at[20 + index])

    ended = []

    def act(name):
        start, kind, rest = name[0] == "S", name[1], [int(c) for c in name[2:]]
        ended.append(name)
        if kind in "rgt":
            (job_start if start else job_end)(kind, *rest)
            if kind == "t" and not start and {"Et%d0" % rest[0], "Et%d1" % rest[0]} <= set(ended):
                result_copy(2 + rest[0]).start()
        elif kind == "s":
            (small_start if start else small_end)(*rest)
            if not start and rest[0] == 3:
                result_copy(8).start()
        elif kind == "d":
            igrad_step()
        elif kind == "i":
            if start:
                igrad_copy(*rest).start()
            else:
                igrad_end(*rest)
                if {"Ei0", "Ei1"} <= set(ended):
                    result_copy(1).start()
        elif kind == "o":
            if start:
                out_copy(*rest).start()
            else:
                out_copy(*rest).wait()
                if {"Eo0", "Eo1"} <= set(ended):
                    result_copy(0).start()
        elif kind == "f":
            factors_on()
        elif kind == "H":
            hidden_make()
        elif kind == "h":
            (hidden_start if start else hidden_arrive)(*rest)
        elif kind == "k":
            hidden_sum()
        elif kind == "m":
            hidden_end()
            result_copy(6).start()
            result_copy(7).start()

    def act_on(name):
        for each in PLAN.get(name, ()):
            act(each)

    gb = gb_both[...].reshape(count, model)
    gctx = dot(gb, wo_t[...]).astype(BF16)
    for pair in range(pairs):
        lanes = slice(pair * 128, pair * 128 + 128)
        pair_keys, pair_values, pair_queries = keys[:, lanes], values_t[lanes, :], queries[:, lanes]
        pair_gctx = gctx[:, lanes]
        dqs, dks, dvs = [], [], []
        for side in range(2):
            keep = lane_is((count, 128), side * 64, side * 64 + 64)
            head_gctx = jnp.where(keep, pair_gctx.astype(F32), 0.0).astype(BF16)
            low_share = probs[pair * 2 + side]
            share = low_share.astype(F32)
            gp = dot(head_gctx, pair_values)
            spread = jnp.sum(share * gp, axis=-1, keepdims=True)
            gs = (share * (gp - spread)).astype(BF16)
            dqs.append(dot(gs, pair_keys))
            dks.append(dot_tn(gs, pair_queries))
            dvs.append(dot_tn(low_share, pair_gctx))
        first = lane_is((count, 128), 0, 64)
        dq = (jnp.where(first, dqs[0], dqs[1]) * 0.125).astype(BF16)
        dq_low[:, lanes] = dq
        first = lane_is((full, 128), 0, 64)
        dk = (jnp.where(first, dks[0], dks[1]) * 0.125).astype(BF16)
        dv = jnp.where(first, dvs[0], dvs[1]).astype(BF16)
        both = slice(pair * 256, pair * 256 + 256)
        dkv_low[:, pair * 256 : pair * 256 + 128] = dk
        dkv_low[:, pair * 256 + 128 : pair * 256 + 256] = dv
        grads[1 + pair, :, :128] = dot_tn(picked[...], dq).astype(BF16)
        grads[1 + pair, :, 128:] = dot(xs_t[...], dkv_low[:, both]).astype(BF16)
        act_on("p" + str(pair))
        if pair == 1:
            ctx_x.wait_recv()
            gb_x.wait_recv()
            near_half = gb_both[:, :, pl.ds(pl.multiple_of(x * width, 128), width)].reshape(count, width)
            value = dot_tn(near_half, context[...]) + dot_tn(gb_far[...].reshape(count, width), ctx_far[...])
            grads[0, at(x * width, width)] = value.astype(BF16)
            act_on("G0")
        there = pl.ds(pl.multiple_of(core * width + pair * 128, 128), 128)
        small_in[0, parts + 6 : parts + 7, there] = jnp.sum(dq.astype(F32), axis=0, keepdims=True)
        small_in[0, parts + 7 : parts + 8, there] = jnp.sum(dv.astype(F32), axis=0, keepdims=True)

    spread_rows = dot(dq_low[...], wq_t[...])
    zero = jnp.zeros((masks, model), F32)
    is_first = core == 0
    gh1 = grad_h1[...]
    spread_rows = spread_rows + jnp.concatenate([jnp.where(is_first, gh1, zero), jnp.where(is_first, zero, gh1)], axis=0)
    high = spread_rows.astype(BF16)
    rest = (spread_rows - high.astype(F32)).astype(BF16)
    for start in (half, half + stretch, 0, stretch):
        here = slice(start, start + stretch)
        value = dot_tn(chosen[:, here], high) + dot_tn(chosen[:, here], rest)
        value = value + dot(dkv_low[here, :], wkv_t[...])
        if start < half:
            input_grad[row if start == 0 else 1 - row] = value
        else:
            dx_send[start - half : start - half + stretch, :] = value.astype(BF16)
            if start > half:
                push(dx_send, dx_in, 28, twin)

    act_on("dx")

    def hooks(step, prefix, count):
        for at in range(count):
            if prefix + str(at) in PLAN:
                @pl.when(step == at)
                def _(at=at):
                    act_on(prefix + str(at))

    def ctx_copy():
        return remote(all_context.at[pl.ds(half, half)], ctx_in, 31, twin)

    def attend_step(step, carry):
        tile, pair = (step // pairs + 2) % 4, step % pairs
        here = pl.ds(pl.multiple_of(tile * stretch, stretch), stretch)
        lanes = pl.ds(pl.multiple_of(pair * 128, 128), 128)
        block = 2 * (y + (tile % 2) * (1 - 2 * y)) + core + (tile // 2) * (1 - 2 * core)
        place = lax.broadcasted_iota(jnp.int32, (stretch, 1), 0) + block * stretch
        seg_col = jnp.where(place.astype(F32) >= split, 1.0, 0.0)
        same_here = seg_col == seg_row
        pair_queries = all_queries[here, lanes].astype(F32)
        pair_keys, pair_values = keys_t[lanes, :], values[:, lanes]
        found = []
        for side in range(2):
            keep = lane_is((stretch, 128), side * 64, side * 64 + 64)
            head_queries = jnp.where(keep, pair_queries, 0.0).astype(BF16)
            scores = jnp.where(same_here, dot(head_queries, pair_keys), MASKED_SCORE)
            weights = jnp.exp(scores - jnp.max(scores, axis=-1, keepdims=True))
            found.append(dot(weights.astype(BF16), pair_values) / jnp.sum(weights, axis=-1, keepdims=True))
        first = lane_is((stretch, 128), 0, 64)
        all_context[here, lanes] = jnp.where(first, found[0], found[1]).astype(BF16)

        @pl.when(step == 2 * pairs - 1)
        def _():
            ctx_copy().start()

        hooks(step, "a", 4 * pairs)
        return carry

    lax.fori_loop(0, 4 * pairs, attend_step, 0)
    ctx_copy().wait()

    def feed_step(step, carry):
        tile, part = 1 - step // parts, step % parts
        here = pl.ds(pl.multiple_of(tile * stretch, stretch), stretch)

        @pl.when(part == 0)
        def _():
            left = jnp.where(is_first, all_context[here, :], ctx_in[here, :])
            right = jnp.where(is_first, ctx_in[here, :], all_context[here, :])
            here_branch = dot(left, wo_v[:width, :]) + dot(right, wo_v[width:, :]) + vector(6)
            normed, _ = norm_parts(xs[here, :].astype(F32) + here_branch)
            value = normed * vector(7) + vector(8)
            y1_keep[...] = value.astype(BF16)
            total[...] = value + vector(9)

        there = pl.ds(pl.multiple_of(part * model, model), model)
        pre = dot(y1_keep[...], wup_v[:, there]) + vecs[pl.ds(part, 1), :]
        total[...] += dot(gelu_only(pre).astype(BF16), wdown_v[there, :])

        @pl.when(part == parts - 1)
        def _():
            normed, _ = norm_parts(total[...])
            value = (normed * vector(10) + vector(11)).astype(BF16)

            @pl.when(tile == 1)
            def _():
                out_send[...] = value

            @pl.when(tile == 0)
            def _():
                layer_out[row] = value

        hooks(step, "f", 2 * parts)
        return carry

    lax.fori_loop(0, 2 * parts, feed_step, 0)
    act_on("end")
    for index in range(len(results)):
        result_copy(index).wait()
    for copy in pending:
        copy.wait_send()


def vmem(count):
    return [pl.BlockSpec(memory_space=pltpu.VMEM)] * count


def local_call(body, outs, name, scratch=()):
    def call(core, *operands):
        return pl.pallas_call(
            body,
            out_shape=outs,
            in_specs=[pl.BlockSpec(memory_space=pltpu.SMEM)] + vmem(len(operands)),
            out_specs=vmem(len(outs)),
            scratch_shapes=list(scratch),
            compiler_params=pltpu.CompilerParams(vmem_limit_bytes=VMEM_LIMIT),
            name=name,
        )(core, *operands)

    return call


def finish_kernel(parts, go, g0, g1, g2, layer_in, igrad_in, up_in, down_in, small_in, wq, wk, wv, wo, layer_out, igrad, up, down, up_bias, *rest):
    vectors, (go_v, pair_v, small, wide, wo_v, *through, in_sem, out_sem) = rest[:8], rest[8:]
    model = go_v.shape[0]
    width, tile = model // 2, 128
    steps = model // tile
    loads = [pltpu.make_async_copy(small_in, small, in_sem.at[0])]
    for step in range(steps):
        rows = pl.ds(step * tile, tile)
        for pair, ref in enumerate((g0, g1, g2)):
            loads.append(pltpu.make_async_copy(ref.at[rows], pair_v.at[pair, rows], in_sem.at[1 + step * 3 + pair]))
    loads.append(pltpu.make_async_copy(go, go_v, in_sem.at[1 + 3 * steps]))
    passed = tuple(zip((igrad_in, layer_in, up_in, down_in), through, (igrad, layer_out, up, down)))
    for index, (src, held, _) in enumerate(passed):
        loads.append(pltpu.make_async_copy(src, held, in_sem.at[2 + 3 * steps + index]))
    for copy in loads:
        copy.start()
    stores = []

    def store(src, dst):
        copy = pltpu.make_async_copy(src, dst, out_sem.at[len(stores)])
        copy.start()
        stores.append(copy)

    loads[0].wait()
    for part in range(parts):
        up_bias[part * model : (part + 1) * model] = small[part]
    for place, out in enumerate(vectors):
        out[...] = small[parts + place]
    for step in range(steps):
        rows = pl.ds(step * tile, tile)
        for pair in range(3):
            loads[1 + step * 3 + pair].wait()
            for core in range(2):
                to = core * width + pair * 128
                for place in range(3):
                    begin = core * width + place * 128
                    wide[place, rows, to : to + 128] = pair_v[pair, rows, begin : begin + 128].astype(F32)
        for place, out in enumerate((wq, wk, wv)):
            store(wide.at[place, rows], out.at[rows])
    for index, (_, held, dst) in enumerate(passed):
        loads[2 + 3 * steps + index].wait()
        store(held, dst)
    loads[1 + 3 * steps].wait()
    for step in range(steps):
        rows = pl.ds(step * tile, tile)
        wo_v[rows, :] = go_v[:, step * tile : (step + 1) * tile].T.astype(F32)
        store(wo_v.at[rows], wo.at[rows])
    for copy in stores:
        copy.wait()


def finish(layer_output, input_grad, go, g0, g1, g2, up_part, down_part, small, hidden):
    model = go.shape[0]
    parts, steps = hidden // model, model // 128
    shaped = jax.ShapeDtypeStruct
    square, vector = shaped((model, model), F32), shaped((model,), F32)
    far = pl.BlockSpec(memory_space=pltpu.HBM)
    found = pl.pallas_call(
        functools.partial(finish_kernel, parts),
        out_shape=(square,) * 4
        + (shaped(layer_output.shape, BF16), shaped(input_grad.shape, F32), shaped(up_part.shape, F32), shaped(down_part.shape, F32))
        + (shaped((hidden,), F32),)
        + (vector,) * 8,
        in_specs=[far] * 9,
        out_specs=[far] * 8 + vmem(9),
        scratch_shapes=[
            pltpu.VMEM((model, model), BF16),
            pltpu.VMEM((3, model, model), BF16),
            pltpu.VMEM(small.shape, F32),
            pltpu.VMEM((3, model, model), F32),
            pltpu.VMEM((model, model), F32),
            pltpu.VMEM(input_grad.shape, F32),
            pltpu.VMEM(layer_output.shape, BF16),
            pltpu.VMEM(up_part.shape, F32),
            pltpu.VMEM(down_part.shape, F32),
            pltpu.SemaphoreType.DMA((6 + 3 * steps,)),
            pltpu.SemaphoreType.DMA((4 + 4 * steps,)),
        ],
        compiler_params=pltpu.CompilerParams(vmem_limit_bytes=VMEM_LIMIT),
        name="finish",
    )(go, g0, g1, g2, layer_output, input_grad, up_part, down_part, small)
    wq, wk, wv, wo, layer_output, input_grad, up_part, down_part, up_bias, g1, s1, g2, s2, ob, db, qb, vb = found
    return layer_output, input_grad, wq, qb, wk, wv, vb, wo, ob, g1, s1, up_part.T, up_bias, down_part, db, g2, s2


def outputs(layer_output, input_grad, grad_wq, grad_wk, grad_wv, grad_wo, up_part, down_part, small):
    model = grad_wq.shape[0]
    base = small.shape[0] - 12
    vector = lambda index: small[index]
    return (
        layer_output,
        input_grad,
        grad_wq.astype(F32),
        vector(base + 6),
        grad_wk.astype(F32),
        grad_wv.astype(F32),
        vector(base + 7),
        grad_wo.astype(F32),
        vector(base + 4),
        vector(base),
        vector(base + 1),
        up_part.T,
        small[:base].reshape(-1),
        down_part,
        vector(base + 5),
        vector(base + 2),
        vector(base + 3),
    )


def layer_call(tokens, cotangent, segment_ids, mask_positions, vectors, weights):
    _, stretch, model = tokens.shape
    hidden = weights[4].shape[1]
    masks = mask_positions.shape[2]
    count, half, full, width = 2 * masks, 2 * stretch, 4 * stretch, model // 2
    units = hidden // 32
    shaped = jax.ShapeDtypeStruct
    low = lambda *shape: pltpu.VMEM(shape, BF16)
    wide = lambda *shape: pltpu.VMEM(shape, F32)
    results = [low(2, stretch, model), wide(2, stretch, model)] + [low(model, model)] * 4
    results += [wide(units, model), wide(units, model), wide(16, model)]
    scratch = results + [pltpu.VMEM(small.shape, small.dtype) for small in (segment_ids, mask_positions) + vectors]
    scratch += [
        wide(hidden // model + 8, model), low(width, model), low(model, model), low(model, width), low(width, full), low(width, full),
        low(full, model), low(model, full), low(2, stretch, model), low(2, 2, masks, model), low(2, masks, model), low(2, masks, model),
        low(masks, model), low(half, model), low(half, model), low(model, width), low(model, width), low(model, width), low(model, model),
        low(model, hidden), low(hidden, model), low(full, width), low(full, width), low(count, width), low(count, width),
        low(HEADS // 2, count, full), low(count, model), low(count, full), low(2, masks, width), low(count, width), low(2, masks, model), low(2, masks, width),
        wide(hidden // model, masks, model), low(count, width), low(full, model), low(4, model, width),
        low(4 * units, 2 * model), low(2, 2 * units, 2 * model), low(2 * units, 2 * model), low(units, 2 * model), low(units, 2 * model), low(2, 4, masks, model), low(2, 4, masks, model),
        wide(masks, model), wide(7, 16, model), wide(4, 16, model),
        low(full, width), low(full, width), low(half, width), wide(stretch, model), low(stretch, model), low(stretch, model),
        low(stretch, model), low(stretch, model),
    ]
    scratch += [low(model - model // 16, width)] * 4
    scratch += [pltpu.SemaphoreType.DMA((32,)), pltpu.SemaphoreType.DMA((120,)), pltpu.SemaphoreType.DMA((120,))]
    anywhere = [pl.BlockSpec(memory_space=pltpu.HBM)]
    return pl.pallas_call(
        layer_kernel,
        out_shape=(
            shaped((2, stretch, model), BF16),
            shaped((2, stretch, model), F32),
            shaped((model, model), BF16),
            shaped((model, model), BF16),
            shaped((model, model), BF16),
            shaped((model, model), BF16),
            shaped((units, model), F32),
            shaped((units, model), F32),
            shaped((16, model), F32),
        ),
        in_specs=anywhere * (4 + len(vectors) + len(weights)),
        out_specs=anywhere * 9,
        scratch_shapes=scratch,
        compiler_params=pltpu.CompilerParams(collective_id=0, has_side_effects=True, vmem_limit_bytes=62 * 2**20),
        name="layer",
    )(tokens, cotangent, segment_ids, mask_positions, *vectors, *weights)


def on_device(
    rows_total,
    tokens,
    cotangent,
    segment_ids,
    mask_positions,
    query_weight,
    query_bias,
    key_weight,
    value_weight,
    value_bias,
    output_weight,
    output_bias,
    first_gain,
    first_shift,
    up_weight,
    up_bias,
    down_weight,
    down_bias,
    second_gain,
    second_shift,
):
    if rows_total == 8:
        vectors = (up_bias, query_bias, value_bias, output_bias, first_gain, first_shift, down_bias, second_gain, second_shift)
        weights = (query_weight, key_weight, value_weight, output_weight, up_weight, down_weight)
        found = layer_call(
            tokens, cotangent, segment_ids, mask_positions, vectors, weights
        )
        return finish(*found, up_weight.shape[1])
    _, stretch, model = tokens.shape
    hidden = up_weight.shape[1]
    width = model // 2
    heads = HEADS // 2
    masks = mask_positions.shape[2]
    seq = lax.axis_index("seq")
    row = seq // 2
    core = seq % 2
    across = [(i, (i + 2) % 4) for i in range(4)]
    beside = [(i, i + 1 - 2 * (i % 2)) for i in range(4)]

    def swap(value):
        return lax.ppermute(value, "seq", across)

    def trade(value):
        return lax.ppermute(value, "seq", beside)

    def take(array, index):
        return lax.dynamic_index_in_dim(array, index, 0, keepdims=False)

    half = jnp.concatenate([take(tokens, row), swap(take(tokens, 1 - row))], axis=0)
    peer = trade(half)
    cot_half = jnp.concatenate([take(cotangent, row), swap(take(cotangent, 1 - row))], axis=0)
    cot_peer = trade(cot_half)
    blocks = jnp.stack([2 * row + core, 2 * (1 - row) + core, 2 * row + 1 - core, 2 * (1 - row) + 1 - core])
    positions = (blocks[:, None] * stretch + jnp.arange(stretch, dtype=jnp.int32)[None, :]).reshape(-1)
    segments = jnp.take(take(segment_ids, row).reshape(4, stretch), blocks, axis=0).reshape(-1)
    slots = take(mask_positions, row).reshape(-1)
    pos, seg, slot_col = positions[None, :], segments[None, :], slots[:, None]
    pos_col, seg_col, slot_row = positions[:, None], segments[:, None], slots[None, :]
    core_scalar = core.reshape(1).astype(jnp.int32)
    line = lambda value: value.reshape(1, -1)
    full = 4 * stretch
    count = 2 * masks
    shaped = jax.ShapeDtypeStruct

    keys, values, queries, context, probs, picked = local_call(
        project_kernel,
        (
            shaped((full, width), BF16),
            shaped((full, width), BF16),
            shaped((count, width), BF16),
            shaped((count, width), BF16),
            shaped((heads, count, full), F32),
            shaped((count, model), BF16),
        ),
        "project",
    )(core_scalar, half, peer, pos, seg, slot_col, query_weight, line(query_bias), key_weight, value_weight, line(value_bias))

    two = context.reshape(2, masks, width)
    ctx_peer = trade(take(two, 1 - core))
    normed_low, feed, branch_low, grad_h1, small = local_call(
        masked_kernel,
        (
            shaped((masks, model), BF16),
            shaped((masks, model), BF16),
            shaped((masks, model), BF16),
            shaped((masks, model), F32),
            shaped((16, model), F32),
        ),
        "masked",
    )(
        core_scalar, take(two, core), ctx_peer, picked, cot_half, cot_peer, pos, slot_col, output_weight, line(output_bias),
        line(first_gain), line(first_shift), up_weight, line(up_bias), down_weight, line(down_bias), line(second_gain), line(second_shift),
    )
    branch_peer = trade(branch_low)
    grads, igrad_own, igrad_peer, bias = local_call(
        back_kernel,
        (
            shaped((4, model, width), BF16),
            shaped((2 * stretch, model), F32),
            shaped((2 * stretch, model), BF16),
            shaped((2, width), F32),
        ),
        "back",
        [pltpu.VMEM((count, width), BF16), pltpu.VMEM((full, width), BF16), pltpu.VMEM((full, width), BF16)],
    )(
        core_scalar, keys, values, queries, context, probs, picked, branch_low, branch_peer, grad_h1, half, peer, pos_col, slot_row,
        query_weight, key_weight, value_weight, output_weight,
    )
    igrad = igrad_own + trade(igrad_peer).astype(F32)
    igrad_other = swap(igrad[stretch:].astype(BF16)).astype(F32)
    igrad_mine = igrad[:stretch]
    input_grad = jnp.where(row == 0, jnp.stack([igrad_mine, igrad_other]), jnp.stack([igrad_other, igrad_mine]))

    ctx_own, ctx_other = local_call(
        attend_kernel, (shaped((2 * stretch, width), BF16), shaped((2 * stretch, width), BF16)), "attend"
    )(core_scalar, half, peer, seg, seg_col, keys, values, query_weight, line(query_bias))
    out_mine, out_other = local_call(
        feed_kernel, (shaped((stretch, model), BF16), shaped((stretch, model), BF16)), "feed"
    )(
        core_scalar, ctx_own, trade(ctx_other), half, output_weight, line(output_bias), line(first_gain), line(first_shift),
        up_weight, line(up_bias), down_weight, line(down_bias), line(second_gain), line(second_shift),
    )
    out_other = swap(out_other)
    layer_output = jnp.where(row == 0, jnp.stack([out_mine, out_other]), jnp.stack([out_other, out_mine]))

    wide = jnp.zeros((2, model), F32)
    bias_rows = lax.dynamic_update_slice(wide, bias, (0, core * width))
    base = hidden // model + 6
    small = jnp.concatenate([small[:base], bias_rows, small[base + 2 :]], axis=0)

    both = ("rows", "seq")
    small = lax.psum(small, both)
    zero = jnp.zeros((model, model), F32)
    wide_grads = [lax.dynamic_update_slice(zero, grads[k].astype(F32), (0, core * width)) for k in (1, 2, 3)]
    rows_wo = grads[0].reshape(2, width, width).transpose(1, 0, 2).reshape(width, model).astype(F32)
    wide_grads.append(lax.dynamic_update_slice(zero, rows_wo, (core * width, 0)))
    grad_wq, grad_wk, grad_wv, grad_wo = lax.psum(tuple(wide_grads), both)
    pieces = []
    units = hidden // 8
    for part in range(8):
        (piece,) = local_call(hidden_kernel, (shaped((units, 2 * model), BF16),), "hidden")(
            jnp.full((1,), part, jnp.int32), normed_low, feed, up_weight, line(up_bias), down_weight
        )
        pieces.append(piece.astype(F32))
    hidden_grads = lax.psum_scatter(jnp.concatenate(pieces, axis=0), both, scatter_dimension=0, tiled=True)

    up_part, down_part = hidden_grads[:, :model], hidden_grads[:, model:]
    return outputs(layer_output, input_grad, grad_wq, grad_wk, grad_wv, grad_wo, up_part, down_part, small)


def solution(mesh):
    split = P("rows", "seq", None)
    in_specs = (split, split, P("rows", None), P("rows", None, None)) + (P(),) * 15
    out_specs = (split, split) + (P(),) * 9 + (P(None, ("rows", "seq")), P(), P(("rows", "seq"), None), P(), P(), P())
    return jax.shard_map(
        functools.partial(on_device, mesh.shape["rows"]), mesh=mesh, in_specs=in_specs, out_specs=out_specs, check_vma=False
    )
```
